32 devices in a mesh: dp: 16 (over z, x, core), tensor: 2 (over y).
Axes of the slice: x: 2, y: 2, z: 4, core: 2. Of those that a mesh axis runs over, the one named last changes fastest.
Arguments:
- inputs: bfloat16 [131072, 512], P(('dp', 'tensor')), may hold values from -6 to 6
- cotangent: bfloat16 [131072, 512], P(('dp', 'tensor')), may hold values from -6 to 6
- lengths: int32 [128], P('dp'), may hold values from 256 to 1024, as said below
- time_span: int32 [128, 2], P('dp'), may hold values from 0 to 1024, as said below
- freq_span: int32 [128, 2], P('dp'), may hold values from 0 to 512, as said below
- gain_one: float32 [512], replicated, may hold values from 0.1 to 1.9
- shift_one: float32 [512], replicated, may hold values from -3 to 3
- qkv_weight: bfloat16 [512, 3, 512], P(None, None, 'tensor'), may hold values from -0.25 to 0.25
- qkv_bias: float32 [2, 512], P(None, 'tensor'), may hold values from -3 to 3
- out_weight: bfloat16 [512, 512], P('tensor'), may hold values from -0.5 to 0.5
- out_bias: float32 [512], replicated, may hold values from -2 to 2
- gain_two: float32 [512], replicated, may hold values from 0.1 to 1.9
- shift_two: float32 [512], replicated, may hold values from -3 to 3
- up_weight: bfloat16 [512, 2048], P(None, 'tensor'), may hold values from -0.25 to 0.25
- up_bias: float32 [2048], P('tensor'), may hold values from -3 to 3
- down_weight: bfloat16 [2048, 512], P('tensor'), may hold values from -0.1875 to 0.1875
- down_bias: float32 [512], replicated, may hold values from -2 to 2
Outputs:
- layer_out: bfloat16 [131072, 512], P(('dp', 'tensor'))
- input_grad: float32 [131072, 512], P(('dp', 'tensor'))
- grad_gain_one: float32 [512], replicated
- grad_shift_one: float32 [512], replicated
- grad_qkv_weight: float32 [512, 3, 512], P(None, None, 'tensor')
- grad_qkv_bias: float32 [2, 512], P(None, 'tensor')
- grad_out_weight: float32 [512, 512], P('tensor')
- grad_out_bias: float32 [512], replicated
- grad_gain_two: float32 [512], replicated
- grad_shift_two: float32 [512], replicated
- grad_up_weight: float32 [512, 2048], P(None, 'tensor')
- grad_up_bias: float32 [2048], P('tensor')
- grad_down_weight: float32 [2048, 512], P('tensor')
- grad_down_bias: float32 [512], replicated
The draws below stay inside these ranges and needn't reach their ends.
Inputs may be any that keep to these rules, and one draw needn't show every extreme that they name: `lengths`: each length is at least 256, and some sequence has all 1024 frames. `time_span`: in each row the second entry minus the first lies between 0 and 40, and in some row it is exactly 40. `freq_span`: in each row the second entry minus the first lies between 0 and 27, and in some row it is exactly 27.
All inputs are finite; a program needn't handle non-finite values.
Results may differ from the reference program's by a relative error of at most 0.02.
Values may be sent and summed in bfloat16 or wider, within the bound.
No kernel may reach another device: no remote copies, remote signals or barrier semaphores. Data moves between devices by JAX's collectives and lax.ppermute only.
A program may use at most 320 MiB of HBM per device.

```python
import math
import jax
import jax.numpy as jnp
from jax import lax

D = 512
HEADS = 8
HEAD_DIM = 64
FF = 2048
SEQ_LEN = 1024
LEFT = 10
RIGHT = 2
TIME_MASK = 40
FREQ_MASK = 27
BLOCK = 512
NSEQ = 128
TOKENS = 131072


def draw_lengths(key, part):
    key = jax.random.fold_in(key, 11)
    key_values, key_chosen = jax.random.split(key)
    values = jax.random.randint(key_values, (NSEQ,), SEQ_LEN // 4, SEQ_LEN + 1)
    chosen = jax.random.randint(key_chosen, (), 0, NSEQ)
    return jnp.where(jnp.arange(NSEQ) == chosen, SEQ_LEN, values).astype(jnp.int32)


def span_rows(key, extent, widest):
    key_starts, key_widths, key_chosen = jax.random.split(key, 3)
    widths = jax.random.randint(key_widths, (NSEQ,), 0, widest + 1)
    chosen = jax.random.randint(key_chosen, (), 0, NSEQ)
    widths = jnp.where(jnp.arange(NSEQ) == chosen, widest, widths)
    starts = jax.random.randint(key_starts, (NSEQ,), 0, extent - widest + 1)
    return jnp.stack([starts, starts + widths], axis=1).astype(jnp.int32)


def draw_time_span(key, part):
    key = jax.random.fold_in(key, 23)
    return span_rows(key, SEQ_LEN, TIME_MASK)


def draw_freq_span(key, part):
    key = jax.random.fold_in(key, 37)
    return span_rows(key, D, FREQ_MASK)


def level_of(own_key, dims, shards, low, top_value):
    level = 1.0
    for dim, blocks in shards:
        draws = jax.random.uniform(jax.random.fold_in(jax.random.fold_in(own_key, 6), dim), (blocks,), jnp.float32, low / len(shards), top_value / len(shards))
        level = level * jnp.repeat(jnp.exp(draws), dims[dim] // blocks).reshape((-1,) + (1,) * (len(dims) - 1 - dim))
    return level


def gaussian(rng, shape, spread, bound, pieces=(), kind=jnp.bfloat16):
    gain = level_of(rng, shape, pieces, -0.22, 0.18) if pieces else 1.0
    drawn = jax.random.normal(rng, shape, jnp.float32) * spread * gain
    return jnp.minimum(jnp.maximum(drawn, -bound), bound).astype(kind)


def setup_inputs(seed: int = 0) -> dict:
    streams_of = jax.random.split(jax.random.key(seed), 18)
    return {
        "inputs": gaussian(streams_of[0], (TOKENS, D), 1.0, 6.0, ((0, 32),)),
        "cotangent": gaussian(streams_of[1], (TOKENS, D), 1.0, 6.0, ((0, 32),)),
        "lengths": draw_lengths(jax.random.fold_in(streams_of[17], 71), 0),
        "time_span": draw_time_span(jax.random.fold_in(streams_of[17], 71), 0),
        "freq_span": draw_freq_span(jax.random.fold_in(streams_of[17], 71), 0),
        "gain_one": jnp.clip(1.0 + 0.18 * jax.random.normal(streams_of[5], (D,), jnp.float32), 0.1, 1.9),
        "shift_one": gaussian(streams_of[6], (D,), 0.5, 3.0, (), jnp.float32),
        "qkv_weight": gaussian(streams_of[7], (D, 3, D), D ** -0.5, 0.25, ((2, 2),)),
        "qkv_bias": gaussian(streams_of[8], (2, D), 0.5, 3.0, ((1, 2),), jnp.float32),
        "out_weight": gaussian(streams_of[9], (D, D), (D // 4) ** -0.5, 0.5, ((0, 2),)),
        "out_bias": gaussian(streams_of[10], (D,), 0.3, 2.0, (), jnp.float32),
        "gain_two": jnp.clip(1.0 + 0.18 * jax.random.normal(streams_of[11], (D,), jnp.float32), 0.1, 1.9),
        "shift_two": gaussian(streams_of[12], (D,), 0.5, 3.0, (), jnp.float32),
        "up_weight": gaussian(streams_of[13], (D, FF), D ** -0.5, 0.25, ((1, 2),)),
        "up_bias": gaussian(streams_of[14], (FF,), 0.5, 3.0, ((0, 2),), jnp.float32),
        "down_weight": gaussian(streams_of[15], (FF, D), (FF // 2) ** -0.5, 0.1875, ((0, 2),)),
        "down_bias": gaussian(streams_of[16], (D,), 0.3, 2.0, (), jnp.float32),
    }


@jax.custom_vjp
def low(v):
    return lax.optimization_barrier(v.astype(jnp.bfloat16)).astype(jnp.float32)

@jax.custom_vjp
def low_back(v):
    return v

def low_keep(v):
    return (low(v), None)

def low_pass(kept, grad):
    return (grad,)

def back_keep(v):
    return (v, None)

def back_low(kept, grad):
    return (low(grad),)
low.defvjp(low_keep, low_pass)
low_back.defvjp(back_keep, back_low)
epsilon = 1e-05
key_margin = 16
highest = lax.Precision.HIGHEST

def layer_norm(values, norm_gain, norm_shift):
    centre = lax.optimization_barrier(jnp.mean(values, axis=-1, keepdims=True))
    offset = values - centre
    variance = lax.optimization_barrier(jnp.mean(offset * offset, axis=-1, keepdims=True))
    return offset * lax.rsqrt(variance + epsilon) * norm_gain + norm_shift

def attention(queries, keys, values, seq_lengths):
    pad_widths = ((0, 0), (key_margin, key_margin), (0, 0), (0, 0))
    keys_pad = jnp.pad(keys, pad_widths)
    values_pad = jnp.pad(values, pad_widths)
    score_scale = HEAD_DIM ** (-0.5)

    def one_block(block_index):
        first_row = block_index * BLOCK
        query_blk = lax.dynamic_slice_in_dim(queries, first_row, BLOCK, 1)
        key_blk = lax.dynamic_slice_in_dim(keys_pad, first_row, BLOCK + 2 * key_margin, 1)
        value_blk = lax.dynamic_slice_in_dim(values_pad, first_row, BLOCK + 2 * key_margin, 1)
        query_pos = first_row + jnp.arange(BLOCK, dtype=jnp.int32)
        key_pos = first_row - key_margin + jnp.arange(BLOCK + 2 * key_margin, dtype=jnp.int32)
        relative = key_pos[None, :] - query_pos[:, None]
        inside = (relative >= -LEFT) & (relative <= RIGHT) & (key_pos[None, :] >= 0)
        key_live = (key_pos[None, None, :] < seq_lengths[:, None, None]) | (relative == 0)[None]
        allowed = (inside[None] & key_live)[:, None]
        scores = jnp.einsum('gqhe,gkhe->ghqk', query_blk, key_blk, precision=highest) * score_scale
        scores = low_back(jnp.where(allowed, scores, -1000000000.0))
        top_score = lax.optimization_barrier(jnp.max(scores, axis=-1, keepdims=True))
        weights = jnp.exp(scores - top_score)
        probabilities = weights / lax.optimization_barrier(jnp.sum(weights, axis=-1, keepdims=True))
        return jnp.einsum('ghqk,gkhe->gqhe', low(probabilities), value_blk, precision=highest)
    blocks = lax.map(jax.checkpoint(one_block), jnp.arange(SEQ_LEN // BLOCK, dtype=jnp.int32))
    return jnp.moveaxis(blocks, 0, 1).reshape(queries.shape)

def encoder_layer(params, frames, keep_mask, seq_lengths):
    gain_one, shift_one, qkv_weight, qkv_bias, out_weight, out_bias, gain_two, shift_two, up_weight, up_bias, down_weight, down_bias = params
    groups = seq_lengths.shape[0]
    masked = frames * keep_mask
    normed_one = low(layer_norm(masked, gain_one, shift_one))
    zero_row = jnp.zeros((1, D), jnp.float32)
    bias_rows = jnp.concatenate([qkv_bias[0:1], zero_row, qkv_bias[1:2]], axis=0)
    projected = jnp.einsum('td,dcf->tcf', normed_one, qkv_weight, precision=highest) + bias_rows[None]
    projected = low(low_back(projected))
    qkv_split = projected.reshape(groups, SEQ_LEN, 3, HEADS, HEAD_DIM)
    context = attention(qkv_split[:, :, 0], qkv_split[:, :, 1], qkv_split[:, :, 2], seq_lengths)
    context = low(low_back(context.reshape(groups * SEQ_LEN, D)))
    branch = low_back(jnp.dot(context, out_weight, precision=highest))
    middle = masked + branch + out_bias
    normed_two = low(layer_norm(middle, gain_two, shift_two))
    hidden_pre = low_back(jnp.dot(normed_two, up_weight, precision=highest) + up_bias)
    hidden = low(jax.nn.gelu(hidden_pre))
    feed_out = low_back(jnp.dot(hidden, down_weight, precision=highest))
    return middle + feed_out + down_bias

def reference(inputs, cotangent, lengths, time_span, freq_span, gain_one, shift_one, qkv_weight, qkv_bias, out_weight, out_bias, gain_two, shift_two, up_weight, up_bias, down_weight, down_bias):
    params = tuple((item.astype(jnp.float32) for item in (gain_one, shift_one, qkv_weight, qkv_bias, out_weight, out_bias, gain_two, shift_two, up_weight, up_bias, down_weight, down_bias)))
    group_count = math.gcd(NSEQ, max(1, 4096 // SEQ_LEN))
    stretches = NSEQ // group_count
    rows_per = group_count * SEQ_LEN
    frames_all = inputs.astype(jnp.float32).reshape(stretches, rows_per, D)
    grads_all = cotangent.astype(jnp.float32).reshape(stretches, rows_per, D)
    lengths_all = lengths.reshape(stretches, group_count)
    time_all = time_span.reshape(stretches, group_count, 2)
    freq_all = freq_span.reshape(stretches, group_count, 2)
    position = jnp.arange(SEQ_LEN, dtype=jnp.int32)
    column = jnp.arange(D, dtype=jnp.int32)

    def one_stretch(carry, items):
        frames, grad_rows, seq_lengths, time_rows, freq_rows = items
        time_cut = (position[None, :] >= time_rows[:, 0:1]) & (position[None, :] < time_rows[:, 1:2])
        freq_cut = (column[None, :] >= freq_rows[:, 0:1]) & (column[None, :] < freq_rows[:, 1:2])
        keep_mask = ((~time_cut)[:, :, None] & (~freq_cut)[:, None, :]).astype(jnp.float32)
        keep_mask = keep_mask.reshape(rows_per, D)
        outputs, pullback = jax.vjp(lambda param_set, frame_rows: encoder_layer(param_set, frame_rows, keep_mask, seq_lengths), params, frames)
        grad_params, grad_frames = pullback(grad_rows)
        carry = jax.tree.map(lambda running, update_term: running + update_term, carry, grad_params)
        return (carry, (outputs.astype(jnp.bfloat16), grad_frames))
    zeros = jax.tree.map(lambda item: jnp.zeros(item.shape, jnp.float32), params)
    totals, (outputs_all, input_all) = lax.scan(one_stretch, zeros, (frames_all, grads_all, lengths_all, time_all, freq_all))
    return (outputs_all.reshape(TOKENS, D), input_all.reshape(TOKENS, D), totals[0], totals[1], totals[2], totals[3], totals[4], totals[5], totals[6], totals[7], totals[8], totals[9], totals[10], totals[11])
```

```python
import jax
import jax.numpy as jnp
from jax import lax
from jax.experimental import pallas as pl
from jax.experimental.pallas import tpu as pltpu
from jax.sharding import PartitionSpec as P

HEAD_DIM = 64
SEQ_LEN = 1024
LEFT = 10
RIGHT = 2
QB = 64
MARGIN = 16
WIN = QB + 2 * MARGIN
NBLK = SEQ_LEN // QB
EPS = 1e-05
NEG = -1000000000.0
VMEM = 60 * 1024 * 1024
F32 = jnp.float32
BF16 = jnp.bfloat16


def dot_nn(a, b):
    return jnp.dot(a, b, preferred_element_type=F32)


def dot_nt(a, b):
    return lax.dot_general(a, b, (((1,), (1,)), ((), ())), preferred_element_type=F32)


def dot_tn(a, b):
    return lax.dot_general(a, b, (((0,), (0,)), ((), ())), preferred_element_type=F32)


def keep_of(shape, first_pos, seq, tspan, fspan):
    pos = first_pos + lax.broadcasted_iota(jnp.int32, (shape[0], 1), 0)
    col = lax.broadcasted_iota(jnp.int32, (1, shape[1]), 1)
    rows = jnp.where((pos >= tspan[seq, 0]) & (pos < tspan[seq, 1]), 0.0, 1.0)
    cols = jnp.where((col >= fspan[seq, 0]) & (col < fspan[seq, 1]), 0.0, 1.0)
    return rows * cols


def normalize(v):
    off = v - jnp.mean(v, axis=-1, keepdims=True)
    r = lax.rsqrt(jnp.mean(off * off, axis=-1, keepdims=True) + EPS)
    return off * r, r


def head_mask(scale, heads):
    row = lax.broadcasted_iota(jnp.int32, (heads * QB, heads * HEAD_DIM), 0)
    col = lax.broadcasted_iota(jnp.int32, (heads * QB, heads * HEAD_DIM), 1)
    return jnp.where(row // QB == col // HEAD_DIM, scale, 0.0).astype(BF16)


def spread(block, mask, heads):
    return jnp.concatenate([block] * heads, axis=0) * mask


def pair_rows(probs, window, heads):
    out = []
    low = lax.broadcasted_iota(jnp.int32, (QB, 2 * HEAD_DIM), 1) < HEAD_DIM
    for p in range(heads // 2):
        both = dot_tn(
            probs[:, p * 2 * QB : (p + 1) * 2 * QB],
            window[:, p * 2 * HEAD_DIM : (p + 1) * 2 * HEAD_DIM],
        )
        out.append(jnp.where(low, both[:QB], both[QB:]))
    return jnp.concatenate(out, axis=1)


def attend(length, proj, kpad, vpad, ctx, probs_out, heads):
    width = heads * HEAD_DIM
    edge = jnp.zeros((MARGIN, width), BF16)
    for pad, j in ((kpad, 1), (vpad, 2)):
        pad[0:MARGIN, :] = edge
        pad[MARGIN + SEQ_LEN :, :] = edge
        pad[MARGIN : MARGIN + SEQ_LEN, :] = proj[:, j * width : (j + 1) * width]
    mask = head_mask(HEAD_DIM**-0.5, heads)
    key = lax.broadcasted_iota(jnp.int32, (WIN, heads * QB), 0)
    query = lax.broadcasted_iota(jnp.int32, (WIN, heads * QB), 1) % QB
    rel = key - MARGIN - query
    band = jnp.where((rel >= -LEFT) & (rel <= RIGHT), 0.0, NEG)
    diagonal = jnp.where(rel == 0, 0.0, NEG)

    def block(b, carry):
        first = pl.multiple_of(b * QB, QB)
        k_win = kpad[pl.ds(first, WIN), :]
        v_win = vpad[pl.ds(first, WIN), :]
        q_all = spread(proj[pl.ds(first, QB), 0:width], mask, heads)
        pos = key + (first - MARGIN)
        live = (pos >= 0) & (pos < length)
        scores = dot_nt(k_win, q_all) + jnp.where(live, band, diagonal)
        weights = jnp.exp(scores - jnp.max(scores, axis=0, keepdims=True))
        probs = (weights / jnp.sum(weights, axis=0, keepdims=True)).astype(BF16)
        probs_out[pl.ds(pl.multiple_of(b * WIN, WIN), WIN), :] = probs
        ctx[pl.ds(first, QB), :] = pair_rows(probs, v_win, heads).astype(BF16)
        return carry

    lax.fori_loop(0, NBLK, block, 0, unroll=4)


def first_kernel(heads, length, tspan, fspan, x, w, bias, gain, shift, n1, proj, ctx, probs, kpad, vpad):
    s = pl.program_id(0)
    masked = x[...].astype(F32) * keep_of(x.shape, 0, s, tspan, fspan)
    n1[...] = (normalize(masked)[0] * gain[...] + shift[...]).astype(BF16)
    proj[...] = (dot_nn(n1[...], w[...]) + bias[...]).astype(BF16)
    attend(length[s], proj, kpad, vpad, ctx, probs, heads)


def second_kernel(heads, length, n1, w, bias, proj, ctx, probs, kpad, vpad):
    s = pl.program_id(0)
    proj[...] = (dot_nn(n1[...], w[...]) + bias[...]).astype(BF16)
    attend(length[s], proj, kpad, vpad, ctx, probs, heads)


def const_spec(shape):
    return pl.BlockSpec(shape, lambda *_: (0,) * len(shape), pipeline_mode=pl.Buffered(1))


def rows_spec(rows, cols):
    return pl.BlockSpec((rows, cols), lambda i, *_: (i, 0))


def params():
    return pltpu.CompilerParams(vmem_limit_bytes=VMEM, dimension_semantics=("arbitrary",))


def attention_forward(first, length, tspan, fspan, rows, w, bias, gain, shift):
    total, width_in = rows.shape
    seqs = total // SEQ_LEN
    width = w.shape[1] // 3
    heads = width // HEAD_DIM
    outs = [
        jax.ShapeDtypeStruct((total, 3 * width), BF16),
        jax.ShapeDtypeStruct((total, width), BF16),
        jax.ShapeDtypeStruct((seqs * NBLK * WIN, heads * QB), BF16),
    ]
    out_specs = [
        rows_spec(SEQ_LEN, 3 * width),
        rows_spec(SEQ_LEN, width),
        rows_spec(NBLK * WIN, heads * QB),
    ]
    scratch = [pltpu.VMEM((SEQ_LEN + 2 * MARGIN, width), BF16)] * 2
    flops = 2 * total * width_in * 3 * width + 8 * total * WIN * width
    cost = pl.CostEstimate(flops=flops, bytes_accessed=total * (width_in + 6 * width) * 2, transcendentals=0)
    in_specs = [rows_spec(SEQ_LEN, width_in), const_spec(w.shape), const_spec(bias.shape)]
    if first:
        in_specs += [const_spec(gain.shape), const_spec(shift.shape)]
        outs = [jax.ShapeDtypeStruct(rows.shape, BF16)] + outs
        out_specs = [rows_spec(SEQ_LEN, width_in)] + out_specs
        scalars = (length, tspan, fspan)
        args = (rows, w, bias, gain, shift)
    else:
        scalars = (length,)
        args = (rows, w, bias)

    def body(*refs):
        (first_kernel if first else second_kernel)(heads, *refs)

    return pl.pallas_call(
        body,
        grid_spec=pltpu.PrefetchScalarGridSpec(
            num_scalar_prefetch=len(scalars),
            grid=(seqs,),
            in_specs=in_specs,
            out_specs=out_specs,
            scratch_shapes=scratch,
        ),
        out_shape=outs,
        compiler_params=params(),
        cost_estimate=cost,
        name="attend_first" if first else "attend_second",
    )(*scalars, *args)


TM = 512
FC = 512
GELU_A = 0.7978845608028654
GELU_B = 0.7978845608028654 * 0.044715


def middle_kernel(
    per_seq, tspan, fspan,
    x, cot, ctx_a, ctx_b, wo_a, wo_b, wu_a, wu_b, wd_a, wd_b,
    bo, gain, shift, bu_a, bu_b, bd,
    layer_out, gmid_out, gctx_a, gctx_b, gwo_a, gwo_b, gwu_a, gwu_b, gwd_a, gwd_b, gbu_a, gbu_b, small,
    acc_o, acc_u, acc_d, acc_bu, acc_small, n2_s, gn2_s, out_s,
):
    i = pl.program_id(0)

    @pl.when(i == 0)
    def _():
        acc_o[...] = jnp.zeros_like(acc_o)
        acc_u[...] = jnp.zeros_like(acc_u)
        acc_d[...] = jnp.zeros_like(acc_d)
        acc_bu[...] = jnp.zeros_like(acc_bu)
        acc_small[...] = jnp.zeros_like(acc_small)

    rows = x.shape[0]
    keep = keep_of(x.shape, (i % per_seq) * rows, i // per_seq, tspan, fspan)
    mid = x[...].astype(F32) * keep + dot_nn(ctx_a[...], wo_a[...]) + dot_nn(ctx_b[...], wo_b[...]) + bo[...]
    nn, r = normalize(mid)
    n2_s[...] = (nn * gain[...] + shift[...]).astype(BF16)
    out_s[...] = mid + bd[...]
    n2 = n2_s[...]
    g = cot[...]
    n2_t = n2.T
    g_t = g.T
    half = wu_a.shape[1]
    for part, (wu, wd, bu) in enumerate(((wu_a, wd_a, bu_a), (wu_b, wd_b, bu_b))):
        for c in range(half // FC):
            cs = slice(c * FC, (c + 1) * FC)
            ts = slice(part * half + c * FC, part * half + (c + 1) * FC)
            v = dot_nn(n2, wu[:, cs]) + bu[:, cs]
            v2 = v * v
            t = jnp.tanh(v * (GELU_A + GELU_B * v2))
            p = 0.5 + 0.5 * t
            hidden = (v * p).astype(BF16)
            slope = p + (v * (0.5 - 0.5 * (t * t))) * (GELU_A + (3 * GELU_B) * v2)
            gpre = (slope * dot_nt(g, wd[cs, :])).astype(BF16)
            out_s[...] += dot_nn(hidden, wd[cs, :])
            acc_d[:, ts] += dot_nn(g_t, hidden)
            acc_u[:, ts] += dot_nn(n2_t, gpre)
            acc_bu[:, ts] += jnp.sum(gpre.astype(F32), axis=0, keepdims=True)
            back = dot_nt(gpre, wu[:, cs])
            if part == 0 and c == 0:
                gn2_s[...] = back
            else:
                gn2_s[...] += back
    layer_out[...] = out_s[...].astype(BF16)
    gn2 = gn2_s[...]
    gf = g.astype(F32)
    u = gn2 * gain[...]
    un = u * nn
    gm = gf + r * (u - jnp.mean(u, axis=-1, keepdims=True) - nn * jnp.mean(un, axis=-1, keepdims=True))
    gmid_out[...] = gm
    acc_small[0:1, :] += jnp.sum(gn2 * nn, axis=0, keepdims=True)
    acc_small[1:2, :] += jnp.sum(gn2, axis=0, keepdims=True)
    acc_small[2:3, :] += jnp.sum(gm, axis=0, keepdims=True)
    acc_small[3:4, :] += jnp.sum(gf, axis=0, keepdims=True)
    gmb = gm.astype(BF16)
    gctx_a[...] = dot_nt(gmb, wo_a[...]).astype(BF16)
    gctx_b[...] = dot_nt(gmb, wo_b[...]).astype(BF16)
    width = ctx_a.shape[1]
    acc_o[0:width, :] += dot_tn(ctx_a[...], gmb)
    acc_o[width:, :] += dot_tn(ctx_b[...], gmb)

    @pl.when(i == pl.num_programs(0) - 1)
    def _():
        gwo_a[...] = acc_o[0:width, :].astype(BF16)
        gwo_b[...] = acc_o[width:, :].astype(BF16)
        gwu_a[...] = acc_u[:, :half].astype(BF16)
        gwu_b[...] = acc_u[:, half:].astype(BF16)
        gwd_a[...] = acc_d[:, :half].astype(BF16).T
        gwd_b[...] = acc_d[:, half:].astype(BF16).T
        gbu_a[...] = acc_bu[:, :half]
        gbu_b[...] = acc_bu[:, half:]
        small[...] = acc_small[...]


def middle_block(tspan, fspan, x, cot, ctx_a, ctx_b, wo, wu, wd, bo, gain, shift, bu, bd):
    total, d = x.shape
    width = ctx_a.shape[1]
    half = wu[0].shape[1]
    args = (x, cot, ctx_a, ctx_b, *wo, *wu, *wd, bo, gain, shift, *bu, bd)
    in_specs = [rows_spec(TM, d), rows_spec(TM, d), rows_spec(TM, width), rows_spec(TM, width)]
    in_specs += [const_spec(a.shape) for a in args[4:]]
    outs = [
        ((total, d), BF16, True), ((total, d), F32, True), ((total, width), BF16, True), ((total, width), BF16, True),
        ((width, d), BF16, False), ((width, d), BF16, False),
        ((d, half), BF16, False), ((d, half), BF16, False),
        ((half, d), BF16, False), ((half, d), BF16, False),
        ((1, half), F32, False), ((1, half), F32, False), ((8, d), F32, False),
    ]
    out_specs = [rows_spec(TM, s[1]) if tiled else const_spec(s) for s, _, tiled in outs]
    scratch = [
        pltpu.VMEM((2 * width, d), F32), pltpu.VMEM((d, 2 * half), F32), pltpu.VMEM((d, 2 * half), F32),
        pltpu.VMEM((1, 2 * half), F32), pltpu.VMEM((8, d), F32),
        pltpu.VMEM((TM, d), BF16), pltpu.VMEM((TM, d), F32), pltpu.VMEM((TM, d), F32),
    ]
    flops = 2 * total * d * (2 * half * 6 + 2 * width * 3)
    per_seq = SEQ_LEN // TM

    def body(*refs):
        middle_kernel(per_seq, *refs)

    return pl.pallas_call(
        body,
        grid_spec=pltpu.PrefetchScalarGridSpec(
            num_scalar_prefetch=2, grid=(total // TM,), in_specs=in_specs, out_specs=out_specs, scratch_shapes=scratch
        ),
        out_shape=[jax.ShapeDtypeStruct(s, t) for s, t, _ in outs],
        compiler_params=params(),
        cost_estimate=pl.CostEstimate(flops=flops, bytes_accessed=total * d * 14, transcendentals=0),
        name="feed_forward",
    )(tspan, fspan, *args)


def attend_back_kernel(heads, n1, proj, probs, gctx, gproj, gw, gb, kpad, vpad, dk, dv, acc, acc_b):
    s = pl.program_id(0)

    @pl.when(s == 0)
    def _():
        acc[...] = jnp.zeros_like(acc)
        acc_b[...] = jnp.zeros_like(acc_b)

    width = heads * HEAD_DIM
    edge = jnp.zeros((MARGIN, width), BF16)
    for pad, j in ((kpad, 1), (vpad, 2)):
        pad[0:MARGIN, :] = edge
        pad[MARGIN + SEQ_LEN :, :] = edge
        pad[MARGIN : MARGIN + SEQ_LEN, :] = proj[:, j * width : (j + 1) * width]
    mask = head_mask(1.0, heads)
    dk[0 : 2 * MARGIN, :] = jnp.zeros((2 * MARGIN, width), F32)
    dv[0 : 2 * MARGIN, :] = jnp.zeros((2 * MARGIN, width), F32)
    scale = HEAD_DIM**-0.5

    def block(b, carry):
        first = pl.multiple_of(b * QB, QB)
        k_win = kpad[pl.ds(first, WIN), :]
        v_win = vpad[pl.ds(first, WIN), :]
        q_all = spread(proj[pl.ds(first, QB), 0:width], mask, heads)
        o_all = spread(gctx[pl.ds(first, QB), :], mask, heads)
        pb = probs[pl.ds(pl.multiple_of(b * WIN, WIN), WIN), :]
        p = pb.astype(F32)
        gp = dot_nt(v_win, o_all)
        gs = (p * (gp - jnp.sum(p * gp, axis=0, keepdims=True))).astype(BF16)
        gproj[pl.ds(first, QB), 0:width] = (pair_rows(gs, k_win, heads) * scale).astype(BF16)
        for total, term in ((dk, dot_nn(gs, q_all) * scale), (dv, dot_nn(pb, o_all))):
            total[pl.ds(first, 2 * MARGIN), :] += term[: 2 * MARGIN]
            total[pl.ds(first + 2 * MARGIN, QB), :] = term[2 * MARGIN :]
        return carry

    lax.fori_loop(0, NBLK, block, 0, unroll=4)
    gproj[:, width : 2 * width] = dk[MARGIN : MARGIN + SEQ_LEN, :].astype(BF16)
    gproj[:, 2 * width :] = dv[MARGIN : MARGIN + SEQ_LEN, :].astype(BF16)
    gp_all = gproj[...]
    acc[...] += dot_tn(n1[...], gp_all)
    acc_b[...] += jnp.sum(gp_all.astype(F32), axis=0, keepdims=True)

    @pl.when(s == pl.num_programs(0) - 1)
    def _():
        gw[...] = acc[...].astype(BF16)
        gb[...] = acc_b[...]


def attention_backward(n1, proj, probs, gctx):
    total, d = n1.shape
    seqs = total // SEQ_LEN
    width = gctx.shape[1]
    heads = width // HEAD_DIM

    def body(*refs):
        attend_back_kernel(heads, *refs)

    pad = SEQ_LEN + 2 * MARGIN
    return pl.pallas_call(
        body,
        grid=(seqs,),
        in_specs=[
            rows_spec(SEQ_LEN, d), rows_spec(SEQ_LEN, 3 * width),
            rows_spec(NBLK * WIN, heads * QB), rows_spec(SEQ_LEN, width),
        ],
        out_specs=[rows_spec(SEQ_LEN, 3 * width), const_spec((d, 3 * width)), const_spec((1, 3 * width))],
        out_shape=[
            jax.ShapeDtypeStruct((total, 3 * width), BF16),
            jax.ShapeDtypeStruct((d, 3 * width), BF16),
            jax.ShapeDtypeStruct((1, 3 * width), F32),
        ],
        scratch_shapes=[
            pltpu.VMEM((pad, width), BF16), pltpu.VMEM((pad, width), BF16),
            pltpu.VMEM((pad, width), F32), pltpu.VMEM((pad, width), F32),
            pltpu.VMEM((d, 3 * width), F32), pltpu.VMEM((1, 3 * width), F32),
        ],
        compiler_params=params(),
        cost_estimate=pl.CostEstimate(
            flops=2 * total * d * 3 * width + 16 * total * WIN * width,
            bytes_accessed=total * (d + 9 * width) * 2, transcendentals=0,
        ),
        name="attend_back",
    )(n1, proj, probs, gctx)


def last_kernel(per_seq, tspan, fspan, x, gmid, gp_a, gp_b, w_a, w_b, gain, gin, small, acc):
    i = pl.program_id(0)

    @pl.when(i == 0)
    def _():
        acc[...] = jnp.zeros_like(acc)

    keep = keep_of(x.shape, (i % per_seq) * x.shape[0], i // per_seq, tspan, fspan)
    nn, r = normalize(x[...].astype(F32) * keep)
    gn1 = dot_nt(gp_a[...], w_a[...]) + dot_nt(gp_b[...], w_b[...])
    u = gn1 * gain[...]
    a = r * (u - jnp.mean(u, axis=-1, keepdims=True) - nn * jnp.mean(u * nn, axis=-1, keepdims=True))
    gin[...] = (gmid[...] + a) * keep
    acc[0:1, :] += jnp.sum(gn1 * nn, axis=0, keepdims=True)
    acc[1:2, :] += jnp.sum(gn1, axis=0, keepdims=True)

    @pl.when(i == pl.num_programs(0) - 1)
    def _():
        small[...] = acc[...]


def last_block(tspan, fspan, x, gmid, gp_a, gp_b, w_a, w_b, gain):
    total, d = x.shape
    per_seq = SEQ_LEN // TM

    def body(*refs):
        last_kernel(per_seq, *refs)

    return pl.pallas_call(
        body,
        grid_spec=pltpu.PrefetchScalarGridSpec(
            num_scalar_prefetch=2,
            grid=(total // TM,),
            in_specs=[
                rows_spec(TM, d), rows_spec(TM, d), rows_spec(TM, gp_a.shape[1]), rows_spec(TM, gp_b.shape[1]),
                const_spec(w_a.shape), const_spec(w_b.shape), const_spec(gain.shape),
            ],
            out_specs=[rows_spec(TM, d), const_spec((8, d))],
            scratch_shapes=[pltpu.VMEM((8, d), F32)],
        ),
        out_shape=[jax.ShapeDtypeStruct((total, d), F32), jax.ShapeDtypeStruct((8, d), F32)],
        compiler_params=params(),
        cost_estimate=pl.CostEstimate(
            flops=2 * total * d * (gp_a.shape[1] + gp_b.shape[1]), bytes_accessed=total * d * 16, transcendentals=0
        ),
        name="input_gradient",
    )(tspan, fspan, x, gmid, gp_a, gp_b, w_a, w_b, gain)


def make_body(mesh):
    tp = mesh.shape["tensor"]

    def pick(own, other):
        return own, other

    def halves(local, axis):
        if tp == 2:
            return local, lax.ppermute(local, "tensor", [(0, 1), (1, 0)])
        whole = lax.all_gather(local, "tensor", axis=axis, tiled=True)
        return tuple(jnp.split(whole, 2, axis=axis))

    def reduce_halves(own, other, axis):
        if tp == 2:
            own = own + lax.ppermute(other, "tensor", [(0, 1), (1, 0)])
        else:
            own = lax.psum_scatter(
                jnp.concatenate([own, other], axis=axis), "tensor", scatter_dimension=axis, tiled=True
            )
        return own

    def body(
        inputs, cotangent, lengths, time_span, freq_span, gain_one, shift_one, qkv_weight, qkv_bias,
        out_weight, out_bias, gain_two, shift_two, up_weight, up_bias, down_weight, down_bias,
    ):
        total, d = inputs.shape
        seqs = total // SEQ_LEN
        here = lax.axis_index("tensor") * seqs
        length = lax.dynamic_slice_in_dim(lengths, here, seqs, 0)
        tspan = lax.dynamic_slice_in_dim(time_span, here, seqs, 0)
        fspan = lax.dynamic_slice_in_dim(freq_span, here, seqs, 0)
        row = lambda v: v.reshape(1, -1)

        qkv = halves(qkv_weight, 2)
        qkv = [w.reshape(d, -1) for w in qkv]
        qb = halves(qkv_bias, 1)
        qb = [jnp.concatenate([b[0:1], jnp.zeros_like(b[0:1]), b[1:2]], axis=1) for b in qb]
        wo = halves(out_weight, 0)
        wu = halves(up_weight, 1)
        bu = [row(b) for b in halves(up_bias, 0)]
        wd = halves(down_weight, 0)

        n1, proj_a, ctx_a, probs_a = attention_forward(
            True, length, tspan, fspan, inputs, qkv[0], qb[0], row(gain_one), row(shift_one)
        )
        proj_b, ctx_b, probs_b = attention_forward(
            False, length, tspan, fspan, n1, qkv[1], qb[1], None, None
        )
        (
            layer_out, gmid, gctx_a, gctx_b, gwo_a, gwo_b, gwu_a, gwu_b, gwd_a, gwd_b, gbu_a, gbu_b, small_two
        ) = middle_block(
            tspan, fspan, inputs, cotangent, ctx_a, ctx_b, wo, wu, wd,
            row(out_bias), row(gain_two), row(shift_two), bu, row(down_bias),
        )
        gproj_b, gwq_b, gbq_b = attention_backward(n1, proj_b, probs_b, gctx_b)
        gproj_a, gwq_a, gbq_a = attention_backward(n1, proj_a, probs_a, gctx_a)
        input_grad, small_one = last_block(
            tspan, fspan, inputs, gmid, gproj_a, gproj_b, qkv[0], qkv[1], row(gain_one)
        )

        def finish(own, other, axis):
            return lax.psum(reduce_halves(own, other, axis), "dp").astype(F32)

        def three(v):
            return v.reshape(v.shape[0], 3, -1)

        g_qkv = finish(three(gwq_a), three(gwq_b), 2)
        g_qb = finish(three(gbq_a)[0], three(gbq_b)[0], 1)
        g_qb = jnp.stack([g_qb[0], g_qb[2]], axis=0)
        g_out = finish(gwo_a, gwo_b, 0)
        g_up = finish(gwu_a, gwu_b, 1)
        g_bu = finish(gbu_a[0], gbu_b[0], 0)
        g_down = finish(gwd_a, gwd_b, 0)
        small = lax.psum(jnp.concatenate([small_one[0:2], small_two[0:4]], axis=0), ("dp", "tensor"))
        return (
            layer_out, input_grad, small[0], small[1], g_qkv, g_qb, g_out, small[4], small[2], small[3],
            g_up, g_bu, g_down, small[5],
        )

    return body


def solution(mesh):
    in_specs = (
        P(("dp", "tensor"), None), P(("dp", "tensor"), None), P("dp"), P("dp", None), P("dp", None), P(), P(),
        P(None, None, "tensor"), P(None, "tensor"), P("tensor", None), P(), P(), P(), P(None, "tensor"),
        P("tensor"), P("tensor", None), P(),
    )
    out_specs = (
        P(("dp", "tensor"), None), P(("dp", "tensor"), None), P(), P(), P(None, None, "tensor"), P(None, "tensor"),
        P("tensor", None), P(), P(), P(), P(None, "tensor"), P("tensor"), P("tensor", None), P(),
    )
    return jax.shard_map(make_body(mesh), mesh=mesh, in_specs=in_specs, out_specs=out_specs, check_vma=False)
```

```python
import jax
import jax.numpy as jnp
from jax import lax
from jax.experimental import pallas as pl
from jax.experimental.pallas import tpu as pltpu
from jax.sharding import PartitionSpec as P

HEAD_DIM = 64
SEQ_LEN = 1024
LEFT = 10
RIGHT = 2
QB = 64
MARGIN = 16
WIN = QB + 2 * MARGIN
NBLK = SEQ_LEN // QB
EPS = 1e-05
LN_ROWS = 256
NEG = -1000000000.0
VMEM = 60 * 1024 * 1024
F32 = jnp.float32
BF16 = jnp.bfloat16


def dot_nn(a, b):
    return jnp.dot(a, b, preferred_element_type=F32)


def dot_nt(a, b):
    return lax.dot_general(a, b, (((1,), (1,)), ((), ())), preferred_element_type=F32)


def dot_tn(a, b):
    return lax.dot_general(a, b, (((0,), (0,)), ((), ())), preferred_element_type=F32)


def length_of(scal, seq):
    return scal[1 + seq]


def keep_of(shape, first_pos, seq, scal):
    seqs = (scal.shape[0] - 1) // 5
    ends = [scal[1 + k * seqs + seq] for k in range(1, 5)]
    pos = first_pos + lax.broadcasted_iota(jnp.int32, (shape[0], 1), 0)
    col = lax.broadcasted_iota(jnp.int32, (1, shape[1]), 1)
    rows = jnp.where((pos >= ends[0]) & (pos < ends[1]), 0.0, 1.0)
    cols = jnp.where((col >= ends[2]) & (col < ends[3]), 0.0, 1.0)
    return rows * cols


def normalize(v):
    off = v - jnp.mean(v, axis=-1, keepdims=True)
    r = lax.rsqrt(jnp.mean(off * off, axis=-1, keepdims=True) + EPS)
    return off * r, r


def head_mask(scale, heads):
    row = lax.broadcasted_iota(jnp.int32, (heads * QB, heads * HEAD_DIM), 0)
    col = lax.broadcasted_iota(jnp.int32, (heads * QB, heads * HEAD_DIM), 1)
    return jnp.where(row // QB == col // HEAD_DIM, scale, 0.0).astype(BF16)


def spread(block, mask, heads):
    return jnp.concatenate([block] * heads, axis=0) * mask


def pair_rows(probs, window, heads):
    out = []
    low = lax.broadcasted_iota(jnp.int32, (QB, 2 * HEAD_DIM), 1) < HEAD_DIM
    for p in range(heads // 2):
        both = dot_tn(
            probs[:, p * 2 * QB : (p + 1) * 2 * QB],
            window[:, p * 2 * HEAD_DIM : (p + 1) * 2 * HEAD_DIM],
        )
        out.append(jnp.where(low, both[:QB], both[QB:]))
    return jnp.concatenate(out, axis=1)


def attend(length, proj, kpad, vpad, scores, ctx, probs_out, heads):
    width = heads * HEAD_DIM
    edge = jnp.zeros((MARGIN, width), BF16)
    for pad, j in ((kpad, 1), (vpad, 2)):
        pad[0:MARGIN, :] = edge
        pad[MARGIN + SEQ_LEN :, :] = edge
        pad[MARGIN : MARGIN + SEQ_LEN, :] = proj[:, j * width : (j + 1) * width]
    mask = head_mask(HEAD_DIM**-0.5, heads)
    key = lax.broadcasted_iota(jnp.int32, (WIN, heads * QB), 0)
    query = lax.broadcasted_iota(jnp.int32, (WIN, heads * QB), 1) % QB
    rel = key - MARGIN - query
    band = jnp.where((rel >= -LEFT) & (rel <= RIGHT), 0.0, NEG)
    diagonal = jnp.where(rel == 0, 0.0, NEG)

    for b in range(NBLK):
        q_all = spread(proj[b * QB : (b + 1) * QB, 0:width], mask, heads)
        scores[b * WIN : (b + 1) * WIN, :] = dot_nt(kpad[b * QB : b * QB + WIN, :], q_all)
    for b in range(NBLK):
        at = slice(b * WIN, (b + 1) * WIN)
        pos = key + (b * QB - MARGIN)
        live = (pos < length) if b else (pos >= 0) & (pos < length)
        masked = scores[at, :] + jnp.where(live, band, diagonal)
        weights = jnp.exp(masked - jnp.max(masked, axis=0, keepdims=True))
        probs_out[at, :] = (weights / jnp.sum(weights, axis=0, keepdims=True)).astype(BF16)
    for b in range(NBLK):
        v_win = vpad[b * QB : b * QB + WIN, :]
        ctx[b * QB : (b + 1) * QB, :] = pair_rows(probs_out[b * WIN : (b + 1) * WIN, :], v_win, heads).astype(BF16)


def first_kernel(heads, scal, x, w, bias, gain, shift, n1, proj, ctx, probs, *scratch):
    s = pl.program_id(0)
    for first in range(0, SEQ_LEN, LN_ROWS):
        at = slice(first, first + LN_ROWS)
        for r in range(first, first + LN_ROWS, SUB):
            sub = slice(r, r + SUB)
            keep = keep_of((SUB, x.shape[1]), r, s, scal)
            n1[sub, :] = (normalize(x[sub, :].astype(F32) * keep)[0] * gain[...] + shift[...]).astype(BF16)
        proj[at, :] = (dot_nn(n1[at, :], w[...]) + bias[...]).astype(BF16)
    attend(length_of(scal, s), proj, *scratch, ctx, probs, heads)


def second_kernel(heads, scal, n1, w, bias, proj, ctx, probs, *scratch):
    s = pl.program_id(0)
    for first in range(0, SEQ_LEN, LN_ROWS):
        at = slice(first, first + LN_ROWS)
        proj[at, :] = (dot_nn(n1[at, :], w[...]) + bias[...]).astype(BF16)
    attend(length_of(scal, s), proj, *scratch, ctx, probs, heads)


def const_spec(shape):
    return pl.BlockSpec(shape, lambda *_: (0,) * len(shape), pipeline_mode=pl.Buffered(1))


def rows_spec(rows, cols):
    return pl.BlockSpec((rows, cols), lambda i, *_: (i, 0))


def params():
    return pltpu.CompilerParams(vmem_limit_bytes=VMEM, dimension_semantics=("arbitrary",))


def attention_forward(first, scal, rows, w, bias, gain, shift):
    total, width_in = rows.shape
    seqs = total // SEQ_LEN
    width = w.shape[1] // 3
    heads = width // HEAD_DIM
    outs = [
        jax.ShapeDtypeStruct((total, 3 * width), BF16),
        jax.ShapeDtypeStruct((total, width), BF16),
        jax.ShapeDtypeStruct((seqs * NBLK * WIN, heads * QB), BF16),
    ]
    out_specs = [
        rows_spec(SEQ_LEN, 3 * width),
        rows_spec(SEQ_LEN, width),
        rows_spec(NBLK * WIN, heads * QB),
    ]
    scratch = [pltpu.VMEM((SEQ_LEN + 2 * MARGIN, width), BF16)] * 2
    scratch += [pltpu.VMEM((NBLK * WIN, heads * QB), F32)]
    flops = 2 * total * width_in * 3 * width + 8 * total * WIN * width
    cost = pl.CostEstimate(flops=flops, bytes_accessed=total * (width_in + 6 * width) * 2, transcendentals=0)
    in_specs = [rows_spec(SEQ_LEN, width_in), const_spec(w.shape), const_spec(bias.shape)]
    if first:
        in_specs += [const_spec(gain.shape), const_spec(shift.shape)]
        outs = [jax.ShapeDtypeStruct(rows.shape, BF16)] + outs
        out_specs = [rows_spec(SEQ_LEN, width_in)] + out_specs
        args = (rows, w, bias, gain, shift)
    else:
        args = (rows, w, bias)

    def body(*refs):
        (first_kernel if first else second_kernel)(heads, *refs)

    return pl.pallas_call(
        body,
        grid_spec=pltpu.PrefetchScalarGridSpec(
            num_scalar_prefetch=1,
            grid=(seqs,),
            in_specs=in_specs,
            out_specs=out_specs,
            scratch_shapes=scratch,
        ),
        out_shape=outs,
        compiler_params=params(),
        cost_estimate=cost,
        name="attend_first" if first else "attend_second",
    )(scal, *args)


TM = 512
FC = 512
SUB = 32
GELU_A = 0.7978845608028654
GELU_B = 0.7978845608028654 * 0.044715


def subs(rows):
    return [slice(r, r + SUB) for r in range(0, rows, SUB)]


def fold_rows(v):
    return jnp.sum(v.reshape(-1, 8, v.shape[-1]), axis=0)


def clear(i, *refs):
    @pl.when(i == 0)
    def _():
        for ref in refs:
            ref[...] = jnp.zeros_like(ref)


EXTRA = 128
BLOCKS = 16


def put_blocks(me, packs, acc, columns):
    rows = acc.shape[0] // BLOCKS
    each = BLOCKS // len(packs)
    for j in range(BLOCKS):
        first = pl.multiple_of((j ^ me) * rows, rows)
        packs[j // each][j % each] = acc[pl.ds(first, rows), columns].astype(BF16)


def put_vectors(acc, first, vectors):
    spare = EXTRA - len(vectors)
    acc[:, first:] = jnp.concatenate(vectors + [jnp.zeros((spare, acc.shape[0]), F32)], axis=0).T


def up_kernel(
    per_seq, scal,
    x, cot, ctx_a, ctx_b, wo_a, wo_b, wu_a, wu_b, bo, gain, shift, bu_a, bu_b,
    mid_out, n2_out, hidden_out, slope_out, pack_own, pack_other, small,
    acc_d, acc_small, branch_a, branch_b, n2_half, pre_even, pre_odd,
):
    i = pl.program_id(0)
    clear(i, acc_d, acc_small)
    rows = x.shape[0]
    branch_a[...] = dot_nn(ctx_a[...], wo_a[...])
    branch_b[...] = dot_nn(ctx_b[...], wo_b[...])
    g = cot[...]
    g_t = g.T
    bias_sum = jnp.zeros(acc_small.shape, F32)
    for sub in subs(rows):
        keep = keep_of((SUB, x.shape[1]), (i % per_seq) * rows + sub.start, i // per_seq, scal)
        mid = x[sub, :].astype(F32) * keep + branch_a[sub, :] + branch_b[sub, :] + bo[...]
        mid_out[sub, :] = mid
        n2 = (normalize(mid)[0] * gain[...] + shift[...]).astype(BF16)
        n2_out[sub, :] = n2
        n2_half[sub, :] = n2 * 0.5
        bias_sum += fold_rows(cot[sub, :].astype(F32))
    acc_small[...] += bias_sum
    half = wu_a.shape[1]
    chunks = [(part, c) for part in range(2) for c in range(half // FC)]
    pres = (pre_even, pre_odd)

    def up(n):
        part, c = chunks[n]
        pres[n % 2][...] = dot_nn(n2_half[...], (wu_a, wu_b)[part][:, c * FC : (c + 1) * FC])

    up(0)
    for n, (part, c) in enumerate(chunks):
        if n + 1 < len(chunks):
            up(n + 1)
        bias = (bu_a, bu_b)[part][:, c * FC : (c + 1) * FC] * 0.5
        ts = slice(part * half + c * FC, part * half + (c + 1) * FC)
        for sub in subs(rows):
            v = pres[n % 2][sub, :] + bias
            v2 = v * v
            t = jnp.tanh(v * (2 * GELU_A + (8 * GELU_B) * v2))
            hidden_out[sub, ts] = (v + v * t).astype(BF16)
            w = v * (GELU_A + (12 * GELU_B) * v2)
            slope_out[sub, ts] = ((0.5 + 0.5 * t) + w * (1.0 - t * t)).astype(BF16)
        acc_d[:, ts] += dot_nn(g_t, hidden_out[:, ts])

    @pl.when(i == pl.num_programs(0) - 1)
    def _():
        put_blocks(scal[0], [pack_own], acc_d, slice(0, half))
        put_blocks(scal[0], [pack_other], acc_d, slice(half, 2 * half))
        small[...] = acc_small[...]


def call(kernel, name, grid, scalars, in_specs, outs, out_specs, scratch, flops, nbytes, args, alias=()):
    return pl.pallas_call(
        kernel,
        grid_spec=pltpu.PrefetchScalarGridSpec(
            num_scalar_prefetch=len(scalars), grid=(grid,), in_specs=in_specs, out_specs=out_specs,
            scratch_shapes=scratch,
        ),
        out_shape=[jax.ShapeDtypeStruct(s, t) for s, t in outs],
        compiler_params=params(),
        input_output_aliases=dict(alias),
        cost_estimate=pl.CostEstimate(flops=flops, bytes_accessed=nbytes, transcendentals=0),
        name=name,
    )(*scalars, *args)


def up_block(scal, x, cot, ctx_a, ctx_b, wo, wu, bo, gain, shift, bu):
    total, d = x.shape
    width = ctx_a.shape[1]
    half = wu[0].shape[1]
    args = (x, cot, ctx_a, ctx_b, *wo, *wu, bo, gain, shift, *bu)
    in_specs = [rows_spec(TM, d), rows_spec(TM, d), rows_spec(TM, width), rows_spec(TM, width)]
    in_specs += [const_spec(a.shape) for a in args[4:]]
    pack = (BLOCKS, d // BLOCKS, half)
    outs = [
        ((total, d), F32), ((total, d), BF16), ((total, 2 * half), BF16), ((total, 2 * half), BF16),
        (pack, BF16), (pack, BF16), ((8, d), F32),
    ]
    out_specs = [rows_spec(TM, d), rows_spec(TM, d), rows_spec(TM, 2 * half), rows_spec(TM, 2 * half)]
    out_specs += [const_spec(pack), const_spec(pack), const_spec((8, d))]
    scratch = [pltpu.VMEM((d, 2 * half), F32), pltpu.VMEM((8, d), F32)]
    scratch += [pltpu.VMEM((TM, d), F32)] * 2 + [pltpu.VMEM((TM, d), BF16)] + [pltpu.VMEM((TM, FC), F32)] * 2

    def body(*refs):
        up_kernel(SEQ_LEN // TM, *refs)

    return call(
        body, "feed_up", total // TM, (scal,), in_specs, outs, out_specs, scratch,
        2 * total * d * (4 * half + 2 * width), total * (18 * d + 8 * half), args,
    )


def down_kernel(
    scal,
    cot, mid, n2_in, slope, ctx_a, ctx_b, wo_a, wo_b, wu_a, wu_b, wd_a, wd_b, gain, small_up,
    gmid_out, gctx_a, gctx_b, keep_own, keep_other, send_own, send_other,
    acc_own, acc_other, acc_bu, acc_small, gh_even, gh_odd, gpre, back_a, back_b, gmid_low,
):
    i = pl.program_id(0)
    clear(i, acc_own, acc_other, acc_bu, acc_small)
    rows = cot.shape[0]
    n2_t = n2_in[...].T
    half = wu_a.shape[1]
    chunks = [(part, c) for part in range(2) for c in range(half // FC)]
    ghs = (gh_even, gh_odd)

    def up(n):
        part, c = chunks[n]
        ghs[n % 2][...] = dot_nt(cot[...], (wd_a, wd_b)[part][c * FC : (c + 1) * FC, :])

    up(0)
    for n, (part, c) in enumerate(chunks):
        if n + 1 < len(chunks):
            up(n + 1)
        ts = slice(part * half + c * FC, part * half + (c + 1) * FC)
        bias_sum = jnp.zeros((8, FC), F32)
        for sub in subs(rows):
            value = slope[sub, ts].astype(F32) * ghs[n % 2][sub, :]
            gpre[sub, ts] = value.astype(BF16)
            bias_sum += fold_rows(value)
        acc_bu[:, ts] += bias_sum
        (acc_own, acc_other)[part][:, c * FC : (c + 1) * FC] += dot_nn(n2_t, gpre[:, ts])
    back_a[...] = dot_nt(gpre[:, :half], wu_a[...])
    back_b[...] = dot_nt(gpre[:, half:], wu_b[...])
    sums = [jnp.zeros((8, cot.shape[1]), F32) for _ in range(3)]
    for sub in subs(rows):
        gn2 = back_a[sub, :] + back_b[sub, :]
        nn, r = normalize(mid[sub, :])
        gnn = gn2 * nn
        u = gn2 * gain[...]
        mean_un = jnp.mean(gnn * gain[...], axis=-1, keepdims=True)
        gm = cot[sub, :].astype(F32) + r * (u - jnp.mean(u, axis=-1, keepdims=True) - nn * mean_un)
        gmid_out[sub, :] = gm
        gmid_low[sub, :] = gm.astype(BF16)
        for k, term in enumerate((gnn, gn2, gm)):
            sums[k] += fold_rows(term)
    for k in range(3):
        acc_small[8 * k : 8 * k + 8, :] += sums[k]
    gctx_a[...] = dot_nt(gmid_low[...], wo_a[...]).astype(BF16)
    gctx_b[...] = dot_nt(gmid_low[...], wo_b[...]).astype(BF16)
    width = ctx_a.shape[1]
    side = gmid_low.shape[1] // 2
    for acc, ctx in ((acc_own, ctx_a), (acc_other, ctx_b)):
        both = dot_tn(ctx[...], gmid_low[...])
        acc[:width, half : half + side] += both[:, :side]
        acc[width:, half : half + side] += both[:, side:]

    @pl.when(i == pl.num_programs(0) - 1)
    def _():
        vectors = [jnp.sum(acc_small[8 * k : 8 * k + 8, :], axis=0, keepdims=True) for k in range(3)]
        vectors += [jnp.sum(small_up[...], axis=0, keepdims=True)]
        biases = jnp.sum(acc_bu[...], axis=0, keepdims=True)
        d = cot.shape[1]
        for part, (acc, keep, send) in enumerate(((acc_own, keep_own, send_own), (acc_other, keep_other, send_other))):
            mine = biases[:, part * half : (part + 1) * half]
            put_vectors(acc, half + side, vectors + [mine[:, :d], mine[:, d:]])
            put_blocks(scal[0], [keep, send], acc, slice(None))


def down_block(scal, cot, mid, n2, slope, ctx_a, ctx_b, wo, wu, wd, gain, small_up):
    total, d = cot.shape
    width = ctx_a.shape[1]
    half = wu[0].shape[1]
    args = (cot, mid, n2, slope, ctx_a, ctx_b, *wo, *wu, *wd, gain, small_up)
    in_specs = [rows_spec(TM, d), rows_spec(TM, d), rows_spec(TM, d), rows_spec(TM, 2 * half)]
    in_specs += [rows_spec(TM, width), rows_spec(TM, width)]
    in_specs += [const_spec(a.shape) for a in args[6:]]
    columns = half + d // 2 + EXTRA
    pack = (BLOCKS // 2, d // BLOCKS, columns)
    outs = [
        ((total, d), F32), ((total, width), BF16), ((total, width), BF16),
        *[(pack, BF16)] * 4,
    ]
    out_specs = [rows_spec(TM, d), rows_spec(TM, width), rows_spec(TM, width)]
    out_specs += [const_spec(s) for s, _ in outs[3:]]
    scratch = [
        pltpu.VMEM((d, columns), F32), pltpu.VMEM((d, columns), F32), pltpu.VMEM((8, 2 * half), F32),
        pltpu.VMEM((24, d), F32), pltpu.VMEM((TM, FC), F32), pltpu.VMEM((TM, FC), F32),
        pltpu.VMEM((TM, 2 * half), BF16), pltpu.VMEM((TM, d), F32), pltpu.VMEM((TM, d), F32), pltpu.VMEM((TM, d), BF16),
    ]
    return call(
        down_kernel, "feed_back", total // TM, (scal,), in_specs, outs, out_specs, scratch,
        2 * total * d * (6 * half + 4 * width), total * (16 * d + 4 * half), args,
    )


def out_kernel(mid, hidden, wd_a, wd_b, bd, *refs):
    half = wd_a.shape[0]
    refs[-1][...] = (
        mid[...] + dot_nn(hidden[:, :half], wd_a[...]) + dot_nn(hidden[:, half:], wd_b[...]) + bd[...]
    ).astype(BF16)


def part_spec(tiles, part, cols):
    return pl.BlockSpec((TM, cols), lambda i, *_: (i + part * tiles, 0))


def out_block(part, parts, mid, hidden, wd, bd, before):
    total, d = mid.shape
    tiles = total // TM // parts
    args = (mid, hidden, *wd, bd)
    specs = [part_spec(tiles, part, d), part_spec(tiles, part, hidden.shape[1])]
    specs += [const_spec(a.shape) for a in (*wd, bd)]
    alias = {}
    if before is not None:
        alias = {len(args): 0}
        args += (before,)
        specs += [pl.BlockSpec(memory_space=pl.ANY)]
    return call(
        out_kernel, "layer_out", tiles, (), specs, [((total, d), BF16)], [part_spec(tiles, part, d)], [],
        2 * tiles * TM * d * hidden.shape[1], tiles * TM * (6 * d + 2 * hidden.shape[1]), args, alias,
    )[0]


def attend_back_kernel(
    heads, scal, n1, proj, probs, gctx, gproj, pack_keep, pack_send, kpad, vpad, dk, dv, acc, acc_b, gprob, gscore
):
    s = pl.program_id(0)
    clear(s, acc, acc_b)
    width = heads * HEAD_DIM
    edge = jnp.zeros((MARGIN, width), BF16)
    for pad, j in ((kpad, 1), (vpad, 2)):
        pad[0:MARGIN, :] = edge
        pad[MARGIN + SEQ_LEN :, :] = edge
        pad[MARGIN : MARGIN + SEQ_LEN, :] = proj[:, j * width : (j + 1) * width]
    mask = head_mask(1.0, heads)
    dk[0 : 2 * MARGIN, :] = jnp.zeros((2 * MARGIN, width), F32)
    dv[0 : 2 * MARGIN, :] = jnp.zeros((2 * MARGIN, width), F32)
    scale = HEAD_DIM**-0.5

    def rows(b):
        return slice(b * QB, (b + 1) * QB)

    def keys(b):
        return slice(b * QB, b * QB + WIN)

    def own(b):
        return slice(b * WIN, (b + 1) * WIN)

    for b in range(NBLK):
        gprob[own(b), :] = dot_nt(vpad[keys(b), :], spread(gctx[rows(b), :], mask, heads))
    for b in range(NBLK):
        p = probs[own(b), :].astype(F32)
        gp = gprob[own(b), :]
        gscore[own(b), :] = (p * (gp - jnp.sum(p * gp, axis=0, keepdims=True))).astype(BF16)
    for b in range(NBLK):
        gproj[rows(b), 0:width] = (pair_rows(gscore[own(b), :], kpad[keys(b), :], heads) * scale).astype(BF16)
    for b in range(NBLK):
        key_term = dot_nn(gscore[own(b), :], spread(proj[rows(b), 0:width], mask, heads)) * scale
        value_term = dot_nn(probs[own(b), :], spread(gctx[rows(b), :], mask, heads))
        for total, term in ((dk, key_term), (dv, value_term)):
            total[b * QB : b * QB + 2 * MARGIN, :] += term[: 2 * MARGIN]
            total[b * QB + 2 * MARGIN : b * QB + WIN, :] = term[2 * MARGIN :]
    gproj[:, width : 2 * width] = dk[MARGIN : MARGIN + SEQ_LEN, :].astype(BF16)
    gproj[:, 2 * width :] = dv[MARGIN : MARGIN + SEQ_LEN, :].astype(BF16)
    gp_all = gproj[...]
    acc[:, : 3 * width] += dot_tn(n1[...], gp_all)
    acc_b[...] += jnp.sum(gp_all.astype(F32), axis=0, keepdims=True)

    @pl.when(s == pl.num_programs(0) - 1)
    def _():
        put_vectors(acc, 3 * width, [jnp.concatenate([acc_b[:, :width], acc_b[:, 2 * width :]], axis=1)])
        put_blocks(scal[0], [pack_keep, pack_send], acc, slice(None))


def attention_backward(scal, n1, proj, probs, gctx):
    total, d = n1.shape
    seqs = total // SEQ_LEN
    width = gctx.shape[1]
    heads = width // HEAD_DIM

    def body(*refs):
        attend_back_kernel(heads, *refs)

    pad = SEQ_LEN + 2 * MARGIN
    columns = 3 * width + EXTRA
    pack = (BLOCKS // 2, d // BLOCKS, columns)
    return call(
        body, "attend_back", seqs, (scal,),
        [
            rows_spec(SEQ_LEN, d), rows_spec(SEQ_LEN, 3 * width),
            rows_spec(NBLK * WIN, heads * QB), rows_spec(SEQ_LEN, width),
        ],
        [((total, 3 * width), BF16), (pack, BF16), (pack, BF16)],
        [rows_spec(SEQ_LEN, 3 * width), const_spec(pack), const_spec(pack)],
        [
            pltpu.VMEM((pad, width), BF16), pltpu.VMEM((pad, width), BF16),
            pltpu.VMEM((pad, width), F32), pltpu.VMEM((pad, width), F32),
            pltpu.VMEM((d, columns), F32), pltpu.VMEM((1, 3 * width), F32),
            pltpu.VMEM((NBLK * WIN, heads * QB), F32), pltpu.VMEM((NBLK * WIN, heads * QB), BF16),
        ],
        2 * total * d * 3 * width + 16 * total * WIN * width, total * (d + 9 * width) * 2,
        (n1, proj, probs, gctx),
    )


def last_kernel(per_seq, first, scal, x, gmid, gp_a, gp_b, w_a, w_b, gain, *refs):
    gin, small, acc, back_a, back_b = refs[-5:]
    i = pl.program_id(0)
    clear(i, acc)
    rows = x.shape[0]
    tile = i + first
    back_a[...] = dot_nt(gp_a[...], w_a[...])
    back_b[...] = dot_nt(gp_b[...], w_b[...])
    sums = [jnp.zeros((8, x.shape[1]), F32) for _ in range(2)]
    for sub in subs(rows):
        keep = keep_of((SUB, x.shape[1]), (tile % per_seq) * rows + sub.start, tile // per_seq, scal)
        nn, r = normalize(x[sub, :].astype(F32) * keep)
        gn1 = back_a[sub, :] + back_b[sub, :]
        gnn = gn1 * nn
        u = gn1 * gain[...]
        mean_un = jnp.mean(gnn * gain[...], axis=-1, keepdims=True)
        a = r * (u - jnp.mean(u, axis=-1, keepdims=True) - nn * mean_un)
        gin[sub, :] = (gmid[sub, :] + a) * keep
        sums[0] += fold_rows(gnn)
        sums[1] += fold_rows(gn1)
    acc[0:8, :] += sums[0]
    acc[8:16, :] += sums[1]

    @pl.when(i == pl.num_programs(0) - 1)
    def _():
        small[...] = acc[...]


def last_block(part, parts, scal, x, gmid, gp_a, gp_b, w_a, w_b, gain, before):
    total, d = x.shape
    tiles = total // TM // parts

    def body(*refs):
        last_kernel(SEQ_LEN // TM, part * tiles, *refs)

    width = gp_a.shape[1]
    args = (x, gmid, gp_a, gp_b, w_a, w_b, gain)
    specs = [part_spec(tiles, part, c) for c in (d, d, width, width)]
    specs += [const_spec(a.shape) for a in args[4:]]
    alias = {}
    if before is not None:
        alias = {len(args) + 1: 0}
        args += (before,)
        specs += [pl.BlockSpec(memory_space=pl.ANY)]
    return call(
        body, "input_gradient", tiles, (scal,), specs,
        [((total, d), F32), ((16, d), F32)], [part_spec(tiles, part, d), const_spec((16, d))],
        [pltpu.VMEM((16, d), F32), pltpu.VMEM((TM, d), F32), pltpu.VMEM((TM, d), F32)],
        4 * tiles * TM * d * width, tiles * TM * (10 * d + 4 * width), args, alias,
    )


def place(me, pieces, out, kind):
    each = pieces[0].shape[0]
    rows = pieces[0].shape[1]
    for j in range(BLOCKS):
        at = pl.ds(pl.multiple_of((j ^ me) * rows, rows), rows)
        out[at, :] = pieces[j // each][j % each].astype(kind)


def unpack_turned(scal, p0, p1, out, natural):
    place(scal[0], (p0, p1), natural, BF16)
    out[...] = natural[...].T.astype(F32)


def unpack_pair(scal, p0, p1, out, beside, small, natural):
    place(scal[0], (p0, p1), natural, F32)
    half = out.shape[1]
    rows, cols = beside.shape
    side = cols // 2
    out[...] = natural[:, :half]
    beside[:, :side] = natural[:rows, half : half + side]
    beside[:, side:] = natural[rows:, half : half + side]
    small[...] = natural[:, half + side :].T[0:8, :]


def unpack_plain(scal, p0, p1, out, small, natural):
    place(scal[0], (p0, p1), natural, F32)
    width = out.shape[1]
    out[...] = natural[:, :width]
    small[...] = natural[:, width:].T[0:8, :]


def unpack(kernel, name, scal, pieces, shapes, natural):
    size = sum(p.size for p in pieces)
    return call(
        kernel, name, 1, (scal,), [const_spec(p.shape) for p in pieces], [(s, F32) for s in shapes],
        [const_spec(s) for s in shapes], natural, 0, 6 * size, tuple(pieces),
    )


def make_body(mesh):
    tp = mesh.shape["tensor"]
    dp = mesh.shape["dp"]
    paired = tp == 2 and dp == BLOCKS

    def across(v):
        return lax.ppermute(v, "tensor", [(0, 1), (1, 0)])

    def swap(v, distance):
        return lax.ppermute(v, "dp", [(i, i ^ distance) for i in range(dp)])

    def core(v):
        return swap(v, 1)

    def plus(first, *rest):
        total = first.astype(F32)
        for v in rest:
            total = total + v.astype(F32)
        return total.astype(first.dtype)

    def lower(v):
        return v[: v.shape[0] // 2]

    def upper(v):
        return v[v.shape[0] // 2 :]

    def join(a, b):
        return jnp.concatenate([a, b], axis=0)

    def window(kernel, args, moves):
        args, sent = lax.optimization_barrier((args, [v for v, _ in moves]))
        arrived = [move(v) for v, (_, move) in zip(sent, moves)]
        return lax.optimization_barrier((kernel(*args), arrived, sent))

    def body(
        inputs, cotangent, lengths, time_span, freq_span, gain_one, shift_one, qkv_weight, qkv_bias,
        out_weight, out_bias, gain_two, shift_two, up_weight, up_bias, down_weight, down_bias,
    ):
        total, d = inputs.shape
        width = out_weight.shape[0]
        seqs = total // SEQ_LEN
        here = lax.axis_index("tensor") * seqs
        index = lax.axis_index("dp")
        label = jnp.int32(0)
        if paired:
            label = ((index & 1) << 3) | ((index & 2) << 1) | ((index & 4) >> 1)
        table = jnp.concatenate([lengths[:, None], time_span, freq_span], axis=1)
        table = lax.dynamic_slice_in_dim(table, here, seqs, 0)
        scal = jnp.concatenate([label.astype(jnp.int32).reshape(1), table.T.reshape(-1)])
        row = lambda v: v.reshape(1, -1)
        rows_of = lambda v: jnp.sum(v.reshape(-1, 8, d), axis=1)
        three_biases = lambda b: jnp.concatenate([b[0:1], jnp.zeros_like(b[0:1]), b[1:2]], axis=1)

        def attend_a(rows, w, bias):
            return attention_forward(True, scal, rows, w, bias, row(gain_one), row(shift_one))

        def attend_b(rows, w, bias):
            return attention_forward(False, scal, rows, w, bias, None, None)

        def up(ctx_a, ctx_b, wo, wu, bu):
            return up_block(
                scal, inputs, cotangent, ctx_a, ctx_b, wo, wu, row(out_bias), row(gain_two), row(shift_two), bu
            )

        def down(mid, n2, slope, ctx_a, ctx_b, wo, wu, wd, small_up):
            return down_block(scal, cotangent, mid, n2, slope, ctx_a, ctx_b, wo, wu, wd, row(gain_two), small_up)

        def back(n1, proj, probs, gctx):
            return attention_backward(scal, n1, proj, probs, gctx)

        def last(part, parts):
            return lambda gmid, gp_a, gp_b, w_a, w_b, before: last_block(
                part, parts, scal, inputs, gmid, gp_a, gp_b, w_a, w_b, row(gain_one), before
            )

        def out(part, parts):
            return lambda mid, hidden, wd, before: out_block(part, parts, mid, hidden, wd, row(down_bias), before)

        flat = lambda w: w.reshape(d, -1)
        if paired:
            odd = index & 1

            def part_of(v):
                rows = v.shape[0] // 2
                return lax.dynamic_slice_in_dim(v, odd * rows, rows, 0)

            def whole(mine, theirs):
                return jnp.concatenate([jnp.where(odd == 0, mine, theirs), jnp.where(odd == 0, theirs, mine)], axis=0)

            biases = jnp.concatenate([qkv_bias, up_bias.reshape(-1, qkv_bias.shape[1])], axis=0)
            qkv_a = flat(qkv_weight)
            qkv_half = part_of(qkv_a)
            up_half = part_of(jnp.concatenate([out_weight.reshape(-1, up_weight.shape[1]), up_weight], axis=0))
            (n1, proj_a, ctx_a, probs_a), (qkv_half, up_half, biases_b), (qkv_mine, up_mine, _) = window(
                attend_a, (inputs, qkv_a, three_biases(qkv_bias)),
                [(qkv_half, across), (up_half, across), (biases, across)],
            )
            qkv_b = whole(qkv_half, core(qkv_half))
            (proj_b, ctx_b, probs_b), (up_theirs, down_half), (up_half, _) = window(
                attend_b, (n1, qkv_b, three_biases(biases_b[:2])), [(up_half, core), (part_of(down_weight), across)]
            )
            both = whole(up_half, up_theirs)
            split = width * d // up_weight.shape[1]
            wo = (out_weight, both[:split].reshape(out_weight.shape))
            wu = (up_weight, both[split:])
            bu = (row(up_bias), row(biases_b[2:]))
            (mid, n2, hidden, slope, d_own, d_other, small_up), (down_theirs,), (down_half,) = window(
                up, (ctx_a, ctx_b, wo, wu, bu), [(down_half, core)]
            )
            wd = (down_weight, whole(down_half, down_theirs))
            (gmid, gctx_a, gctx_b, u_own, u_other, u_send_own, u_send_other), (d_cross,), _ = window(
                down, (mid, n2, slope, ctx_a, ctx_b, wo, wu, wd, small_up), [(d_other, across)]
            )
            u_other, u_own = plus(u_other, core(u_send_other)), plus(u_own, core(u_send_own))
            d_sum = plus(d_own, d_cross)
            d_sum = plus(lower(d_sum), core(upper(d_sum)))
            (gproj_b, q_other, q_send), (u_cross, d_in), _ = window(
                back, (n1, proj_b, probs_b, gctx_b), [(u_other, across), (upper(d_sum), lambda v: swap(v, 2))]
            )
            u_sum = plus(u_own, u_cross)
            d_sum = plus(lower(d_sum), d_in)
            q_other = plus(q_other, core(q_send))
            (gproj_a, q_own, q_send), (u_in, d_in, q_cross), _ = window(
                back, (n1, proj_a, probs_a, gctx_a),
                [(upper(u_sum), lambda v: swap(v, 2)), (upper(d_sum), lambda v: swap(v, 4)), (q_other, across)],
            )
            u_sum = plus(lower(u_sum), u_in)
            d_sum = plus(lower(d_sum), d_in)
            q_sum = plus(q_own, core(q_send), q_cross)
            (input_grad, small_a), (u_in, d_in, q_in), _ = window(
                last(0, 2), (gmid, gproj_a, gproj_b, qkv_a, qkv_b, None),
                [
                    (upper(u_sum), lambda v: swap(v, 4)), (d_sum, lambda v: swap(v, 8)),
                    (upper(q_sum), lambda v: swap(v, 2)),
                ],
            )
            u_sum = plus(lower(u_sum), u_in)
            d_sum = plus(d_sum, d_in)
            q_sum = plus(lower(q_sum), q_in)
            (input_grad, small_b), (u_in, d_in, q_in), _ = window(
                last(1, 2), (gmid, gproj_a, gproj_b, qkv_a, qkv_b, input_grad),
                [(u_sum, lambda v: swap(v, 8)), (d_sum, lambda v: swap(v, 4)), (upper(q_sum), lambda v: swap(v, 4))],
            )
            u_sum = plus(u_sum, u_in)
            d_sum = join(d_sum, d_in)
            q_sum = plus(lower(q_sum), q_in)
            s_sum = rows_of(small_a + small_b)
            (layer_out,), (u_in, d_in, q_in, s_in), _ = window(
                lambda *a: [out(0, 4)(*a)], (mid, hidden, wd, None),
                [
                    (u_sum, lambda v: swap(v, 4)), (d_sum, lambda v: swap(v, 2)), (q_sum, lambda v: swap(v, 8)),
                    (s_sum, across),
                ],
            )
            u_sum = join(u_sum, u_in)
            d_sum = join(d_sum, d_in)
            q_sum = plus(q_sum, q_in)
            s_sum = plus(s_sum, s_in)
            (layer_out,), (u_in, d_in, q_in, s_in), _ = window(
                lambda *a: [out(1, 4)(*a)], (mid, hidden, wd, layer_out),
                [(u_sum, lambda v: swap(v, 2)), (d_sum, core), (q_sum, lambda v: swap(v, 4)), (s_sum, core)],
            )
            u_sum = join(u_sum, u_in)
            q_sum = join(q_sum, q_in)
            s_sum = plus(s_sum, s_in)
            (layer_out,), (u_in, q_in, s_in), _ = window(
                lambda *a: [out(2, 4)(*a)], (mid, hidden, wd, layer_out),
                [(u_sum, core), (q_sum, lambda v: swap(v, 2)), (s_sum, lambda v: swap(v, 2))],
            )
            q_sum = join(q_sum, q_in)
            s_sum = plus(s_sum, s_in)
            (layer_out,), (q_in, s_in), _ = window(
                lambda *a: [out(3, 4)(*a)], (mid, hidden, wd, layer_out),
                [(q_sum, core), (s_sum, lambda v: swap(v, 4))],
            )
            s_sum = plus(s_sum, s_in)
            s_sum = plus(s_sum, swap(s_sum, 8))
            half = up_weight.shape[1]
            (g_down,) = unpack(
                unpack_turned, "unpack_down", scal, (d_sum, d_in), [down_weight.shape], [pltpu.VMEM((d, half), BF16)]
            )
            g_up, g_out, small_two = unpack(
                unpack_pair, "unpack_up", scal, (u_sum, u_in), [up_weight.shape, out_weight.shape, (8, d)],
                [pltpu.VMEM((d, u_sum.shape[2]), F32)],
            )
            g_qkv, small_q = unpack(
                unpack_plain, "unpack_qkv", scal, (q_sum, q_in), [(d, 3 * width), (8, d)],
                [pltpu.VMEM((d, q_sum.shape[2]), F32)],
            )
            g_qkv = g_qkv.reshape(d, 3, -1)
            g_qb = small_q[0].reshape(2, -1)
            g_bu = small_two[4:6].reshape(-1)
            shared_one, shared_two = s_sum, small_two
        else:
            def halves(local, axis):
                return tuple(jnp.split(lax.all_gather(local, "tensor", axis=axis, tiled=True), 2, axis=axis))

            def sums(own, other, axis):
                whole = jnp.concatenate([own, other], axis=axis)
                part = lax.psum_scatter(whole, "tensor", scatter_dimension=axis, tiled=True)
                return lax.psum(part, "dp").astype(F32)

            natural = lambda *packs: jnp.concatenate(packs, axis=0).reshape(d, -1)
            qkv = [flat(w) for w in halves(qkv_weight, 2)]
            qb = [three_biases(b) for b in halves(qkv_bias, 1)]
            bu = [row(b) for b in halves(up_bias, 0)]
            wo, wu, wd = halves(out_weight, 0), halves(up_weight, 1), halves(down_weight, 0)
            n1, proj_a, ctx_a, probs_a = attend_a(inputs, qkv[0], qb[0])
            proj_b, ctx_b, probs_b = attend_b(n1, qkv[1], qb[1])
            mid, n2, hidden, slope, d_own, d_other, small_up = up(ctx_a, ctx_b, wo, wu, bu)
            gmid, gctx_a, gctx_b, *u_packs = down(mid, n2, slope, ctx_a, ctx_b, wo, wu, wd, small_up)
            gproj_b, *q_other = back(n1, proj_b, probs_b, gctx_b)
            gproj_a, *q_own = back(n1, proj_a, probs_a, gctx_a)
            input_grad, small_one = last(0, 1)(gmid, gproj_a, gproj_b, *qkv, None)
            layer_out = out(0, 1)(mid, hidden, wd, None)
            g_down = sums(natural(d_own), natural(d_other), 1).T
            u = natural(u_packs[0], u_packs[2]), natural(u_packs[1], u_packs[3])
            half, side = wu[0].shape[1], d // 2
            g_up = sums(u[0][:, :half], u[1][:, :half], 1)
            beside = [jnp.concatenate(jnp.split(v[:, half : half + side], 2, axis=0), axis=1) for v in u]
            g_out = sums(*beside, 0)
            q = natural(*q_own), natural(*q_other)
            wide = 3 * qkv[0].shape[1] // 3
            g_qkv = sums(*[v[:, :wide].reshape(d, 3, -1) for v in q], 2)
            g_qb = sums(*[v[:, wide].reshape(2, -1) for v in q], 1)
            small_two = [v[:, half + side :].T for v in u]
            g_bu = sums(*[v[4:6].reshape(-1) for v in small_two], 0)
            shared_two = lax.psum(small_two[0][:4], ("dp", "tensor")).astype(F32)
            shared_one = lax.psum(rows_of(small_one), ("dp", "tensor"))
        return (
            layer_out, input_grad, shared_one[0], shared_one[1], g_qkv, g_qb, g_out, shared_two[2],
            shared_two[0], shared_two[1], g_up, g_bu, g_down, shared_two[3],
        )

    return body


def solution(mesh):
    in_specs = (
        P(("dp", "tensor"), None), P(("dp", "tensor"), None), P("dp"), P("dp", None), P("dp", None), P(), P(),
        P(None, None, "tensor"), P(None, "tensor"), P("tensor", None), P(), P(), P(), P(None, "tensor"),
        P("tensor"), P("tensor", None), P(),
    )
    out_specs = (
        P(("dp", "tensor"), None), P(("dp", "tensor"), None), P(), P(), P(None, None, "tensor"), P(None, "tensor"),
        P("tensor", None), P(), P(), P(), P(None, "tensor"), P("tensor"), P("tensor", None), P(),
    )
    return jax.shard_map(make_body(mesh), mesh=mesh, in_specs=in_specs, out_specs=out_specs, check_vma=False)
```

```python
import jax
import jax.numpy as jnp
from jax import lax
from jax.experimental import pallas as pl
from jax.experimental.pallas import tpu as pltpu
from jax.sharding import PartitionSpec as P

HEAD_DIM = 64
SEQ_LEN = 1024
LEFT = 10
RIGHT = 2
QB = 64
MARGIN = 16
WIN = QB + 2 * MARGIN
NBLK = SEQ_LEN // QB
EPS = 1e-05
LN_ROWS = 256
NEG = -1000000000.0
VMEM = 60 * 1024 * 1024
F32 = jnp.float32
BF16 = jnp.bfloat16


def dot_nn(a, b):
    return jnp.dot(a, b, preferred_element_type=F32)


def dot_nt(a, b):
    return lax.dot_general(a, b, (((1,), (1,)), ((), ())), preferred_element_type=F32)


def dot_tn(a, b):
    return lax.dot_general(a, b, (((0,), (0,)), ((), ())), preferred_element_type=F32)


def length_of(scal, seq):
    return scal[3 + scal[2] + seq]


def keep_of(shape, first_pos, seq, scal):
    seqs = (scal.shape[0] - 3) // 5
    ends = [scal[3 + k * seqs + scal[2] + seq] for k in range(1, 5)]
    pos = first_pos + lax.broadcasted_iota(jnp.int32, (shape[0], 1), 0)
    col = lax.broadcasted_iota(jnp.int32, (1, shape[1]), 1)
    rows = jnp.where((pos >= ends[0]) & (pos < ends[1]), 0.0, 1.0)
    cols = jnp.where((col >= ends[2]) & (col < ends[3]), 0.0, 1.0)
    return rows * cols


def normalize(v):
    off = v - jnp.mean(v, axis=-1, keepdims=True)
    r = lax.rsqrt(jnp.mean(off * off, axis=-1, keepdims=True) + EPS)
    return off * r, r


def head_mask(scale, heads):
    row = lax.broadcasted_iota(jnp.int32, (heads * QB, heads * HEAD_DIM), 0)
    col = lax.broadcasted_iota(jnp.int32, (heads * QB, heads * HEAD_DIM), 1)
    return jnp.where(row // QB == col // HEAD_DIM, scale, 0.0).astype(BF16)


def spread(block, mask, heads):
    return jnp.concatenate([block] * heads, axis=0) * mask


def pair_rows(probs, window, heads):
    out = []
    low = lax.broadcasted_iota(jnp.int32, (QB, 2 * HEAD_DIM), 1) < HEAD_DIM
    for p in range(heads // 2):
        both = dot_tn(
            probs[:, p * 2 * QB : (p + 1) * 2 * QB],
            window[:, p * 2 * HEAD_DIM : (p + 1) * 2 * HEAD_DIM],
        )
        out.append(jnp.where(low, both[:QB], both[QB:]))
    return jnp.concatenate(out, axis=1)


def attend(length, proj, kpad, vpad, scores, ctx, probs_out, heads):
    width = heads * HEAD_DIM
    edge = jnp.zeros((MARGIN, width), BF16)
    for pad, j in ((kpad, 1), (vpad, 2)):
        pad[0:MARGIN, :] = edge
        pad[MARGIN + SEQ_LEN :, :] = edge
        pad[MARGIN : MARGIN + SEQ_LEN, :] = proj[:, j * width : (j + 1) * width]
    mask = head_mask(HEAD_DIM**-0.5, heads)
    key = lax.broadcasted_iota(jnp.int32, (WIN, heads * QB), 0)
    query = lax.broadcasted_iota(jnp.int32, (WIN, heads * QB), 1) % QB
    rel = key - MARGIN - query
    band = jnp.where((rel >= -LEFT) & (rel <= RIGHT), 0.0, NEG)
    diagonal = jnp.where(rel == 0, 0.0, NEG)

    for b in range(NBLK):
        q_all = spread(proj[b * QB : (b + 1) * QB, 0:width], mask, heads)
        scores[b * WIN : (b + 1) * WIN, :] = dot_nt(kpad[b * QB : b * QB + WIN, :], q_all)
    for b in range(NBLK):
        at = slice(b * WIN, (b + 1) * WIN)
        pos = key + (b * QB - MARGIN)
        live = (pos < length) if b else (pos >= 0) & (pos < length)
        masked = scores[at, :] + jnp.where(live, band, diagonal)
        weights = jnp.exp(masked - jnp.max(masked, axis=0, keepdims=True))
        probs_out[at, :] = (weights / jnp.sum(weights, axis=0, keepdims=True)).astype(BF16)
    for b in range(NBLK):
        v_win = vpad[b * QB : b * QB + WIN, :]
        ctx[b * QB : (b + 1) * QB, :] = pair_rows(probs_out[b * WIN : (b + 1) * WIN, :], v_win, heads).astype(BF16)


def project(at, n1, w_side, bias, proj):
    width = bias.shape[1]
    value = dot_nn(n1[at, :], w_side[...])
    proj[at, :width] = (value[:, :width] + bias[0:1, :]).astype(BF16)
    proj[at, width : 2 * width] = value[:, width : 2 * width].astype(BF16)
    proj[at, 2 * width :] = (value[:, 2 * width :] + bias[1:2, :]).astype(BF16)


def side_by_side(i, w, w_side):
    @pl.when(i == 0)
    def _():
        width = w.shape[2]
        for j in range(3):
            w_side[:, j * width : (j + 1) * width] = w[j]


def first_kernel(heads, scal, x, w, bias, gain, shift, nn, n1, proj, ctx, probs, w_side, *scratch):
    s = pl.program_id(0)
    side_by_side(s, w, w_side)
    for first in range(0, SEQ_LEN, LN_ROWS):
        at = slice(first, first + LN_ROWS)
        for r in range(first, first + LN_ROWS, SUB):
            sub = slice(r, r + SUB)
            keep = keep_of((SUB, x.shape[1]), r, s, scal)
            value = normalize(x[sub, :].astype(F32) * keep)[0]
            nn[sub, :] = value.astype(BF16)
            n1[sub, :] = (value * gain[...] + shift[...]).astype(BF16)
        project(at, n1, w_side, bias, proj)
    attend(length_of(scal, s), proj, *scratch, ctx, probs, heads)


def second_kernel(heads, scal, n1, w, bias, proj, ctx, probs, w_side, *scratch):
    s = pl.program_id(0)
    side_by_side(s, w, w_side)
    for first in range(0, SEQ_LEN, LN_ROWS):
        project(slice(first, first + LN_ROWS), n1, w_side, bias, proj)
    attend(length_of(scal, s), proj, *scratch, ctx, probs, heads)


def const_spec(shape):
    return pl.BlockSpec(shape, lambda *_: (0,) * len(shape), pipeline_mode=pl.Buffered(1))


def rows_spec(rows, cols):
    return pl.BlockSpec((rows, cols), lambda i, *_: (i, 0))


def params():
    return pltpu.CompilerParams(vmem_limit_bytes=VMEM, dimension_semantics=("arbitrary",))


def attention_forward(first, scal, rows, w, bias, gain, shift):
    total, width_in = rows.shape
    seqs = total // SEQ_LEN
    width = w.shape[2]
    heads = width // HEAD_DIM
    outs = [
        jax.ShapeDtypeStruct((total, 3 * width), BF16),
        jax.ShapeDtypeStruct((total, width), BF16),
        jax.ShapeDtypeStruct((seqs * NBLK * WIN, heads * QB), BF16),
    ]
    out_specs = [
        rows_spec(SEQ_LEN, 3 * width),
        rows_spec(SEQ_LEN, width),
        rows_spec(NBLK * WIN, heads * QB),
    ]
    scratch = [pltpu.VMEM((width_in, 3 * width), BF16)]
    scratch += [pltpu.VMEM((SEQ_LEN + 2 * MARGIN, width), BF16)] * 2
    scratch += [pltpu.VMEM((NBLK * WIN, heads * QB), F32)]
    flops = 2 * total * width_in * 3 * width + 8 * total * WIN * width
    cost = pl.CostEstimate(flops=flops, bytes_accessed=total * (width_in + 6 * width) * 2, transcendentals=0)
    in_specs = [rows_spec(SEQ_LEN, width_in), const_spec(w.shape), const_spec(bias.shape)]
    if first:
        in_specs += [const_spec(gain.shape), const_spec(shift.shape)]
        outs = [jax.ShapeDtypeStruct(rows.shape, BF16)] * 2 + outs
        out_specs = [rows_spec(SEQ_LEN, width_in)] * 2 + out_specs
        args = (rows, w, bias, gain, shift)
    else:
        args = (rows, w, bias)

    def body(*refs):
        (first_kernel if first else second_kernel)(heads, *refs)

    return pl.pallas_call(
        body,
        grid_spec=pltpu.PrefetchScalarGridSpec(
            num_scalar_prefetch=1,
            grid=(seqs,),
            in_specs=in_specs,
            out_specs=out_specs,
            scratch_shapes=scratch,
        ),
        out_shape=outs,
        compiler_params=params(),
        cost_estimate=cost,
        name="attend_first" if first else "attend_second",
    )(scal, *args)


TM = 512
TU = 1024
TB = 512
FC = 512
FB = 512
SUB = 32
GELU_A = 0.7978845608028654
GELU_K = 0.044715 / 0.7978845608028654**2


def subs(rows):
    return [slice(r, r + SUB) for r in range(0, rows, SUB)]


def fold_rows(v):
    return jnp.sum(v.reshape(-1, 8, v.shape[-1]), axis=0)


def clear(i, *refs):
    @pl.when(i == 0)
    def _():
        for ref in refs:
            ref[...] = jnp.zeros_like(ref)


TAIL = 2
ONES = 16
EXTRA = 128
BLOCKS = 16


def put_blocks(me, packs, acc, columns):
    rows = packs[0].shape[1]
    each = BLOCKS // len(packs)
    for j in range(BLOCKS):
        first = pl.multiple_of((j ^ me) * rows, rows)
        packs[j // each][j % each] = acc[pl.ds(first, rows), columns].astype(BF16)


def put_vectors(acc, first, vectors):
    spare = EXTRA - len(vectors)
    rows = vectors[0].shape[1]
    acc[:rows, first:] = jnp.concatenate(vectors + [jnp.zeros((spare, rows), F32)], axis=0).T


def bias_chunk(biases, first, count):
    width = biases.shape[1]
    rows = range(2 + first // width, 2 + (first + count) // width)
    return jnp.concatenate([biases[r : r + 1, :] for r in rows], axis=1)


def up_kernel(
    per_seq, scal,
    x, cot, ctx_a, ctx_b, wo_a, wo_b, wu_a, wu_b, bo, gain, shift, bias_a, bias_b,
    mid_out, n2_out, hidden_out, pre_out, pack_own, pack_other,
    acc_d, wo_s, ctx_s, branch, n2_half, pre_even, pre_odd,
):
    i = pl.program_id(0)
    clear(i, acc_d)
    width = ctx_a.shape[1]

    @pl.when(i == 0)
    def _():
        wo_s[:width, :] = wo_a[...]
        wo_s[width:, :] = wo_b[...]

    rows = x.shape[0]
    ctx_s[:, :width] = ctx_a[...]
    ctx_s[:, width:] = ctx_b[...]
    branch[...] = dot_nn(ctx_s[...], wo_s[...])
    g_t = cot[...].T
    for sub in subs(rows):
        keep = keep_of((SUB, x.shape[1]), (i % per_seq) * rows + sub.start, i // per_seq, scal)
        mid = x[sub, :].astype(F32) * keep + branch[sub, :] + bo[...]
        mid_out[sub, :] = mid
        n2 = (normalize(mid)[0] * gain[...] + shift[...]).astype(BF16)
        n2_out[sub, :] = n2
        n2_half[sub, :] = n2 * 0.5
    half = wu_a.shape[1]
    chunks = [(part, c) for part in range(2) for c in range(half // FC)]
    pres = (pre_even, pre_odd)

    def up(n):
        part, c = chunks[n]
        pres[n % 2][...] = dot_nn(n2_half[...], (wu_a, wu_b)[part][:, c * FC : (c + 1) * FC])

    up(0)
    for n, (part, c) in enumerate(chunks):
        if n + 1 < len(chunks):
            up(n + 1)
        bias = bias_chunk((bias_a, bias_b)[part], c * FC, FC) * 0.5
        ts = slice(part * half + c * FC, part * half + (c + 1) * FC)
        for sub in subs(rows):
            v = pres[n % 2][sub, :] + bias
            z = v * (2 * GELU_A)
            pre_out[sub, ts] = z.astype(BF16)
            t = jnp.tanh(z * (1.0 + GELU_K * (z * z)))
            hidden_out[sub, ts] = (v + v * t).astype(BF16)
        acc_d[:, ts] += dot_nn(g_t, hidden_out[:, ts])

    @pl.when(i == pl.num_programs(0) - 1)
    def _():
        put_blocks(scal[0], [pack_own], acc_d, slice(0, half))
        put_blocks(scal[0], [pack_other], acc_d, slice(half, 2 * half))


def call(kernel, name, grid, scalars, in_specs, outs, out_specs, scratch, flops, nbytes, args, alias=()):
    return pl.pallas_call(
        kernel,
        grid_spec=pltpu.PrefetchScalarGridSpec(
            num_scalar_prefetch=len(scalars), grid=(grid,), in_specs=in_specs, out_specs=out_specs,
            scratch_shapes=scratch,
        ),
        out_shape=[jax.ShapeDtypeStruct(s, t) for s, t in outs],
        compiler_params=params(),
        input_output_aliases=dict(alias),
        cost_estimate=pl.CostEstimate(flops=flops, bytes_accessed=nbytes, transcendentals=0),
        name=name,
    )(*scalars, *args)


def up_block(scal, x, cot, ctx_a, ctx_b, wo, wu, bo, gain, shift, biases):
    total, d = x.shape
    width = ctx_a.shape[1]
    half = wu[0].shape[1]
    args = (x, cot, ctx_a, ctx_b, *wo, *wu, bo, gain, shift, *biases)
    in_specs = [rows_spec(TU, d), rows_spec(TU, d), rows_spec(TU, width), rows_spec(TU, width)]
    in_specs += [const_spec(a.shape) for a in args[4:]]
    pack = (BLOCKS, d // BLOCKS, half)
    outs = [
        ((total, d), F32), ((total, d), BF16), ((total, 2 * half), BF16), ((total, 2 * half), BF16),
        (pack, BF16), (pack, BF16),
    ]
    out_specs = [rows_spec(TU, d), rows_spec(TU, d), rows_spec(TU, 2 * half), rows_spec(TU, 2 * half)]
    out_specs += [const_spec(pack), const_spec(pack)]
    scratch = [
        pltpu.VMEM((d, 2 * half), F32), pltpu.VMEM((2 * width, d), BF16), pltpu.VMEM((TU, 2 * width), BF16),
        pltpu.VMEM((TU, d), F32), pltpu.VMEM((TU, d), BF16), pltpu.VMEM((TU, FC), F32), pltpu.VMEM((TU, FC), F32),
    ]

    def body(*refs):
        up_kernel(SEQ_LEN // TU, *refs)

    return call(
        body, "feed_up", total // TU, (scal,), in_specs, outs, out_specs, scratch,
        2 * total * d * (4 * half + 2 * width), total * (18 * d + 8 * half), args,
    )


def down_kernel(
    scal,
    cot, mid, n2_in, pre, ctx_a, ctx_b, wo_a, wo_b, wu_a, wu_b, wd_a, wd_b, gain,
    gmid_out, gctx_a, gctx_b, keep_own, keep_other, send_own, send_other,
    acc_own, acc_other, acc_small, wo_s, ctx_s, n2_t, gh_even, gh_odd, gpre, back_a, back_b,
):
    i = pl.program_id(0)
    clear(i, acc_own, acc_other, acc_small)
    width = ctx_a.shape[1]

    @pl.when(i == 0)
    def _():
        wo_s[:width, :] = wo_a[...]
        wo_s[width:, :] = wo_b[...]

    rows = cot.shape[0]
    ctx_s[:, :width] = ctx_a[...]
    ctx_s[:, width:] = ctx_b[...]
    n2_t[:-ONES, :] = n2_in[...].T
    n2_t[-ONES:, :] = jnp.ones((ONES, rows), BF16)
    half = wu_a.shape[1]
    chunks = [(part, c) for part in range(2) for c in range(half // FB)]
    ghs = (gh_even, gh_odd)

    def up(n):
        part, c = chunks[n]
        ghs[n % 2][...] = dot_nt(cot[...], (wd_a, wd_b)[part][c * FB : (c + 1) * FB, :]).astype(BF16)

    def vector(n):
        part, c = chunks[n]
        ts = slice(part * half + c * FB, part * half + (c + 1) * FB)
        for sub in subs(rows):
            z = pre[sub, ts]
            k = z * z * GELU_K
            t = jnp.tanh(z * (k + 1.0))
            slope = (t + 1.0) * ((z * (k * 1.5 + 0.5)) * (1.0 - t) + 0.5)
            gpre[sub, ts] = slope * ghs[n % 2][sub, :]

    def use(n):
        part, c = chunks[n]
        ts = slice(part * half + c * FB, part * half + (c + 1) * FB)
        (acc_own, acc_other)[part][:, c * FB : (c + 1) * FB] += dot_nn(n2_t[...], gpre[:, ts])

    up(0)
    for n in range(len(chunks)):
        if n + 1 < len(chunks):
            up(n + 1)
        if n:
            use(n - 1)
        vector(n)
    use(len(chunks) - 1)
    sums = [jnp.zeros((8, cot.shape[1]), F32) for _ in range(4)]
    side = cot.shape[1] // 2
    parts = [slice(k * rows // TAIL, (k + 1) * rows // TAIL) for k in range(TAIL)]

    def back(at):
        back_a[at, :] = dot_nt(gpre[at, :half], wu_a[...])
        back_b[at, :] = dot_nt(gpre[at, half:], wu_b[...])

    back(parts[0])
    for k, at in enumerate(parts):
        if k + 1 < TAIL:
            back(parts[k + 1])
        for r in range(at.start, at.stop, SUB):
            sub = slice(r, r + SUB)
            gn2 = back_a[sub, :] + back_b[sub, :]
            nn, r_std = normalize(mid[sub, :])
            gnn = gn2 * nn
            u = gn2 * gain[...]
            mean_un = jnp.mean(gnn * gain[...], axis=-1, keepdims=True)
            g = cot[sub, :].astype(F32)
            gm = g + r_std * (u - jnp.mean(u, axis=-1, keepdims=True) - nn * mean_un)
            gmid_out[sub, :] = gm.astype(BF16)
            for q, term in enumerate((gnn, gn2, gm, g)):
                sums[q] += fold_rows(term)
        gctx = dot_nt(gmid_out[at, :], wo_s[...])
        gctx_a[at, :] = gctx[:, :width].astype(BF16)
        gctx_b[at, :] = gctx[:, width:].astype(BF16)
    both = dot_tn(ctx_s[...], gmid_out[...])
    for acc, part in ((acc_own, both[:width]), (acc_other, both[width:])):
        acc[:width, half : half + side] += part[:, :side]
        acc[width : 2 * width, half : half + side] += part[:, side:]
    for k in range(4):
        acc_small[8 * k : 8 * k + 8, :] += sums[k]

    @pl.when(i == pl.num_programs(0) - 1)
    def _():
        vectors = [jnp.sum(acc_small[8 * k : 8 * k + 8, :], axis=0, keepdims=True) for k in range(4)]
        d = cot.shape[1]
        for acc, keep, send in ((acc_own, keep_own, send_own), (acc_other, keep_other, send_other)):
            mine = acc[d : d + 1, :half]
            put_vectors(acc, half + side, vectors + [mine[:, :d], mine[:, d:]])
            put_blocks(scal[0], [keep, send], acc, slice(None))


def down_block(scal, cot, mid, n2, pre, ctx_a, ctx_b, wo, wu, wd, gain):
    total, d = cot.shape
    width = ctx_a.shape[1]
    half = wu[0].shape[1]
    args = (cot, mid, n2, pre, ctx_a, ctx_b, *wo, *wu, *wd, gain)
    in_specs = [rows_spec(TB, d), rows_spec(TB, d), rows_spec(TB, d), rows_spec(TB, 2 * half)]
    in_specs += [rows_spec(TB, width), rows_spec(TB, width)]
    in_specs += [const_spec(a.shape) for a in args[6:]]
    columns = half + d // 2 + EXTRA
    pack = (BLOCKS // 2, d // BLOCKS, columns)
    outs = [((total, d), BF16), ((total, width), BF16), ((total, width), BF16), *[(pack, BF16)] * 4]
    out_specs = [rows_spec(TB, d), rows_spec(TB, width), rows_spec(TB, width)]
    out_specs += [const_spec(s) for s, _ in outs[3:]]
    scratch = [
        pltpu.VMEM((d + ONES, columns), F32), pltpu.VMEM((d + ONES, columns), F32),
        pltpu.VMEM((32, d), F32), pltpu.VMEM((2 * width, d), BF16), pltpu.VMEM((TB, 2 * width), BF16),
        pltpu.VMEM((d + ONES, TB), BF16),
        pltpu.VMEM((TB, FB), BF16), pltpu.VMEM((TB, FB), BF16), pltpu.VMEM((TB, 2 * half), BF16),
        pltpu.VMEM((TB, d), F32), pltpu.VMEM((TB, d), F32),
    ]
    return call(
        down_kernel, "feed_back", total // TB, (scal,), in_specs, outs, out_specs, scratch,
        2 * total * d * (6 * half + 4 * width), total * (16 * d + 4 * half), args,
    )


def out_rows(mid, hidden, wd_a, wd_b, bd, out):
    half = wd_a.shape[0]
    out[...] = (
        mid[...] + dot_nn(hidden[:, :half], wd_a[...]) + dot_nn(hidden[:, half:], wd_b[...]) + bd[...]
    ).astype(BF16)


def out_kernel(scal, mid, hidden, wd_a, wd_b, bd, *refs):
    out_rows(mid, hidden, wd_a, wd_b, bd, refs[-1])


def out_down_kernel(scal, mid, hidden, wd_a, wd_b, bd, before, d0, d1, out, down, d_all):
    out_rows(mid, hidden, wd_a, wd_b, bd, out)

    @pl.when(pl.program_id(0) == 0)
    def _():
        place(scal[0], (d0, d1), d_all, BF16)
        down[...] = d_all[...].T.astype(F32)


def part_spec(first, cols):
    return pl.BlockSpec((TM, cols), lambda i, *_: (i + first, 0))


def out_block(first, tiles, scal, mid, hidden, wd, bd, before, pieces=()):
    total, d = mid.shape
    args = (mid, hidden, *wd, bd)
    specs = [part_spec(first, d), part_spec(first, hidden.shape[1])]
    specs += [const_spec(a.shape) for a in (*wd, bd)]
    alias = {}
    if before is not None:
        alias = {len(args) + 1: 0}
        args += (before,)
        specs += [pl.BlockSpec(memory_space=pl.ANY)]
    outs, out_specs, scratch = [((total, d), BF16)], [part_spec(first, d)], []
    if pieces:
        args += tuple(pieces)
        specs += [const_spec(p.shape) for p in pieces]
        shape = (pieces[0].shape[2], d)
        outs += [(shape, F32)]
        out_specs += [const_spec(shape)]
        scratch = [pltpu.VMEM(shape[::-1], BF16)]
    return call(
        out_down_kernel if pieces else out_kernel, "layer_out", tiles, (scal,), specs, outs, out_specs, scratch,
        2 * tiles * TM * d * hidden.shape[1], tiles * TM * (6 * d + 2 * hidden.shape[1]), args, alias,
    )


def attend_back_kernel(
    heads, scal, nn, proj, probs, gctx, w, gain, shift, gproj, pack_keep, pack_send, kpad, vpad, dk, dv, acc, acc_b, gprob, gscore
):
    s = pl.program_id(0)
    clear(s, acc, acc_b)
    width = heads * HEAD_DIM
    edge = jnp.zeros((MARGIN, width), BF16)
    for pad, j in ((kpad, 1), (vpad, 2)):
        pad[0:MARGIN, :] = edge
        pad[MARGIN + SEQ_LEN :, :] = edge
        pad[MARGIN : MARGIN + SEQ_LEN, :] = proj[:, j * width : (j + 1) * width]
    mask = head_mask(1.0, heads)
    dk[0 : 2 * MARGIN, :] = jnp.zeros((2 * MARGIN, width), F32)
    dv[0 : 2 * MARGIN, :] = jnp.zeros((2 * MARGIN, width), F32)
    scale = HEAD_DIM**-0.5

    def rows(b):
        return slice(b * QB, (b + 1) * QB)

    def keys(b):
        return slice(b * QB, b * QB + WIN)

    def own(b):
        return slice(b * WIN, (b + 1) * WIN)

    for b in range(NBLK):
        gprob[own(b), :] = dot_nt(vpad[keys(b), :], spread(gctx[rows(b), :], mask, heads))
    for b in range(NBLK):
        p = probs[own(b), :].astype(F32)
        gp = gprob[own(b), :]
        gscore[own(b), :] = (p * (gp - jnp.sum(p * gp, axis=0, keepdims=True))).astype(BF16)
    for b in range(NBLK):
        gproj[rows(b), 0:width] = (pair_rows(gscore[own(b), :], kpad[keys(b), :], heads) * scale).astype(BF16)
    for b in range(NBLK):
        key_term = dot_nn(gscore[own(b), :], spread(proj[rows(b), 0:width], mask, heads)) * scale
        value_term = dot_nn(probs[own(b), :], spread(gctx[rows(b), :], mask, heads))
        for total, term in ((dk, key_term), (dv, value_term)):
            total[b * QB : b * QB + 2 * MARGIN, :] += term[: 2 * MARGIN]
            total[b * QB + 2 * MARGIN : b * QB + WIN, :] = term[2 * MARGIN :]
    gproj[:, width : 2 * width] = dk[MARGIN : MARGIN + SEQ_LEN, :].astype(BF16)
    gproj[:, 2 * width :] = dv[MARGIN : MARGIN + SEQ_LEN, :].astype(BF16)
    gp_all = gproj[...]
    acc[:, : 3 * width] += dot_tn(nn[...], gp_all)
    acc_b[...] += jnp.sum(gp_all.astype(F32), axis=0, keepdims=True)

    @pl.when(s == pl.num_programs(0) - 1)
    def _():
        d = acc.shape[0]
        column = lambda v: jnp.broadcast_to(v[...], (EXTRA, d)).T[:, 0:1]
        gain_col, shift_col = column(gain), column(shift)
        gain_grad, shift_grad = jnp.zeros((d, 1), F32), jnp.zeros((d, 1), F32)
        for j in range(3):
            at = slice(j * width, (j + 1) * width)
            weight = w[j].astype(F32)
            gain_grad += jnp.sum(weight * acc[:, at], axis=1, keepdims=True)
            shift_grad += jnp.sum(weight * acc_b[:, at], axis=1, keepdims=True)
            acc[:, at] = gain_col * acc[:, at] + shift_col * acc_b[:, at]
        put_vectors(acc, 3 * width, [jnp.concatenate([acc_b[:, :width], acc_b[:, 2 * width :]], axis=1)])
        lane = lax.broadcasted_iota(jnp.int32, (d, EXTRA), 1)
        extra = jnp.where(lane == 1, gain_grad, acc[:, 3 * width :])
        acc[:, 3 * width :] = jnp.where(lane == 2, shift_grad, extra)
        put_blocks(scal[1], [pack_keep, pack_send], acc, slice(None))


def attention_backward(scal, nn, proj, probs, gctx, w, gain, shift):
    total, d = nn.shape
    seqs = total // SEQ_LEN
    width = gctx.shape[1]
    heads = width // HEAD_DIM

    def body(*refs):
        attend_back_kernel(heads, *refs)

    pad = SEQ_LEN + 2 * MARGIN
    columns = 3 * width + EXTRA
    pack = (BLOCKS // 2, d // BLOCKS, columns)
    return call(
        body, "attend_back", seqs, (scal,),
        [
            rows_spec(SEQ_LEN, d), rows_spec(SEQ_LEN, 3 * width),
            rows_spec(NBLK * WIN, heads * QB), rows_spec(SEQ_LEN, width),
            const_spec(w.shape), const_spec(gain.shape), const_spec(shift.shape),
        ],
        [((total, 3 * width), BF16), (pack, BF16), (pack, BF16)],
        [rows_spec(SEQ_LEN, 3 * width), const_spec(pack), const_spec(pack)],
        [
            pltpu.VMEM((pad, width), BF16), pltpu.VMEM((pad, width), BF16),
            pltpu.VMEM((pad, width), F32), pltpu.VMEM((pad, width), F32),
            pltpu.VMEM((d, columns), F32), pltpu.VMEM((1, 3 * width), F32),
            pltpu.VMEM((NBLK * WIN, heads * QB), F32), pltpu.VMEM((NBLK * WIN, heads * QB), BF16),
        ],
        2 * total * d * 3 * width + 16 * total * WIN * width, total * (d + 9 * width) * 2,
        (nn, proj, probs, gctx, w, gain, shift),
    )


def last_kernel(per_seq, first, scal, x, gmid, gp_a, gp_b, w_a, w_b, gain, *refs):
    gin, back_a, back_b, side_a, side_b = refs[-5:]
    i = pl.program_id(0)
    side_by_side(i, w_a, side_a)
    side_by_side(i, w_b, side_b)
    rows = x.shape[0]
    tile = i + first
    back_a[...] = dot_nt(gp_a[...], side_a[...])
    back_b[...] = dot_nt(gp_b[...], side_b[...])
    for sub in subs(rows):
        keep = keep_of((SUB, x.shape[1]), (tile % per_seq) * rows + sub.start, tile // per_seq, scal)
        nn, r = normalize(x[sub, :].astype(F32) * keep)
        u = (back_a[sub, :] + back_b[sub, :]) * gain[...]
        mean_un = jnp.mean(u * nn, axis=-1, keepdims=True)
        a = r * (u - jnp.mean(u, axis=-1, keepdims=True) - nn * mean_un)
        gin[sub, :] = (gmid[sub, :].astype(F32) + a) * keep


def last_block(part, parts, scal, x, gmid, gp_a, gp_b, w_a, w_b, gain, before):
    total, d = x.shape
    tiles = total // TM // parts

    def body(*refs):
        last_kernel(SEQ_LEN // TM, part * tiles, *refs)

    width = gp_a.shape[1]
    args = (x, gmid, gp_a, gp_b, w_a, w_b, gain)
    specs = [part_spec(part * tiles, c) for c in (d, d, width, width)]
    specs += [const_spec(a.shape) for a in args[4:]]
    alias = {}
    if before is not None:
        alias = {len(args) + 1: 0}
        args += (before,)
        specs += [pl.BlockSpec(memory_space=pl.ANY)]
    return call(
        body, "input_gradient", tiles, (scal,), specs, [((total, d), F32)], [part_spec(part * tiles, d)],
        [pltpu.VMEM((TM, d), F32)] * 2 + [pltpu.VMEM((d, width), BF16)] * 2,
        4 * tiles * TM * d * width, tiles * TM * (10 * d + 4 * width), args, alias,
    )[0]


def place(me, pieces, out, kind, columns=slice(None)):
    each = pieces[0].shape[0]
    rows = pieces[0].shape[1]
    for j in range(BLOCKS):
        at = pl.ds(pl.multiple_of((j ^ me) * rows, rows), rows)
        out[at, :] = pieces[j // each][j % each, :, columns].astype(kind)


def unpack_kernel(scal, u0, u1, q0, q1, up, out, *refs):
    vectors, (bias_up, qkv, bias_q, gain, shift, u_side, q_all) = refs[:4], refs[4:]
    me = scal[0]
    half, side = up.shape[1], out.shape[1] // 2
    rows = out.shape[0]
    place(me, (u0, u1), up, F32, slice(0, half))
    place(me, (u0, u1), u_side, F32, slice(half, u0.shape[2]))
    out[:, :side] = u_side[:rows, :side]
    out[:, side:] = u_side[rows:, :side]
    sums = u_side[:, side:].T
    for k in range(4):
        vectors[k][...] = sums[k : k + 1, :]
    bias_up[...] = jnp.concatenate([sums[4:5, :], sums[5:6, :]], axis=1)
    place(scal[1], (q0, q1), q_all, F32)
    width = qkv.shape[2]
    for j in range(3):
        qkv[j] = q_all[:, j * width : (j + 1) * width]
    sums = q_all[:, 3 * width :].T
    bias_q[...] = jnp.concatenate([sums[0:1, :width], sums[0:1, width:]], axis=0)
    gain[...] = sums[1:2, :]
    shift[...] = sums[2:3, :]


def unpack(scal, pieces, up, out, qkv):
    d = up[0]
    shapes = [up, out, *[(1, d)] * 4, (1, up[1]), qkv, (2, qkv[2]), (1, d), (1, d)]
    natural = [(d, pieces[0].shape[2] - up[1]), (d, pieces[2].shape[2])]
    return call(
        unpack_kernel, "unpack", 1, (scal,), [const_spec(p.shape) for p in pieces], [(s, F32) for s in shapes],
        [const_spec(s) for s in shapes], [pltpu.VMEM(s, F32) for s in natural], 0,
        6 * sum(p.size for p in pieces), tuple(pieces),
    )


def make_body(mesh):
    tp = mesh.shape["tensor"]
    dp = mesh.shape["dp"]
    paired = tp == 2 and dp == BLOCKS

    def across(v):
        return lax.ppermute(v, "tensor", [(0, 1), (1, 0)])

    def swap(v, distance):
        return lax.ppermute(v, "dp", [(i, i ^ distance) for i in range(dp)])

    def core(v):
        return swap(v, 1)

    def diagonal(v):
        pairs = [(2 * i + j, 2 * (i ^ 8) + 1 - j) for i in range(dp) for j in range(2)]
        return lax.ppermute(v, ("dp", "tensor"), pairs)

    def plus(first, *rest):
        total = first.astype(F32)
        for v in rest:
            total = total + v.astype(F32)
        return total.astype(first.dtype)

    def lower(v):
        return v[: v.shape[0] // 2]

    def upper(v):
        return v[v.shape[0] // 2 :]

    def join(a, b):
        return jnp.concatenate([a, b], axis=0)

    def window(kernel, args, moves):
        args, sent = lax.optimization_barrier((args, [v for v, _ in moves]))
        arrived = [move(v) for v, (_, move) in zip(sent, moves)]
        return lax.optimization_barrier((kernel(*args), arrived, sent))

    def body(
        inputs, cotangent, lengths, time_span, freq_span, gain_one, shift_one, qkv_weight, qkv_bias,
        out_weight, out_bias, gain_two, shift_two, up_weight, up_bias, down_weight, down_bias,
    ):
        total, d = inputs.shape
        seqs = total // SEQ_LEN
        here = lax.axis_index("tensor") * seqs
        index = lax.axis_index("dp")
        label = label_q = jnp.int32(0)
        if paired:
            label = ((index & 1) << 3) | ((index & 2) << 1) | ((index & 4) >> 1)
            label_q = ((index & 1) << 3) | (index & 4)
        place_here = jnp.stack([label, label_q, here]).astype(jnp.int32)
        ends = [span[:, k] for span in (time_span, freq_span) for k in range(2)]
        scal = jnp.concatenate([place_here, lengths, *ends])
        row = lambda v: v.reshape(1, -1)
        stack_biases = lambda b, u: jnp.concatenate([b, u.reshape(-1, b.shape[1])], axis=0)

        def attend_a(rows, w, bias):
            return attention_forward(True, scal, rows, w, bias, row(gain_one), row(shift_one))

        def attend_b(rows, w, bias):
            return attention_forward(False, scal, rows, w, bias, None, None)

        def up(ctx_a, ctx_b, wo, wu, biases):
            return up_block(
                scal, inputs, cotangent, ctx_a, ctx_b, wo, wu, row(out_bias), row(gain_two), row(shift_two), biases
            )

        def down(mid, n2, pre, ctx_a, ctx_b, wo, wu, wd):
            return down_block(scal, cotangent, mid, n2, pre, ctx_a, ctx_b, wo, wu, wd, row(gain_two))

        def back(nn, proj, probs, gctx, w):
            return attention_backward(scal, nn, proj, probs, gctx, w, row(gain_one), row(shift_one))

        def last(part, parts):
            return lambda gmid, gp_a, gp_b, w_a, w_b, before: last_block(
                part, parts, scal, inputs, gmid, gp_a, gp_b, w_a, w_b, row(gain_one), before
            )

        def out(first, tiles):
            return lambda mid, hidden, wd, before, *pieces: out_block(
                first, tiles, scal, mid, hidden, wd, row(down_bias), before, pieces
            )

        turned = lambda w: jnp.transpose(w, (1, 0, 2))
        if paired:
            odd = index & 1

            def part_of(v):
                rows = v.shape[0] // 2
                return lax.dynamic_slice_in_dim(v, odd * rows, rows, 0)

            def whole(mine, theirs):
                return jnp.concatenate([jnp.where(odd == 0, mine, theirs), jnp.where(odd == 0, theirs, mine)], axis=0)

            biases = stack_biases(qkv_bias, up_bias)
            qkv_a = turned(qkv_weight)
            qkv_rows = qkv_a.reshape(-1, qkv_a.shape[2])
            (nn, n1, proj_a, ctx_a, probs_a), (qkv_half, out_half, biases_b), _ = window(
                attend_a, (inputs, qkv_a, biases),
                [(part_of(qkv_rows), across), (part_of(out_weight), across), (biases, across)],
            )
            qkv_b = whole(qkv_half, core(qkv_half)).reshape(qkv_a.shape)
            (proj_b, ctx_b, probs_b), (up_half, out_theirs), (_, out_half) = window(
                attend_b, (n1, qkv_b, biases_b), [(part_of(up_weight), across), (out_half, core)]
            )
            wo = (out_weight, whole(out_half, out_theirs))
            wu = (up_weight, whole(up_half, core(up_half)))
            (mid, n2, hidden, pre, d_own, d_other), (down_b,), _ = window(
                up, (ctx_a, ctx_b, wo, wu, (biases, biases_b)), [(down_weight, across)]
            )
            wd = (down_weight, down_b)
            (gmid, gctx_a, gctx_b, u_own, u_other, u_send_own, u_send_other), (d_cross,), _ = window(
                down, (mid, n2, pre, ctx_a, ctx_b, wo, wu, wd), [(d_other, across)]
            )
            u_other, u_own = plus(u_other, core(u_send_other)), plus(u_own, core(u_send_own))
            d_sum = plus(d_own, d_cross)
            d_sum = plus(lower(d_sum), core(upper(d_sum)))
            step = lambda distance: lambda v: swap(v, distance)
            (gproj_b, q_other, q_send), (u_cross, d_in), _ = window(
                back, (nn, proj_b, probs_b, gctx_b, qkv_b), [(u_other, across), (upper(d_sum), step(2))]
            )
            u_sum = plus(u_own, u_cross)
            d_sum = plus(lower(d_sum), d_in)
            q_other = plus(q_other, core(q_send))
            (gproj_a, q_own, q_send), (u_in, d_in, q_cross), _ = window(
                back, (nn, proj_a, probs_a, gctx_a, qkv_a),
                [(upper(u_sum), step(2)), (upper(d_sum), step(4)), (q_other, across)],
            )
            u_sum = plus(lower(u_sum), u_in)
            d_sum = plus(lower(d_sum), d_in)
            q_sum = plus(q_own, core(q_send), q_cross)
            input_grad, (u_in, d_in, q_in), _ = window(
                last(0, 2), (gmid, gproj_a, gproj_b, qkv_a, qkv_b, None),
                [(upper(u_sum), step(4)), (d_sum, step(8)), (q_sum, step(2))],
            )
            u_sum = plus(lower(u_sum), u_in)
            d_sum = plus(d_sum, d_in)
            q_sum = plus(q_sum, q_in)
            input_grad, (u_in, d_in, q_in), _ = window(
                last(1, 2), (gmid, gproj_a, gproj_b, qkv_a, qkv_b, input_grad),
                [(u_sum, step(8)), (d_sum, step(4)), (upper(q_sum), step(4))],
            )
            u_sum = plus(u_sum, u_in)
            d_sum = join(d_sum, d_in)
            q_sum = plus(lower(q_sum), q_in)
            third = q_sum.shape[2] - EXTRA
            q_sides = q_sum[:, :, third:]
            tiles = total // TM
            cuts = (0, tiles // 2, tiles * 3 // 4, tiles)
            (layer_out,), (u_in, d_in, q_in, q_side_y, q_side_d), _ = window(
                out(cuts[0], cuts[1] - cuts[0]), (mid, hidden, wd, None),
                [(u_sum, step(4)), (d_sum, step(2)), (q_sum, step(8)), (q_sides, across), (q_sides, diagonal)],
            )
            u_sum = join(u_sum, u_in)
            d_sum = join(d_sum, d_in)
            lane = lax.broadcasted_iota(jnp.int32, q_sides.shape, 2)
            f32 = lambda v: v.astype(F32)
            q_in_side = f32(q_in[:, :, third:])
            own = f32(q_sides) + q_in_side
            both = own + (f32(q_side_y) + f32(q_side_d))
            q_side = jnp.where((lane == 1) | (lane == 2), both, own).astype(BF16)
            q_sum = jnp.concatenate([plus(q_sum[:, :, :third], q_in[:, :, :third]), q_side], axis=2)
            (layer_out,), (u_in, d_in, q_in), _ = window(
                out(cuts[1], cuts[2] - cuts[1]), (mid, hidden, wd, layer_out),
                [(u_sum, step(2)), (d_sum, core), (q_sum, step(4))],
            )
            u_sum = join(u_sum, u_in)
            q_sum = join(q_sum, q_in)
            (layer_out, g_down), (u_in, q_in), _ = window(
                out(cuts[2], cuts[3] - cuts[2]), (mid, hidden, wd, layer_out, d_sum, d_in),
                [(u_sum, core), (q_sum, core)],
            )
            g_up, g_out, *shared_two, g_bu, g_qkv, g_qb, gain_grad, shift_grad = unpack(
                scal, (u_sum, u_in, q_sum, q_in), up_weight.shape, out_weight.shape, qkv_a.shape
            )
            g_qkv = turned(g_qkv)
            g_bu = g_bu.reshape(-1)
            shared_two = [v.reshape(-1) for v in shared_two]
            shared_one = [v.reshape(-1) for v in (gain_grad, shift_grad)]
        else:
            def halves(local, axis):
                return tuple(jnp.split(lax.all_gather(local, "tensor", axis=axis, tiled=True), 2, axis=axis))

            def sums(own, other, axis):
                whole = jnp.concatenate([own, other], axis=axis)
                part = lax.psum_scatter(whole, "tensor", scatter_dimension=axis, tiled=True)
                return lax.psum(part, "dp").astype(F32)

            natural = lambda *packs: jnp.concatenate(packs, axis=0).reshape(d, -1)
            qkv = [turned(w) for w in halves(qkv_weight, 2)]
            biases = [stack_biases(q, u) for q, u in zip(halves(qkv_bias, 1), halves(up_bias, 0))]
            wo, wu, wd = halves(out_weight, 0), halves(up_weight, 1), halves(down_weight, 0)
            nn, n1, proj_a, ctx_a, probs_a = attend_a(inputs, qkv[0], biases[0])
            proj_b, ctx_b, probs_b = attend_b(n1, qkv[1], biases[1])
            mid, n2, hidden, pre, d_own, d_other = up(ctx_a, ctx_b, wo, wu, biases)
            gmid, gctx_a, gctx_b, *u_packs = down(mid, n2, pre, ctx_a, ctx_b, wo, wu, wd)
            gproj_b, *q_other = back(nn, proj_b, probs_b, gctx_b, qkv[1])
            gproj_a, *q_own = back(nn, proj_a, probs_a, gctx_a, qkv[0])
            input_grad = last(0, 1)(gmid, gproj_a, gproj_b, *qkv, None)
            layer_out = out(0, total // TM)(mid, hidden, wd, None)[0]
            g_down = sums(natural(d_own), natural(d_other), 1).T
            u = natural(u_packs[0], u_packs[2]), natural(u_packs[1], u_packs[3])
            half, side = wu[0].shape[1], d // 2
            g_up = sums(u[0][:, :half], u[1][:, :half], 1)
            beside = [jnp.concatenate(jnp.split(v[:, half : half + side], 2, axis=0), axis=1) for v in u]
            g_out = sums(*beside, 0)
            q = natural(*q_own), natural(*q_other)
            wide = 3 * qkv[0].shape[2]
            g_qkv = sums(*[v[:, :wide].reshape(d, 3, -1) for v in q], 2)
            g_qb = sums(*[v[:, wide].reshape(2, -1) for v in q], 1)
            small_two = [v[:, half + side :].T for v in u]
            g_bu = sums(*[v[4:6].reshape(-1) for v in small_two], 0)
            shared_two = lax.psum(small_two[0][:4], ("dp", "tensor")).astype(F32)
            vectors = (q[0] + q[1])[:, wide + 1 : wide + 3].T
            shared_one = lax.psum(vectors, ("dp", "tensor")).astype(F32)
        return (
            layer_out, input_grad, shared_one[0], shared_one[1], g_qkv, g_qb, g_out, shared_two[2],
            shared_two[0], shared_two[1], g_up, g_bu, g_down, shared_two[3],
        )

    return body


def solution(mesh):
    in_specs = (
        P(("dp", "tensor"), None), P(("dp", "tensor"), None), P("dp"), P("dp", None), P("dp", None), P(), P(),
        P(None, None, "tensor"), P(None, "tensor"), P("tensor", None), P(), P(), P(), P(None, "tensor"),
        P("tensor"), P("tensor", None), P(),
    )
    out_specs = (
        P(("dp", "tensor"), None), P(("dp", "tensor"), None), P(), P(), P(None, None, "tensor"), P(None, "tensor"),
        P("tensor", None), P(), P(), P(), P(None, "tensor"), P("tensor"), P("tensor", None), P(),
    )
    return jax.shard_map(make_body(mesh), mesh=mesh, in_specs=in_specs, out_specs=out_specs, check_vma=False)
```

```python
import jax
import jax.numpy as jnp
from jax import lax
from jax.experimental import pallas as pl
from jax.experimental.pallas import tpu as pltpu
from jax.sharding import PartitionSpec as P

HEAD_DIM = 64
SEQ_LEN = 1024
LEFT = 10
RIGHT = 2
QB = 64
MARGIN = 16
WIN = QB + 2 * MARGIN
NBLK = SEQ_LEN // QB
EPS = 1e-05
LN_ROWS = 256
NEG = -1000000000.0
F32 = jnp.float32
BF16 = jnp.bfloat16


def dot_nn(a, b):
    return jnp.dot(a, b, preferred_element_type=F32)


def dot_nt(a, b):
    return lax.dot_general(a, b, (((1,), (1,)), ((), ())), preferred_element_type=F32)


def dot_tn(a, b):
    return lax.dot_general(a, b, (((0,), (0,)), ((), ())), preferred_element_type=F32)


def length_of(scal, seq):
    return scal[4 + scal[2] + seq]


def keep_of(shape, first_pos, seq, scal):
    seqs = (scal.shape[0] - 4) // 5
    ends = [scal[4 + k * seqs + scal[2] + seq] for k in range(1, 5)]
    pos = first_pos + lax.broadcasted_iota(jnp.int32, (shape[0], 1), 0)
    col = lax.broadcasted_iota(jnp.int32, (1, shape[1]), 1)
    rows = jnp.where((pos >= ends[0]) & (pos < ends[1]), 0.0, 1.0)
    cols = jnp.where((col >= ends[2]) & (col < ends[3]), 0.0, 1.0)
    return rows * cols


def normalize(v):
    off = v - jnp.mean(v, axis=-1, keepdims=True)
    r = lax.rsqrt(jnp.mean(off * off, axis=-1, keepdims=True) + EPS)
    return off * r, r


def head_mask(scale, heads):
    row = lax.broadcasted_iota(jnp.int32, (heads * QB, heads * HEAD_DIM), 0)
    col = lax.broadcasted_iota(jnp.int32, (heads * QB, heads * HEAD_DIM), 1)
    return jnp.where(row // QB == col // HEAD_DIM, scale, 0.0).astype(BF16)


def spread(block, mask, heads):
    return jnp.concatenate([block] * heads, axis=0) * mask


def pair_rows(probs, window, heads):
    out = []
    low = lax.broadcasted_iota(jnp.int32, (QB, 2 * HEAD_DIM), 1) < HEAD_DIM
    for p in range(heads // 2):
        both = dot_tn(
            probs[:, p * 2 * QB : (p + 1) * 2 * QB],
            window[:, p * 2 * HEAD_DIM : (p + 1) * 2 * HEAD_DIM],
        )
        out.append(jnp.where(low, both[:QB], both[QB:]))
    return jnp.concatenate(out, axis=1)


def attend(length, proj, kpad, vpad, scores, ctx, probs_out, heads):
    width = heads * HEAD_DIM
    edge = jnp.zeros((MARGIN, width), BF16)
    for pad, j in ((kpad, 1), (vpad, 2)):
        pad[0:MARGIN, :] = edge
        pad[MARGIN + SEQ_LEN :, :] = edge
        pad[MARGIN : MARGIN + SEQ_LEN, :] = proj[:, j * width : (j + 1) * width]
    mask = head_mask(HEAD_DIM**-0.5, heads)
    key = lax.broadcasted_iota(jnp.int32, (WIN, heads * QB), 0)
    query = lax.broadcasted_iota(jnp.int32, (WIN, heads * QB), 1) % QB
    rel = key - MARGIN - query
    band = jnp.where((rel >= -LEFT) & (rel <= RIGHT), 0.0, NEG)
    diagonal = jnp.where(rel == 0, 0.0, NEG)

    for b in range(NBLK):
        q_all = spread(proj[b * QB : (b + 1) * QB, 0:width], mask, heads)
        scores[b * WIN : (b + 1) * WIN, :] = dot_nt(kpad[b * QB : b * QB + WIN, :], q_all)
    for b in range(NBLK):
        at = slice(b * WIN, (b + 1) * WIN)
        pos = key + (b * QB - MARGIN)
        live = (pos < length) if b else (pos >= 0) & (pos < length)
        masked = scores[at, :] + jnp.where(live, band, diagonal)
        weights = jnp.exp(masked - jnp.max(masked, axis=0, keepdims=True))
        probs_out[at, :] = (weights / jnp.sum(weights, axis=0, keepdims=True)).astype(BF16)
    for b in range(NBLK):
        v_win = vpad[b * QB : b * QB + WIN, :]
        ctx[b * QB : (b + 1) * QB, :] = pair_rows(probs_out[b * WIN : (b + 1) * WIN, :], v_win, heads).astype(BF16)


def project(at, n1, w_side, bias, proj):
    width = bias.shape[1]
    value = dot_nn(n1[at, :], w_side[...])
    proj[at, :width] = (value[:, :width] + bias[0:1, :]).astype(BF16)
    proj[at, width : 2 * width] = value[:, width : 2 * width].astype(BF16)
    proj[at, 2 * width :] = (value[:, 2 * width :] + bias[1:2, :]).astype(BF16)


def parts_in_order(scal, mine, theirs):
    odd = jnp.where(scal[3] == 0, 0, 1)
    return ((mine, odd), (theirs, 1 - odd))


def first_kernel(heads, scal, x, w, bias, gain, shift, nn, n1, proj, ctx, probs, w_side, *scratch):
    s = pl.program_id(0)

    @pl.when(s == 0)
    def _():
        width = w.shape[2]
        for j in range(3):
            w_side[:, j * width : (j + 1) * width] = w[j]

    for first in range(0, SEQ_LEN, LN_ROWS):
        at = slice(first, first + LN_ROWS)
        for r in range(first, first + LN_ROWS, SUB):
            sub = slice(r, r + SUB)
            keep = keep_of((SUB, x.shape[1]), r, s, scal)
            value = normalize(x[sub, :].astype(F32) * keep)[0]
            nn[sub, :] = value.astype(BF16)
            n1[sub, :] = (value * gain[...] + shift[...]).astype(BF16)
        project(at, n1, w_side, bias, proj)
    attend(length_of(scal, s), proj, *scratch, ctx, probs, heads)


def second_kernel(heads, scal, n1, mine, theirs, bias, proj, ctx, probs, w_side, *scratch):
    s = pl.program_id(0)

    @pl.when(s == 0)
    def _():
        width = bias.shape[1]
        half = n1.shape[1] // 2
        for part, place_of in parts_in_order(scal, mine, theirs):
            for k in range(3):
                stretch = 3 * place_of + k
                row = pl.multiple_of((stretch % 2) * half, half)
                column = pl.multiple_of((stretch // 2) * width, width)
                w_side[pl.ds(row, half), pl.ds(column, width)] = part[k * half : (k + 1) * half, :]

    for first in range(0, SEQ_LEN, LN_ROWS):
        project(slice(first, first + LN_ROWS), n1, w_side, bias, proj)
    attend(length_of(scal, s), proj, *scratch, ctx, probs, heads)


def const_spec(shape):
    return pl.BlockSpec(shape, lambda *_: (0,) * len(shape), pipeline_mode=pl.Buffered(1))


def rows_spec(rows, cols):
    return pl.BlockSpec((rows, cols), lambda i, *_: (i, 0))


NEEDS = {
    "attend_first": 60, "attend_second": 60, "feed_up": 60, "feed_back": 44, "attend_back": 60,
    "input_gradient": 60, "layer_out": 57, "unpack": 20,
}


def params(name):
    return pltpu.CompilerParams(vmem_limit_bytes=NEEDS[name] * 1024 * 1024, dimension_semantics=("arbitrary",))


def attention_forward(first, scal, rows, w, bias, gain, shift):
    total, width_in = rows.shape
    seqs = total // SEQ_LEN
    width = bias.shape[1]
    heads = width // HEAD_DIM
    outs = [
        jax.ShapeDtypeStruct((total, 3 * width), BF16),
        jax.ShapeDtypeStruct((total, width), BF16),
        jax.ShapeDtypeStruct((seqs * NBLK * WIN, heads * QB), BF16),
        jax.ShapeDtypeStruct((width_in, 3 * width), BF16),
    ]
    out_specs = [
        rows_spec(SEQ_LEN, 3 * width),
        rows_spec(SEQ_LEN, width),
        rows_spec(NBLK * WIN, heads * QB),
        const_spec((width_in, 3 * width)),
    ]
    scratch = [pltpu.VMEM((SEQ_LEN + 2 * MARGIN, width), BF16)] * 2
    scratch += [pltpu.VMEM((NBLK * WIN, heads * QB), F32)]
    flops = 2 * total * width_in * 3 * width + 8 * total * WIN * width
    cost = pl.CostEstimate(flops=flops, bytes_accessed=total * (width_in + 6 * width) * 2, transcendentals=0)
    if first:
        in_specs = [rows_spec(SEQ_LEN, width_in)] + [const_spec(v.shape) for v in (w, bias, gain, shift)]
        outs = [jax.ShapeDtypeStruct(rows.shape, BF16)] * 2 + outs
        out_specs = [rows_spec(SEQ_LEN, width_in)] * 2 + out_specs
        args = (rows, w, bias, gain, shift)
    else:
        half_spec = pl.BlockSpec((3 * width_in // 2, width), lambda *_: (0, 0), pipeline_mode=pl.Buffered(1))
        in_specs = [rows_spec(SEQ_LEN, width_in), half_spec, half_spec, const_spec(bias.shape)]
        args = (rows, *w, bias)

    def body(*refs):
        (first_kernel if first else second_kernel)(heads, *refs)

    return pl.pallas_call(
        body,
        grid_spec=pltpu.PrefetchScalarGridSpec(
            num_scalar_prefetch=1,
            grid=(seqs,),
            in_specs=in_specs,
            out_specs=out_specs,
            scratch_shapes=scratch,
        ),
        out_shape=outs,
        compiler_params=params("attend_first" if first else "attend_second"),
        cost_estimate=cost,
        name="attend_first" if first else "attend_second",
    )(scal, *args)


TM = 512
TU = 1024
TB = 512
FC = 512
FB = 512
SUB = 32
GELU_A = 0.7978845608028654
GELU_K = 0.044715 / 0.7978845608028654**2


def subs(rows):
    return [slice(r, r + SUB) for r in range(0, rows, SUB)]


def fold_rows(v):
    return jnp.sum(v.reshape(-1, 8, v.shape[-1]), axis=0)


def clear(i, *refs):
    @pl.when(i == 0)
    def _():
        for ref in refs:
            ref[...] = jnp.zeros_like(ref)


TAIL = 2
ONES = 16
EXTRA = 128
BLOCKS = 16


def put_blocks(me, packs, acc, columns):
    rows = packs[0].shape[1]
    each = BLOCKS // len(packs)
    for j in range(BLOCKS):
        first = pl.multiple_of((j ^ me) * rows, rows)
        packs[j // each][j % each] = acc[pl.ds(first, rows), columns].astype(BF16)


def put_vectors(acc, first, vectors):
    spare = EXTRA - len(vectors)
    rows = vectors[0].shape[1]
    acc[:rows, first:] = jnp.concatenate(vectors + [jnp.zeros((spare, rows), F32)], axis=0).T


def bias_chunk(biases, first, count):
    width = biases.shape[1]
    rows = range(2 + first // width, 2 + (first + count) // width)
    return jnp.concatenate([biases[r : r + 1, :] for r in rows], axis=1)


def up_kernel(
    per_seq, scal,
    x, cot, ctx_a, ctx_b, wo_a, wo_m, wo_t, wu_a, wu_m, wu_t, bo, gain, shift, bias_a, bias_b,
    mid_out, n2_out, hidden_out, pre_out, pack_own, pack_other, wo_s, wu_b,
    acc_d, ctx_s, branch, n2_half, pre_even, pre_odd,
):
    i = pl.program_id(0)
    clear(i, acc_d)
    width = ctx_a.shape[1]

    @pl.when(i == 0)
    def _():
        wo_s[:width, :] = wo_a[...]
        side, half_rows = wo_m.shape[1], wu_m.shape[0]
        for part, place_of in parts_in_order(scal, wo_m, wo_t):
            wo_s[width:, pl.ds(pl.multiple_of(place_of * side, side), side)] = part[...]
        for part, place_of in parts_in_order(scal, wu_m, wu_t):
            wu_b[pl.ds(pl.multiple_of(place_of * half_rows, half_rows), half_rows), :] = part[...]

    rows = x.shape[0]
    ctx_s[:, :width] = ctx_a[...]
    ctx_s[:, width:] = ctx_b[...]
    branch[...] = dot_nn(ctx_s[...], wo_s[...])
    g_t = cot[...].T
    for sub in subs(rows):
        keep = keep_of((SUB, x.shape[1]), (i % per_seq) * rows + sub.start, i // per_seq, scal)
        mid = x[sub, :].astype(F32) * keep + branch[sub, :] + bo[...]
        mid_out[sub, :] = mid
        n2 = (normalize(mid)[0] * gain[...] + shift[...]).astype(BF16)
        n2_out[sub, :] = n2
        n2_half[sub, :] = n2 * 0.5
    half = wu_a.shape[1]
    chunks = [(part, c) for part in range(2) for c in range(half // FC)]
    pres = (pre_even, pre_odd)

    def up(n):
        part, c = chunks[n]
        pres[n % 2][...] = dot_nn(n2_half[...], (wu_a, wu_b)[part][:, c * FC : (c + 1) * FC])

    up(0)
    for n, (part, c) in enumerate(chunks):
        if n + 1 < len(chunks):
            up(n + 1)
        bias = bias_chunk((bias_a, bias_b)[part], c * FC, FC) * 0.5
        ts = slice(part * half + c * FC, part * half + (c + 1) * FC)
        for sub in subs(rows):
            v = pres[n % 2][sub, :] + bias
            z = v * (2 * GELU_A)
            pre_out[sub, ts] = z.astype(BF16)
            t = jnp.tanh(z * (1.0 + GELU_K * (z * z)))
            hidden_out[sub, ts] = (v + v * t).astype(BF16)
        acc_d[:, ts] += dot_nn(g_t, hidden_out[:, ts])

    @pl.when(i == pl.num_programs(0) - 1)
    def _():
        put_blocks(scal[1], [pack_own], acc_d, slice(0, half))
        put_blocks(scal[1], [pack_other], acc_d, slice(half, 2 * half))


def call(kernel, name, grid, scalars, in_specs, outs, out_specs, scratch, flops, nbytes, args, alias=()):
    return pl.pallas_call(
        kernel,
        grid_spec=pltpu.PrefetchScalarGridSpec(
            num_scalar_prefetch=len(scalars), grid=(grid,), in_specs=in_specs, out_specs=out_specs,
            scratch_shapes=scratch,
        ),
        out_shape=[jax.ShapeDtypeStruct(s, t) for s, t in outs],
        compiler_params=params(name),
        input_output_aliases=dict(alias),
        cost_estimate=pl.CostEstimate(flops=flops, bytes_accessed=nbytes, transcendentals=0),
        name=name,
    )(*scalars, *args)


def up_block(scal, x, cot, ctx_a, ctx_b, wo_a, wu_a, parts, bo, gain, shift, biases):
    total, d = x.shape
    width = ctx_a.shape[1]
    half = wu_a.shape[1]
    args = (x, cot, ctx_a, ctx_b, wo_a, *parts[0], wu_a, *parts[1], bo, gain, shift, *biases)
    in_specs = [rows_spec(TU, d), rows_spec(TU, d), rows_spec(TU, width), rows_spec(TU, width)]
    tail_spec = lambda v: pl.BlockSpec(
        (width, v.shape[1]), lambda *_: (v.shape[0] // width - 1, 0), pipeline_mode=pl.Buffered(1)
    )
    in_specs += [tail_spec(v) if k in (1, 2) else const_spec(v.shape) for k, v in enumerate(args[4:])]
    pack = (BLOCKS, d // BLOCKS, half)
    outs = [
        ((total, d), F32), ((total, d), BF16), ((total, 2 * half), BF16), ((total, 2 * half), BF16),
        (pack, BF16), (pack, BF16), ((2 * width, d), BF16), ((d, half), BF16),
    ]
    out_specs = [rows_spec(TU, d), rows_spec(TU, d), rows_spec(TU, 2 * half), rows_spec(TU, 2 * half)]
    out_specs += [const_spec(s) for s, _ in outs[4:]]
    scratch = [
        pltpu.VMEM((d, 2 * half), F32), pltpu.VMEM((TU, 2 * width), BF16),
        pltpu.VMEM((TU, d), F32), pltpu.VMEM((TU, d), BF16), pltpu.VMEM((TU, FC), F32), pltpu.VMEM((TU, FC), F32),
    ]

    def body(*refs):
        up_kernel(SEQ_LEN // TU, *refs)

    return call(
        body, "feed_up", total // TU, (scal,), in_specs, outs, out_specs, scratch,
        2 * total * d * (4 * half + 2 * width), total * (18 * d + 8 * half), args,
    )


def down_kernel(
    scal,
    cot, mid, n2_in, pre, ctx_a, ctx_b, wo_s, wu_a, wu_b, wd_a, wd_b, gain,
    gmid_out, gctx_a, gctx_b, keep_own, keep_other, send_own, send_other,
    acc_own, acc_other, acc_small, ctx_s, n2_t, gh_even, gh_odd, gpre, back_a, back_b,
):
    i = pl.program_id(0)
    clear(i, acc_own, acc_other, acc_small)
    width = ctx_a.shape[1]

    rows = cot.shape[0]
    ctx_s[:, :width] = ctx_a[...]
    ctx_s[:, width:] = ctx_b[...]
    n2_t[:-ONES, :] = n2_in[...].T
    n2_t[-ONES:, :] = jnp.ones((ONES, rows), BF16)
    half = wu_a.shape[1]
    chunks = [(part, c) for part in range(2) for c in range(half // FB)]
    ghs = (gh_even, gh_odd)

    def up(n):
        part, c = chunks[n]
        ghs[n % 2][...] = dot_nt(cot[...], (wd_a, wd_b)[part][c * FB : (c + 1) * FB, :]).astype(BF16)

    def vector(n):
        part, c = chunks[n]
        ts = slice(part * half + c * FB, part * half + (c + 1) * FB)
        for sub in subs(rows):
            z = pre[sub, ts]
            k = z * z * GELU_K
            t = jnp.tanh(z * (k + 1.0))
            slope = (t + 1.0) * ((z * (k * 1.5 + 0.5)) * (1.0 - t) + 0.5)
            gpre[sub, ts] = slope * ghs[n % 2][sub, :]

    def use(n):
        part, c = chunks[n]
        ts = slice(part * half + c * FB, part * half + (c + 1) * FB)
        (acc_own, acc_other)[part][:, c * FB : (c + 1) * FB] += dot_nn(n2_t[...], gpre[:, ts])

    up(0)
    for n in range(len(chunks)):
        if n + 1 < len(chunks):
            up(n + 1)
        if n:
            use(n - 1)
        vector(n)
    use(len(chunks) - 1)
    sums = [jnp.zeros((8, cot.shape[1]), F32) for _ in range(4)]
    side = cot.shape[1] // 2
    parts = [slice(k * rows // TAIL, (k + 1) * rows // TAIL) for k in range(TAIL)]

    def back(at):
        back_a[at, :] = dot_nt(gpre[at, :half], wu_a[...])
        back_b[at, :] = dot_nt(gpre[at, half:], wu_b[...])

    back(parts[0])
    for k, at in enumerate(parts):
        if k + 1 < TAIL:
            back(parts[k + 1])
        for r in range(at.start, at.stop, SUB):
            sub = slice(r, r + SUB)
            gn2 = back_a[sub, :] + back_b[sub, :]
            nn, r_std = normalize(mid[sub, :])
            gnn = gn2 * nn
            u = gn2 * gain[...]
            mean_un = jnp.mean(gnn * gain[...], axis=-1, keepdims=True)
            g = cot[sub, :].astype(F32)
            gm = g + r_std * (u - jnp.mean(u, axis=-1, keepdims=True) - nn * mean_un)
            gmid_out[sub, :] = gm.astype(BF16)
            for q, term in enumerate((gnn, gn2, gm, g)):
                sums[q] += fold_rows(term)
        gctx = dot_nt(gmid_out[at, :], wo_s[...])
        gctx_a[at, :] = gctx[:, :width].astype(BF16)
        gctx_b[at, :] = gctx[:, width:].astype(BF16)
    both = dot_tn(ctx_s[...], gmid_out[...])
    for acc, part in ((acc_own, both[:width]), (acc_other, both[width:])):
        acc[:width, half : half + side] += part[:, :side]
        acc[width : 2 * width, half : half + side] += part[:, side:]
    for k in range(4):
        acc_small[8 * k : 8 * k + 8, :] += sums[k]

    @pl.when(i == pl.num_programs(0) - 1)
    def _():
        vectors = [jnp.sum(acc_small[8 * k : 8 * k + 8, :], axis=0, keepdims=True) for k in range(4)]
        d = cot.shape[1]
        for acc, keep, send in ((acc_own, keep_own, send_own), (acc_other, keep_other, send_other)):
            mine = acc[d : d + 1, :half]
            put_vectors(acc, half + side, vectors + [mine[:, :d], mine[:, d:]])
            put_blocks(scal[0], [keep, send], acc, slice(None))


def down_block(scal, cot, mid, n2, pre, ctx_a, ctx_b, wo, wu, wd, gain):
    total, d = cot.shape
    width = ctx_a.shape[1]
    half = wu[0].shape[1]
    args = (cot, mid, n2, pre, ctx_a, ctx_b, wo, *wu, *wd, gain)
    in_specs = [rows_spec(TB, d), rows_spec(TB, d), rows_spec(TB, d), rows_spec(TB, 2 * half)]
    in_specs += [rows_spec(TB, width), rows_spec(TB, width)]
    in_specs += [const_spec(a.shape) for a in args[6:]]
    columns = half + d // 2 + EXTRA
    pack = (BLOCKS // 2, d // BLOCKS, columns)
    outs = [((total, d), BF16), ((total, width), BF16), ((total, width), BF16), *[(pack, BF16)] * 4]
    out_specs = [rows_spec(TB, d), rows_spec(TB, width), rows_spec(TB, width)]
    out_specs += [const_spec(s) for s, _ in outs[3:]]
    scratch = [
        pltpu.VMEM((d + ONES, columns), F32), pltpu.VMEM((d + ONES, columns), F32),
        pltpu.VMEM((32, d), F32), pltpu.VMEM((TB, 2 * width), BF16),
        pltpu.VMEM((d + ONES, TB), BF16),
        pltpu.VMEM((TB, FB), BF16), pltpu.VMEM((TB, FB), BF16), pltpu.VMEM((TB, 2 * half), BF16),
        pltpu.VMEM((TB, d), F32), pltpu.VMEM((TB, d), F32),
    ]
    return call(
        down_kernel, "feed_back", total // TB, (scal,), in_specs, outs, out_specs, scratch,
        2 * total * d * (6 * half + 4 * width), total * (16 * d + 4 * half), args,
    )


def out_rows(mid, hidden, wd_a, wd_b, bd, out):
    half = wd_a.shape[0]
    out[...] = (
        mid[...] + dot_nn(hidden[:, :half], wd_a[...]) + dot_nn(hidden[:, half:], wd_b[...]) + bd[...]
    ).astype(BF16)


def out_kernel(scal, mid, hidden, wd_a, wd_b, bd, *refs):
    out_rows(mid, hidden, wd_a, wd_b, bd, refs[-1])


def out_down_kernel(scal, mid, hidden, wd_a, wd_b, bd, before, d0, d1, out, down, d_all):
    out_rows(mid, hidden, wd_a, wd_b, bd, out)

    @pl.when(pl.program_id(0) == 0)
    def _():
        place(scal[1], (d0, d1), d_all, BF16)
        down[...] = d_all[...].T.astype(F32)


def part_spec(first, cols):
    return pl.BlockSpec((TM, cols), lambda i, *_: (i + first, 0))


def out_block(first, tiles, scal, mid, hidden, wd, bd, before, pieces=()):
    total, d = mid.shape
    args = (mid, hidden, *wd, bd)
    specs = [part_spec(first, d), part_spec(first, hidden.shape[1])]
    specs += [const_spec(a.shape) for a in (*wd, bd)]
    alias = {}
    if before is not None:
        alias = {len(args) + 1: 0}
        args += (before,)
        specs += [pl.BlockSpec(memory_space=pl.ANY)]
    outs, out_specs, scratch = [((total, d), BF16)], [part_spec(first, d)], []
    if pieces:
        args += tuple(pieces)
        specs += [const_spec(p.shape) for p in pieces]
        shape = (pieces[0].shape[2], d)
        outs += [(shape, F32)]
        out_specs += [const_spec(shape)]
        scratch = [pltpu.VMEM(shape[::-1], BF16)]
    return call(
        out_down_kernel if pieces else out_kernel, "layer_out", tiles, (scal,), specs, outs, out_specs, scratch,
        2 * tiles * TM * d * hidden.shape[1], tiles * TM * (6 * d + 2 * hidden.shape[1]), args, alias,
    )


def attend_back_kernel(
    heads, scal, nn, proj, probs, gctx, w, gain, shift, gproj, pack_keep, pack_send, kpad, vpad, dk, dv, acc, acc_b, gprob, gscore
):
    s = pl.program_id(0)
    clear(s, acc, acc_b)
    width = heads * HEAD_DIM
    edge = jnp.zeros((MARGIN, width), BF16)
    for pad, j in ((kpad, 1), (vpad, 2)):
        pad[0:MARGIN, :] = edge
        pad[MARGIN + SEQ_LEN :, :] = edge
        pad[MARGIN : MARGIN + SEQ_LEN, :] = proj[:, j * width : (j + 1) * width]
    mask = head_mask(1.0, heads)
    dk[0 : 2 * MARGIN, :] = jnp.zeros((2 * MARGIN, width), F32)
    dv[0 : 2 * MARGIN, :] = jnp.zeros((2 * MARGIN, width), F32)
    scale = HEAD_DIM**-0.5

    def rows(b):
        return slice(b * QB, (b + 1) * QB)

    def keys(b):
        return slice(b * QB, b * QB + WIN)

    def own(b):
        return slice(b * WIN, (b + 1) * WIN)

    for b in range(NBLK):
        gprob[own(b), :] = dot_nt(vpad[keys(b), :], spread(gctx[rows(b), :], mask, heads))
    for b in range(NBLK):
        p = probs[own(b), :].astype(F32)
        gp = gprob[own(b), :]
        gscore[own(b), :] = (p * (gp - jnp.sum(p * gp, axis=0, keepdims=True))).astype(BF16)
    for b in range(NBLK):
        gproj[rows(b), 0:width] = (pair_rows(gscore[own(b), :], kpad[keys(b), :], heads) * scale).astype(BF16)
    for b in range(NBLK):
        key_term = dot_nn(gscore[own(b), :], spread(proj[rows(b), 0:width], mask, heads)) * scale
        value_term = dot_nn(probs[own(b), :], spread(gctx[rows(b), :], mask, heads))
        for total, term in ((dk, key_term), (dv, value_term)):
            total[b * QB : b * QB + 2 * MARGIN, :] += term[: 2 * MARGIN]
            total[b * QB + 2 * MARGIN : b * QB + WIN, :] = term[2 * MARGIN :]
    gproj[:, width : 2 * width] = dk[MARGIN : MARGIN + SEQ_LEN, :].astype(BF16)
    gproj[:, 2 * width :] = dv[MARGIN : MARGIN + SEQ_LEN, :].astype(BF16)
    gp_all = gproj[...]
    acc[:, : 3 * width] += dot_tn(nn[...], gp_all)
    acc_b[...] += jnp.sum(gp_all.astype(F32), axis=0, keepdims=True)

    @pl.when(s == pl.num_programs(0) - 1)
    def _():
        d = acc.shape[0]
        column = lambda v: jnp.broadcast_to(v[...], (EXTRA, d)).T[:, 0:1]
        gain_col, shift_col = column(gain), column(shift)
        gain_grad, shift_grad = jnp.zeros((d, EXTRA), F32), jnp.zeros((d, EXTRA), F32)
        for j in range(3):
            for c in range(0, width, EXTRA):
                at = slice(j * width + c, j * width + c + EXTRA)
                weight = w[:, at].astype(F32)
                total, sums = acc[:, at], acc_b[:, at]
                gain_grad += weight * total
                shift_grad += weight * sums
                acc[:, at] = gain_col * total + shift_col * sums
        gain_grad = jnp.sum(gain_grad, axis=1, keepdims=True)
        shift_grad = jnp.sum(shift_grad, axis=1, keepdims=True)
        put_vectors(acc, 3 * width, [jnp.concatenate([acc_b[:, :width], acc_b[:, 2 * width :]], axis=1)])
        lane = lax.broadcasted_iota(jnp.int32, (d, EXTRA), 1)
        extra = jnp.where(lane == 1, gain_grad, acc[:, 3 * width :])
        acc[:, 3 * width :] = jnp.where(lane == 2, shift_grad, extra)
        put_blocks(scal[1], [pack_keep, pack_send], acc, slice(None))


def attention_backward(scal, nn, proj, probs, gctx, w, gain, shift):
    total, d = nn.shape
    seqs = total // SEQ_LEN
    width = gctx.shape[1]
    heads = width // HEAD_DIM

    def body(*refs):
        attend_back_kernel(heads, *refs)

    pad = SEQ_LEN + 2 * MARGIN
    columns = 3 * width + EXTRA
    pack = (BLOCKS // 2, d // BLOCKS, columns)
    return call(
        body, "attend_back", seqs, (scal,),
        [
            rows_spec(SEQ_LEN, d), rows_spec(SEQ_LEN, 3 * width),
            rows_spec(NBLK * WIN, heads * QB), rows_spec(SEQ_LEN, width),
            const_spec(w.shape), const_spec(gain.shape), const_spec(shift.shape),
        ],
        [((total, 3 * width), BF16), (pack, BF16), (pack, BF16)],
        [rows_spec(SEQ_LEN, 3 * width), const_spec(pack), const_spec(pack)],
        [
            pltpu.VMEM((pad, width), BF16), pltpu.VMEM((pad, width), BF16),
            pltpu.VMEM((pad, width), F32), pltpu.VMEM((pad, width), F32),
            pltpu.VMEM((d, columns), F32), pltpu.VMEM((1, 3 * width), F32),
            pltpu.VMEM((NBLK * WIN, heads * QB), F32), pltpu.VMEM((NBLK * WIN, heads * QB), BF16),
        ],
        2 * total * d * 3 * width + 16 * total * WIN * width, total * (d + 9 * width) * 2,
        (nn, proj, probs, gctx, w, gain, shift),
    )


def last_kernel(per_seq, first, scal, x, gmid, gp_a, gp_b, w_a, w_b, gain, *refs):
    gin, back_a, back_b = refs[-3:]
    i = pl.program_id(0)
    rows = x.shape[0]
    tile = i + first
    back_a[...] = dot_nt(gp_a[...], w_a[...])
    back_b[...] = dot_nt(gp_b[...], w_b[...])
    for sub in subs(rows):
        keep = keep_of((SUB, x.shape[1]), (tile % per_seq) * rows + sub.start, tile // per_seq, scal)
        nn, r = normalize(x[sub, :].astype(F32) * keep)
        u = (back_a[sub, :] + back_b[sub, :]) * gain[...]
        mean_un = jnp.mean(u * nn, axis=-1, keepdims=True)
        a = r * (u - jnp.mean(u, axis=-1, keepdims=True) - nn * mean_un)
        gin[sub, :] = (gmid[sub, :].astype(F32) + a) * keep


def last_block(part, parts, scal, x, gmid, gp_a, gp_b, w_a, w_b, gain, before):
    total, d = x.shape
    tiles = total // TM // parts

    def body(*refs):
        last_kernel(SEQ_LEN // TM, part * tiles, *refs)

    width = gp_a.shape[1]
    args = (x, gmid, gp_a, gp_b, w_a, w_b, gain)
    specs = [part_spec(part * tiles, c) for c in (d, d, width, width)]
    specs += [const_spec(a.shape) for a in args[4:]]
    alias = {}
    if before is not None:
        alias = {len(args) + 1: 0}
        args += (before,)
        specs += [pl.BlockSpec(memory_space=pl.ANY)]
    return call(
        body, "input_gradient", tiles, (scal,), specs, [((total, d), F32)], [part_spec(part * tiles, d)],
        [pltpu.VMEM((TM, d), F32)] * 2,
        4 * tiles * TM * d * width, tiles * TM * (10 * d + 4 * width), args, alias,
    )[0]


def place(me, pieces, out, kind, columns=slice(None)):
    each = pieces[0].shape[0]
    rows = pieces[0].shape[1]
    for j in range(BLOCKS):
        at = pl.ds(pl.multiple_of((j ^ me) * rows, rows), rows)
        out[at, :] = pieces[j // each][j % each, :, columns].astype(kind)


def unpack_kernel(scal, u0, u1, q0, q1, side_y, side_d, up, out, *refs):
    vectors, (bias_up, qkv, bias_q, gain, shift, u_side, q_all, q_side) = refs[:4], refs[4:]
    me = scal[0]
    half, side = up.shape[1], out.shape[1] // 2
    rows = out.shape[0]
    place(me, (u0, u1), up, F32, slice(0, half))
    place(me, (u0, u1), u_side, F32, slice(half, u0.shape[2]))
    out[:, :side] = u_side[:rows, :side]
    out[:, side:] = u_side[rows:, :side]
    sums = u_side[:, side:].T
    for k in range(4):
        vectors[k][...] = sums[k : k + 1, :]
    bias_up[...] = jnp.concatenate([sums[4:5, :], sums[5:6, :]], axis=1)
    place(scal[1], (q0, q1), q_all, F32)
    width = qkv.shape[2]
    for j in range(3):
        qkv[j] = q_all[:, j * width : (j + 1) * width]
    sums = q_all[:, 3 * width :].T
    bias_q[...] = jnp.concatenate([sums[0:1, :width], sums[0:1, width:]], axis=0)
    place(scal[1], (side_y, side_d), q_side, F32)
    sums += q_side[...].T
    gain[...] = sums[1:2, :]
    shift[...] = sums[2:3, :]


def unpack(scal, pieces, up, out, qkv):
    d = up[0]
    shapes = [up, out, *[(1, d)] * 4, (1, up[1]), qkv, (2, qkv[2]), (1, d), (1, d)]
    natural = [(d, pieces[0].shape[2] - up[1]), (d, pieces[2].shape[2]), (d, EXTRA)]
    return call(
        unpack_kernel, "unpack", 1, (scal,), [const_spec(p.shape) for p in pieces], [(s, F32) for s in shapes],
        [const_spec(s) for s in shapes], [pltpu.VMEM(s, F32) for s in natural], 0,
        6 * sum(p.size for p in pieces), tuple(pieces),
    )


def make_body(mesh):
    tp = mesh.shape["tensor"]
    dp = mesh.shape["dp"]
    paired = tp == 2 and dp == BLOCKS

    def across(v):
        return lax.ppermute(v, "tensor", [(0, 1), (1, 0)])

    def swap(v, distance):
        return lax.ppermute(v, "dp", [(i, i ^ distance) for i in range(dp)])

    def core(v):
        return swap(v, 1)

    def diagonal(v):
        pairs = [(2 * i + j, 2 * (i ^ 1) + 1 - j) for i in range(dp) for j in range(2)]
        return lax.ppermute(v, ("dp", "tensor"), pairs)

    def plus(first, *rest):
        total = first.astype(F32)
        for v in rest:
            total = total + v.astype(F32)
        return total.astype(first.dtype)

    def lower(v):
        return v[: v.shape[0] // 2]

    def upper(v):
        return v[v.shape[0] // 2 :]

    def join(a, b):
        return jnp.concatenate([a, b], axis=0)

    def window(kernel, args, moves):
        args, sent = lax.optimization_barrier((args, [v for v, _ in moves]))
        arrived = [move(v) for v, (_, move) in zip(sent, moves)]
        return lax.optimization_barrier((kernel(*args), arrived, sent))

    def body(
        inputs, cotangent, lengths, time_span, freq_span, gain_one, shift_one, qkv_weight, qkv_bias,
        out_weight, out_bias, gain_two, shift_two, up_weight, up_bias, down_weight, down_bias,
    ):
        total, d = inputs.shape
        seqs = total // SEQ_LEN
        here = lax.axis_index("tensor") * seqs
        index = lax.axis_index("dp")
        label = label_q = jnp.int32(0)
        if paired:
            label = ((index & 1) << 3) | ((index & 2) << 1) | ((index & 4) >> 1)
            label_q = ((index & 1) << 3) | (index & 4)
        place_here = jnp.stack([label, label_q, here, index & 1 if paired else jnp.int32(0)]).astype(jnp.int32)
        ends = [span[:, k] for span in (time_span, freq_span) for k in range(2)]
        scal = jnp.concatenate([place_here, lengths, *ends])
        row = lambda v: v.reshape(1, -1)
        stack_biases = lambda b, u: jnp.concatenate([b, u.reshape(-1, b.shape[1])], axis=0)

        def attend_a(rows, w, bias):
            return attention_forward(True, scal, rows, w, bias, row(gain_one), row(shift_one))

        def attend_b(rows, w, bias):
            return attention_forward(False, scal, rows, w, bias, None, None)

        def up(ctx_a, ctx_b, wo_a, wu_a, parts, biases):
            return up_block(
                scal, inputs, cotangent, ctx_a, ctx_b, wo_a, wu_a, parts, row(out_bias), row(gain_two),
                row(shift_two), biases,
            )

        def down(mid, n2, pre, ctx_a, ctx_b, wo, wu, wd):
            return down_block(scal, cotangent, mid, n2, pre, ctx_a, ctx_b, wo, wu, wd, row(gain_two))

        def back(nn, proj, probs, gctx, w):
            return attention_backward(scal, nn, proj, probs, gctx, w, row(gain_one), row(shift_one))

        def last(part, parts):
            return lambda gmid, gp_a, gp_b, w_a, w_b, before: last_block(
                part, parts, scal, inputs, gmid, gp_a, gp_b, w_a, w_b, row(gain_one), before
            )

        def out(first, tiles):
            return lambda mid, hidden, wd, before, *pieces: out_block(
                first, tiles, scal, mid, hidden, wd, row(down_bias), before, pieces
            )

        turned = lambda w: jnp.transpose(w, (1, 0, 2))
        if paired:
            odd = index & 1

            def part_of(v):
                rows = v.shape[0] // 2
                return lax.dynamic_slice_in_dim(v, odd * rows, rows, 0)

            biases = stack_biases(qkv_bias, up_bias)
            qkv_a = turned(qkv_weight)
            side = d // 2
            low, high = qkv_a.reshape(2, -1, side)
            first_rows = jnp.where(
                odd == 0,
                jnp.concatenate([low, out_weight[:, :side]], axis=0),
                jnp.concatenate([high, out_weight[:, side:]], axis=0),
            )
            (nn, n1, proj_a, ctx_a, probs_a, side_a), (first_half, biases_b), _ = window(
                attend_a, (inputs, qkv_a, biases), [(first_rows, across), (biases, across)]
            )
            first_pair = (first_half, core(first_half))
            (proj_b, ctx_b, probs_b, side_b), (up_half,), _ = window(
                attend_b, (n1, first_pair, biases_b), [(part_of(up_weight), across)]
            )
            pairs = (first_pair, (up_half, core(up_half)))
            (mid, n2, hidden, pre, d_own, d_other, wo, up_b), (down_b,), _ = window(
                up, (ctx_a, ctx_b, out_weight, up_weight, pairs, (biases, biases_b)), [(down_weight, across)]
            )
            wu = (up_weight, up_b)
            wd = (down_weight, down_b)
            (gmid, gctx_a, gctx_b, u_own, u_other, u_send_own, u_send_other), (d_cross,), _ = window(
                down, (mid, n2, pre, ctx_a, ctx_b, wo, wu, wd), [(d_other, across)]
            )
            step = lambda distance: lambda v: swap(v, distance)
            u_other, u_own = plus(u_other, core(u_send_other)), plus(u_own, core(u_send_own))
            d_sum = plus(d_own, d_cross)
            d_sum = plus(lower(d_sum), core(upper(d_sum)))
            (gproj_b, q_other, q_send), (u_cross, d_in), _ = window(
                back, (nn, proj_b, probs_b, gctx_b, side_b), [(u_other, across), (upper(d_sum), step(4))]
            )
            u_sum = plus(u_own, u_cross)
            d_sum = plus(lower(d_sum), d_in)
            q_other = plus(q_other, core(q_send))
            (gproj_a, q_own, q_send), (u_in, d_in, q_cross), _ = window(
                back, (nn, proj_a, probs_a, gctx_a, side_a),
                [(upper(u_sum), step(2)), (d_sum, step(8)), (q_other, across)],
            )
            u_sum = plus(lower(u_sum), u_in)
            d_sum = plus(d_sum, d_in)
            q_sum = plus(q_own, core(q_send), q_cross)
            input_grad, (u_in, d_in, q_in), _ = window(
                last(0, 2), (gmid, gproj_a, gproj_b, side_a, side_b, None),
                [(upper(u_sum), step(4)), (d_sum, step(2)), (upper(q_sum), step(4))],
            )
            u_sum = plus(lower(u_sum), u_in)
            d_sum = plus(d_sum, d_in)
            q_sum = plus(lower(q_sum), q_in)
            input_grad, (u_in, d_in, q_in), _ = window(
                last(1, 2), (gmid, gproj_a, gproj_b, side_a, side_b, input_grad),
                [(u_sum, step(8)), (d_sum, step(4)), (q_sum, step(2))],
            )
            u_sum = plus(u_sum, u_in)
            d_sum = join(d_sum, d_in)
            q_sum = plus(q_sum, q_in)
            tiles = total // TM
            cuts = (0, tiles // 2, tiles * 3 // 4, tiles)
            (layer_out,), (u_in, d_in, q_in), _ = window(
                out(cuts[0], cuts[1] - cuts[0]), (mid, hidden, wd, None),
                [(u_sum, step(4)), (d_sum, core), (q_sum, step(8))],
            )
            u_sum = join(u_sum, u_in)
            q_sum = plus(q_sum, q_in)
            (layer_out, g_down), (u_in, q_in), _ = window(
                out(cuts[1], cuts[2] - cuts[1]), (mid, hidden, wd, layer_out, d_sum, d_in),
                [(u_sum, step(2)), (q_sum, step(4))],
            )
            u_sum = join(u_sum, u_in)
            q_sum = join(q_sum, q_in)
            sides = q_sum[:, :, q_sum.shape[2] - EXTRA :]
            (layer_out,), (u_in, q_in, side_y, side_d), _ = window(
                out(cuts[2], cuts[3] - cuts[2]), (mid, hidden, wd, layer_out),
                [(u_sum, core), (q_sum, core), (sides, across), (sides, diagonal)],
            )
            g_up, g_out, *shared_two, g_bu, g_qkv, g_qb, gain_grad, shift_grad = unpack(
                scal, (u_sum, u_in, q_sum, q_in, side_y, side_d), up_weight.shape, out_weight.shape, qkv_a.shape
            )
            g_qkv = turned(g_qkv)
            g_bu = g_bu.reshape(-1)
            shared_two = [v.reshape(-1) for v in shared_two]
            shared_one = [v.reshape(-1) for v in (gain_grad, shift_grad)]
        else:
            def halves(local, axis):
                return tuple(jnp.split(lax.all_gather(local, "tensor", axis=axis, tiled=True), 2, axis=axis))

            def sums(own, other, axis):
                whole = jnp.concatenate([own, other], axis=axis)
                part = lax.psum_scatter(whole, "tensor", scatter_dimension=axis, tiled=True)
                return lax.psum(part, "dp").astype(F32)

            natural = lambda *packs: jnp.concatenate(packs, axis=0).reshape(d, -1)
            qkv = [turned(w) for w in halves(qkv_weight, 2)]
            biases = [stack_biases(q, u) for q, u in zip(halves(qkv_bias, 1), halves(up_bias, 0))]
            wo, wu, wd = halves(out_weight, 0), halves(up_weight, 1), halves(down_weight, 0)
            nn, n1, proj_a, ctx_a, probs_a, side_a = attend_a(inputs, qkv[0], biases[0])
            halves_b = jnp.split(qkv[1].reshape(-1, qkv[1].shape[2]), 2, axis=0)
            proj_b, ctx_b, probs_b, side_b = attend_b(n1, halves_b, biases[1])
            parts = (jnp.split(wo[1], 2, axis=1), jnp.split(wu[1], 2, axis=0))
            mid, n2, hidden, pre, d_own, d_other, wo, _ = up(ctx_a, ctx_b, wo[0], wu[0], parts, biases)
            gmid, gctx_a, gctx_b, *u_packs = down(mid, n2, pre, ctx_a, ctx_b, wo, wu, wd)
            gproj_b, *q_other = back(nn, proj_b, probs_b, gctx_b, side_b)
            gproj_a, *q_own = back(nn, proj_a, probs_a, gctx_a, side_a)
            input_grad = last(0, 1)(gmid, gproj_a, gproj_b, side_a, side_b, None)
            layer_out = out(0, total // TM)(mid, hidden, wd, None)[0]
            g_down = sums(natural(d_own), natural(d_other), 1).T
            u = natural(u_packs[0], u_packs[2]), natural(u_packs[1], u_packs[3])
            half, side = wu[0].shape[1], d // 2
            g_up = sums(u[0][:, :half], u[1][:, :half], 1)
            beside = [jnp.concatenate(jnp.split(v[:, half : half + side], 2, axis=0), axis=1) for v in u]
            g_out = sums(*beside, 0)
            q = natural(*q_own), natural(*q_other)
            wide = 3 * qkv[0].shape[2]
            g_qkv = sums(*[v[:, :wide].reshape(d, 3, -1) for v in q], 2)
            g_qb = sums(*[v[:, wide].reshape(2, -1) for v in q], 1)
            small_two = [v[:, half + side :].T for v in u]
            g_bu = sums(*[v[4:6].reshape(-1) for v in small_two], 0)
            shared_two = lax.psum(small_two[0][:4], ("dp", "tensor")).astype(F32)
            vectors = (q[0] + q[1])[:, wide + 1 : wide + 3].T
            shared_one = lax.psum(vectors, ("dp", "tensor")).astype(F32)
        return (
            layer_out, input_grad, shared_one[0], shared_one[1], g_qkv, g_qb, g_out, shared_two[2],
            shared_two[0], shared_two[1], g_up, g_bu, g_down, shared_two[3],
        )

    return body


def solution(mesh):
    in_specs = (
        P(("dp", "tensor"), None), P(("dp", "tensor"), None), P("dp"), P("dp", None), P("dp", None), P(), P(),
        P(None, None, "tensor"), P(None, "tensor"), P("tensor", None), P(), P(), P(), P(None, "tensor"),
        P("tensor"), P("tensor", None), P(),
    )
    out_specs = (
        P(("dp", "tensor"), None), P(("dp", "tensor"), None), P(), P(), P(None, None, "tensor"), P(None, "tensor"),
        P("tensor", None), P(), P(), P(), P(None, "tensor"), P("tensor"), P("tensor", None), P(),
    )
    return jax.shard_map(make_body(mesh), mesh=mesh, in_specs=in_specs, out_specs=out_specs, check_vma=False)
```

```python
import jax
import jax.numpy as jnp
from jax import lax
from jax.experimental import pallas as pl
from jax.experimental.pallas import tpu as pltpu
from jax.sharding import PartitionSpec as P

HEAD_DIM = 64
SEQ_LEN = 1024
LEFT = 10
RIGHT = 2
QB = 64
MARGIN = 14
WIN = QB + 16
NBLK = SEQ_LEN // QB
EPS = 1e-05
LN_ROWS = 256
NEG = -1000000000.0
F32 = jnp.float32
BF16 = jnp.bfloat16


def dot_nn(a, b):
    return jnp.dot(a, b, preferred_element_type=F32)


def dot_nt(a, b):
    return lax.dot_general(a, b, (((1,), (1,)), ((), ())), preferred_element_type=F32)


def dot_tn(a, b):
    return lax.dot_general(a, b, (((0,), (0,)), ((), ())), preferred_element_type=F32)


def length_of(scal, seq):
    return scal[4 + scal[2] + seq]


def keep_of(shape, first_pos, seq, scal):
    seqs = (scal.shape[0] - 4) // 5
    ends = [scal[4 + k * seqs + scal[2] + seq] for k in range(1, 5)]
    pos = first_pos + lax.broadcasted_iota(jnp.int32, (shape[0], 1), 0)
    col = lax.broadcasted_iota(jnp.int32, (1, shape[1]), 1)
    rows = jnp.where((pos >= ends[0]) & (pos < ends[1]), 0.0, 1.0)
    cols = jnp.where((col >= ends[2]) & (col < ends[3]), 0.0, 1.0)
    return rows * cols


def normalize(v):
    off = v - jnp.mean(v, axis=-1, keepdims=True)
    r = lax.rsqrt(jnp.mean(off * off, axis=-1, keepdims=True) + EPS)
    return off * r, r


def head_mask(scale, heads):
    row = lax.broadcasted_iota(jnp.int32, (heads * QB, heads * HEAD_DIM), 0)
    col = lax.broadcasted_iota(jnp.int32, (heads * QB, heads * HEAD_DIM), 1)
    return jnp.where(row // QB == col // HEAD_DIM, scale, 0.0).astype(BF16)


def spread(block, mask, heads):
    return jnp.concatenate([block] * heads, axis=0) * mask


def pair_rows(probs, window, heads):
    out = []
    low = lax.broadcasted_iota(jnp.int32, (QB, 2 * HEAD_DIM), 1) < HEAD_DIM
    for p in range(heads // 2):
        both = dot_tn(
            probs[:, p * 2 * QB : (p + 1) * 2 * QB],
            window[:, p * 2 * HEAD_DIM : (p + 1) * 2 * HEAD_DIM],
        )
        out.append(jnp.where(low, both[:QB], both[QB:]))
    return jnp.concatenate(out, axis=1)


def attend(length, proj, kpad, vpad, scores, ctx, probs_out, heads):
    width = heads * HEAD_DIM
    edge = jnp.zeros((WIN - QB, width), BF16)
    for pad, j in ((kpad, 1), (vpad, 2)):
        pad[0 : WIN - QB, :] = edge
        pad[SEQ_LEN:, :] = edge
        pad[MARGIN : MARGIN + SEQ_LEN, :] = proj[:, j * width : (j + 1) * width]
    mask = head_mask(HEAD_DIM**-0.5, heads)
    key = lax.broadcasted_iota(jnp.int32, (WIN, heads * QB), 0)
    query = lax.broadcasted_iota(jnp.int32, (WIN, heads * QB), 1) % QB
    rel = key - MARGIN - query
    band = jnp.where((rel >= -LEFT) & (rel <= RIGHT), 0.0, NEG)
    diagonal = jnp.where(rel == 0, 0.0, NEG)

    for b in range(NBLK):
        q_all = spread(proj[b * QB : (b + 1) * QB, 0:width], mask, heads)
        scores[b * WIN : (b + 1) * WIN, :] = dot_nt(kpad[b * QB : b * QB + WIN, :], q_all)
    for b in range(NBLK):
        at = slice(b * WIN, (b + 1) * WIN)
        pos = key + (b * QB - MARGIN)
        live = (pos < length) if b else (pos >= 0) & (pos < length)
        masked = scores[at, :] + jnp.where(live, band, diagonal)
        weights = jnp.exp(masked - jnp.max(masked, axis=0, keepdims=True))
        probs_out[at, :] = (weights / jnp.sum(weights, axis=0, keepdims=True)).astype(BF16)
    for b in range(NBLK):
        v_win = vpad[b * QB : b * QB + WIN, :]
        ctx[b * QB : (b + 1) * QB, :] = pair_rows(probs_out[b * WIN : (b + 1) * WIN, :], v_win, heads).astype(BF16)


def project(at, n1, w_side, bias, proj):
    width = bias.shape[1]
    value = dot_nn(n1[at, :], w_side[...])
    proj[at, :width] = (value[:, :width] + bias[0:1, :]).astype(BF16)
    proj[at, width : 2 * width] = value[:, width : 2 * width].astype(BF16)
    proj[at, 2 * width :] = (value[:, 2 * width :] + bias[1:2, :]).astype(BF16)


def parts_in_order(scal, mine, theirs):
    odd = jnp.where(scal[3] == 0, 0, 1)
    return ((mine, odd), (theirs, 1 - odd))


def first_kernel(heads, scal, x, w, bias, gain, shift, nn, n1, proj, ctx, probs, w_side, *scratch):
    s = pl.program_id(0)

    @pl.when(s == 0)
    def _():
        width = w.shape[2]
        for j in range(3):
            w_side[:, j * width : (j + 1) * width] = w[j]

    for first in range(0, SEQ_LEN, LN_ROWS):
        at = slice(first, first + LN_ROWS)
        for r in range(first, first + LN_ROWS, SUB):
            sub = slice(r, r + SUB)
            keep = keep_of((SUB, x.shape[1]), r, s, scal)
            value = normalize(x[sub, :].astype(F32) * keep)[0]
            nn[sub, :] = value.astype(BF16)
            n1[sub, :] = (value * gain[...] + shift[...]).astype(BF16)
        project(at, n1, w_side, bias, proj)
    attend(length_of(scal, s), proj, *scratch, ctx, probs, heads)


def second_kernel(heads, scal, n1, mine, theirs, bias, proj, ctx, probs, w_side, *scratch):
    s = pl.program_id(0)

    @pl.when(s == 0)
    def _():
        width = bias.shape[1]
        half = n1.shape[1] // 2
        for part, place_of in parts_in_order(scal, mine, theirs):
            for k in range(3):
                stretch = 3 * place_of + k
                row = pl.multiple_of((stretch % 2) * half, half)
                column = pl.multiple_of((stretch // 2) * width, width)
                w_side[pl.ds(row, half), pl.ds(column, width)] = part[k * half : (k + 1) * half, :]

    for first in range(0, SEQ_LEN, LN_ROWS):
        project(slice(first, first + LN_ROWS), n1, w_side, bias, proj)
    attend(length_of(scal, s), proj, *scratch, ctx, probs, heads)


def const_spec(shape):
    return pl.BlockSpec(shape, lambda *_: (0,) * len(shape), pipeline_mode=pl.Buffered(1))


def rows_spec(rows, cols):
    return pl.BlockSpec((rows, cols), lambda i, *_: (i, 0))


NEEDS = {
    "attend_first": 60, "attend_second": 60, "feed_up": 49, "feed_back": 42, "attend_back": 60,
    "input_gradient": 60, "layer_out": 57, "unpack": 20,
}


def params(name):
    return pltpu.CompilerParams(vmem_limit_bytes=NEEDS[name] * 1024 * 1024, dimension_semantics=("arbitrary",))


def attention_forward(first, scal, rows, w, bias, gain, shift):
    total, width_in = rows.shape
    seqs = total // SEQ_LEN
    width = bias.shape[1]
    heads = width // HEAD_DIM
    outs = [
        jax.ShapeDtypeStruct((total, 3 * width), BF16),
        jax.ShapeDtypeStruct((total, width), BF16),
        jax.ShapeDtypeStruct((seqs * NBLK * WIN, heads * QB), BF16),
        jax.ShapeDtypeStruct((width_in, 3 * width), BF16),
    ]
    out_specs = [
        rows_spec(SEQ_LEN, 3 * width),
        rows_spec(SEQ_LEN, width),
        rows_spec(NBLK * WIN, heads * QB),
        const_spec((width_in, 3 * width)),
    ]
    scratch = [pltpu.VMEM((SEQ_LEN + WIN - QB, width), BF16)] * 2
    scratch += [pltpu.VMEM((NBLK * WIN, heads * QB), F32)]
    flops = 2 * total * width_in * 3 * width + 8 * total * WIN * width
    cost = pl.CostEstimate(flops=flops, bytes_accessed=total * (width_in + 6 * width) * 2, transcendentals=0)
    if first:
        in_specs = [rows_spec(SEQ_LEN, width_in)] + [const_spec(v.shape) for v in (w, bias, gain, shift)]
        outs = [jax.ShapeDtypeStruct(rows.shape, BF16)] * 2 + outs
        out_specs = [rows_spec(SEQ_LEN, width_in)] * 2 + out_specs
        args = (rows, w, bias, gain, shift)
    else:
        half_spec = pl.BlockSpec((3 * width_in // 2, width), lambda *_: (0, 0), pipeline_mode=pl.Buffered(1))
        in_specs = [rows_spec(SEQ_LEN, width_in), half_spec, half_spec, const_spec(bias.shape)]
        args = (rows, *w, bias)

    def body(*refs):
        (first_kernel if first else second_kernel)(heads, *refs)

    return pl.pallas_call(
        body,
        grid_spec=pltpu.PrefetchScalarGridSpec(
            num_scalar_prefetch=1,
            grid=(seqs,),
            in_specs=in_specs,
            out_specs=out_specs,
            scratch_shapes=scratch,
        ),
        out_shape=outs,
        compiler_params=params("attend_first" if first else "attend_second"),
        cost_estimate=cost,
        name="attend_first" if first else "attend_second",
    )(scal, *args)


TM = 512
TU = 1024
TB = 512
FC = 512
FB = 512
SUB = 32
GELU_A = 0.7978845608028654
GELU_K = 0.044715 / 0.7978845608028654**2


def subs(rows):
    return [slice(r, r + SUB) for r in range(0, rows, SUB)]


def fold_rows(v):
    return jnp.sum(v.reshape(-1, 8, v.shape[-1]), axis=0)


def clear(i, *refs):
    @pl.when(i == 0)
    def _():
        for ref in refs:
            ref[...] = jnp.zeros_like(ref)


TAIL = 2
ONES = 16
EXTRA = 128
BLOCKS = 16


def put_blocks(me, packs, acc, columns):
    rows = packs[0].shape[1]
    each = BLOCKS // len(packs)
    for j in range(BLOCKS):
        first = pl.multiple_of((j ^ me) * rows, rows)
        packs[j // each][j % each] = acc[pl.ds(first, rows), columns].astype(BF16)


def put_vectors(acc, first, vectors):
    spare = EXTRA - len(vectors)
    rows = vectors[0].shape[1]
    acc[:rows, first:] = jnp.concatenate(vectors + [jnp.zeros((spare, rows), F32)], axis=0).T


def bias_chunk(biases, first, count):
    width = biases.shape[1]
    rows = range(2 + first // width, 2 + (first + count) // width)
    return jnp.concatenate([biases[r : r + 1, :] for r in rows], axis=1)


def assemble(scal, wo_a, wo_m, wo_t, wu_m, wu_t, wo_s, wu_b):
    width, side, rows = wo_a.shape[0], wo_m.shape[1], wu_m.shape[0]
    wo_s[:width, :] = wo_a[...]
    for part, place_of in parts_in_order(scal, wo_m, wo_t):
        wo_s[width:, pl.ds(pl.multiple_of(place_of * side, side), side)] = part[...]
    for part, place_of in parts_in_order(scal, wu_m, wu_t):
        wu_b[pl.ds(pl.multiple_of(place_of * rows, rows), rows), :] = part[...]


def up_kernel(
    per_seq, scal,
    x, cot, ctx_a, ctx_b, wo_a, wo_m, wo_t, wu_a, wu_m, wu_t, bo, gain, shift, bias_a, bias_b,
    mid_out, n2_out, hidden_out, pre_out, pack_own, pack_other,
    acc_d, wo_s, wu_b, ctx_s, branch, n2_half, pre_even, pre_odd,
):
    i = pl.program_id(0)
    clear(i, acc_d)
    width = ctx_a.shape[1]

    @pl.when(i == 0)
    def _():
        assemble(scal, wo_a, wo_m, wo_t, wu_m, wu_t, wo_s, wu_b)

    rows = x.shape[0]
    ctx_s[:, :width] = ctx_a[...]
    ctx_s[:, width:] = ctx_b[...]
    branch[...] = dot_nn(ctx_s[...], wo_s[...])
    g_t = cot[...].T
    for sub in subs(rows):
        keep = keep_of((SUB, x.shape[1]), (i % per_seq) * rows + sub.start, i // per_seq, scal)
        mid = x[sub, :].astype(F32) * keep + branch[sub, :] + bo[...]
        mid_out[sub, :] = mid
        n2 = (normalize(mid)[0] * gain[...] + shift[...]).astype(BF16)
        n2_out[sub, :] = n2
        n2_half[sub, :] = n2 * 0.5
    half = wu_a.shape[1]
    chunks = [(part, c) for part in range(2) for c in range(half // FC)]
    pres = (pre_even, pre_odd)

    def up(n):
        part, c = chunks[n]
        pres[n % 2][...] = dot_nn(n2_half[...], (wu_a, wu_b)[part][:, c * FC : (c + 1) * FC])

    up(0)
    for n, (part, c) in enumerate(chunks):
        if n + 1 < len(chunks):
            up(n + 1)
        bias = bias_chunk((bias_a, bias_b)[part], c * FC, FC) * 0.5
        ts = slice(part * half + c * FC, part * half + (c + 1) * FC)
        for sub in subs(rows):
            v = pres[n % 2][sub, :] + bias
            z = v * (2 * GELU_A)
            pre_out[sub, ts] = z.astype(BF16)
            t = jnp.tanh(z * (1.0 + GELU_K * (z * z)))
            hidden_out[sub, ts] = (v + v * t).astype(BF16)
        acc_d[:, ts] += dot_nn(g_t, hidden_out[:, ts])

    @pl.when(i == pl.num_programs(0) - 1)
    def _():
        put_blocks(scal[1], [pack_own], acc_d, slice(0, half))
        put_blocks(scal[1], [pack_other], acc_d, slice(half, 2 * half))


def call(kernel, name, grid, scalars, in_specs, outs, out_specs, scratch, flops, nbytes, args, alias=()):
    return pl.pallas_call(
        kernel,
        grid_spec=pltpu.PrefetchScalarGridSpec(
            num_scalar_prefetch=len(scalars), grid=(grid,), in_specs=in_specs, out_specs=out_specs,
            scratch_shapes=scratch,
        ),
        out_shape=[jax.ShapeDtypeStruct(s, t) for s, t in outs],
        compiler_params=params(name),
        input_output_aliases=dict(alias),
        cost_estimate=pl.CostEstimate(flops=flops, bytes_accessed=nbytes, transcendentals=0),
        name=name,
    )(*scalars, *args)


def tail_spec(v, rows):
    return pl.BlockSpec(
        (rows, v.shape[1]), lambda *_: (v.shape[0] // rows - 1, 0), pipeline_mode=pl.Buffered(1)
    )


def up_block(scal, x, cot, ctx_a, ctx_b, wo_a, wu_a, parts, bo, gain, shift, biases):
    total, d = x.shape
    width = ctx_a.shape[1]
    half = wu_a.shape[1]
    args = (x, cot, ctx_a, ctx_b, wo_a, *parts[0], wu_a, *parts[1], bo, gain, shift, *biases)
    in_specs = [rows_spec(TU, d), rows_spec(TU, d), rows_spec(TU, width), rows_spec(TU, width)]
    in_specs += [tail_spec(v, width) if k in (1, 2) else const_spec(v.shape) for k, v in enumerate(args[4:])]
    pack = (BLOCKS, d // BLOCKS, half)
    outs = [
        ((total, d), F32), ((total, d), BF16), ((total, 2 * half), BF16), ((total, 2 * half), BF16),
        (pack, BF16), (pack, BF16),
    ]
    out_specs = [rows_spec(TU, d), rows_spec(TU, d), rows_spec(TU, 2 * half), rows_spec(TU, 2 * half)]
    out_specs += [const_spec(s) for s, _ in outs[4:]]
    scratch = [
        pltpu.VMEM((d, 2 * half), F32), pltpu.VMEM((2 * width, d), BF16), pltpu.VMEM((d, half), BF16),
        pltpu.VMEM((TU, 2 * width), BF16),
        pltpu.VMEM((TU, d), F32), pltpu.VMEM((TU, d), BF16), pltpu.VMEM((TU, FC), F32), pltpu.VMEM((TU, FC), F32),
    ]

    def body(*refs):
        up_kernel(SEQ_LEN // TU, *refs)

    return call(
        body, "feed_up", total // TU, (scal,), in_specs, outs, out_specs, scratch,
        2 * total * d * (4 * half + 2 * width), total * (18 * d + 8 * half), args,
    )


def down_kernel(
    scal,
    cot, mid, n2_in, pre, ctx_a, ctx_b, wo_a, wo_m, wo_t, wu_a, wu_m, wu_t, wd_a, wd_b, gain,
    gmid_out, gctx_a, gctx_b, keep_own, keep_other, send_own, send_other,
    acc_own, acc_other, acc_small, wo_s, wu_b, ctx_s, n2_t, gh_even, gh_odd, gpre, back_a, back_b,
):
    i = pl.program_id(0)
    clear(i, acc_own, acc_other, acc_small)
    width = ctx_a.shape[1]

    @pl.when(i == 0)
    def _():
        assemble(scal, wo_a, wo_m, wo_t, wu_m, wu_t, wo_s, wu_b)


    rows = cot.shape[0]
    ctx_s[:, :width] = ctx_a[...]
    ctx_s[:, width:] = ctx_b[...]
    n2_t[:-ONES, :] = n2_in[...].T
    n2_t[-ONES:, :] = jnp.ones((ONES, rows), BF16)
    half = wu_a.shape[1]
    chunks = [(part, c) for part in range(2) for c in range(half // FB)]
    ghs = (gh_even, gh_odd)

    def up(n):
        part, c = chunks[n]
        ghs[n % 2][...] = dot_nt(cot[...], (wd_a, wd_b)[part][c * FB : (c + 1) * FB, :]).astype(BF16)

    def vector(n):
        part, c = chunks[n]
        ts = slice(part * half + c * FB, part * half + (c + 1) * FB)
        for sub in subs(rows):
            z = pre[sub, ts]
            k = z * z * GELU_K
            t = jnp.tanh(z * (k + 1.0))
            slope = (t + 1.0) * ((z * (k * 1.5 + 0.5)) * (1.0 - t) + 0.5)
            gpre[sub, ts] = slope * ghs[n % 2][sub, :]

    def use(n):
        part, c = chunks[n]
        ts = slice(part * half + c * FB, part * half + (c + 1) * FB)
        (acc_own, acc_other)[part][:, c * FB : (c + 1) * FB] += dot_nn(n2_t[...], gpre[:, ts])

    up(0)
    for n in range(len(chunks)):
        if n + 1 < len(chunks):
            up(n + 1)
        if n:
            use(n - 1)
        vector(n)
    use(len(chunks) - 1)
    sums = [jnp.zeros((8, cot.shape[1]), F32) for _ in range(4)]
    side = cot.shape[1] // 2
    parts = [slice(k * rows // TAIL, (k + 1) * rows // TAIL) for k in range(TAIL)]

    def back(at):
        back_a[at, :] = dot_nt(gpre[at, :half], wu_a[...])
        back_b[at, :] = dot_nt(gpre[at, half:], wu_b[...])

    back(parts[0])
    for k, at in enumerate(parts):
        if k + 1 < TAIL:
            back(parts[k + 1])
        for r in range(at.start, at.stop, SUB):
            sub = slice(r, r + SUB)
            gn2 = back_a[sub, :] + back_b[sub, :]
            nn, r_std = normalize(mid[sub, :])
            gnn = gn2 * nn
            u = gn2 * gain[...]
            mean_un = jnp.mean(gnn * gain[...], axis=-1, keepdims=True)
            g = cot[sub, :].astype(F32)
            gm = g + r_std * (u - jnp.mean(u, axis=-1, keepdims=True) - nn * mean_un)
            gmid_out[sub, :] = gm.astype(BF16)
            for q, term in enumerate((gnn, gn2, gm, g)):
                sums[q] += fold_rows(term)
        gctx = dot_nt(gmid_out[at, :], wo_s[...])
        gctx_a[at, :] = gctx[:, :width].astype(BF16)
        gctx_b[at, :] = gctx[:, width:].astype(BF16)
    both = dot_tn(ctx_s[...], gmid_out[...])
    for acc, part in ((acc_own, both[:width]), (acc_other, both[width:])):
        acc[:width, half : half + side] += part[:, :side]
        acc[width : 2 * width, half : half + side] += part[:, side:]
    for k in range(4):
        acc_small[8 * k : 8 * k + 8, :] += sums[k]

    @pl.when(i == pl.num_programs(0) - 1)
    def _():
        vectors = [jnp.sum(acc_small[8 * k : 8 * k + 8, :], axis=0, keepdims=True) for k in range(4)]
        d = cot.shape[1]
        for acc, keep, send in ((acc_own, keep_own, send_own), (acc_other, keep_other, send_other)):
            mine = acc[d : d + 1, :half]
            put_vectors(acc, half + side, vectors + [mine[:, :d], mine[:, d:]])
            put_blocks(scal[0], [keep, send], acc, slice(None))


def down_block(scal, cot, mid, n2, pre, ctx_a, ctx_b, wo_a, wu_a, parts, wd, gain):
    total, d = cot.shape
    width = ctx_a.shape[1]
    half = wu_a.shape[1]
    args = (cot, mid, n2, pre, ctx_a, ctx_b, wo_a, *parts[0], wu_a, *parts[1], *wd, gain)
    in_specs = [rows_spec(TB, d), rows_spec(TB, d), rows_spec(TB, d), rows_spec(TB, 2 * half)]
    in_specs += [rows_spec(TB, width), rows_spec(TB, width)]
    in_specs += [tail_spec(v, width) if k in (1, 2) else const_spec(v.shape) for k, v in enumerate(args[6:])]
    columns = half + d // 2 + EXTRA
    pack = (BLOCKS // 2, d // BLOCKS, columns)
    outs = [((total, d), BF16), ((total, width), BF16), ((total, width), BF16), *[(pack, BF16)] * 4]
    out_specs = [rows_spec(TB, d), rows_spec(TB, width), rows_spec(TB, width)]
    out_specs += [const_spec(s) for s, _ in outs[3:]]
    scratch = [
        pltpu.VMEM((d + ONES, columns), F32), pltpu.VMEM((d + ONES, columns), F32),
        pltpu.VMEM((32, d), F32), pltpu.VMEM((2 * width, d), BF16), pltpu.VMEM((d, half), BF16),
        pltpu.VMEM((TB, 2 * width), BF16),
        pltpu.VMEM((d + ONES, TB), BF16),
        pltpu.VMEM((TB, FB), BF16), pltpu.VMEM((TB, FB), BF16), pltpu.VMEM((TB, 2 * half), BF16),
        pltpu.VMEM((TB, d), F32), pltpu.VMEM((TB, d), F32),
    ]
    return call(
        down_kernel, "feed_back", total // TB, (scal,), in_specs, outs, out_specs, scratch,
        2 * total * d * (6 * half + 4 * width), total * (16 * d + 4 * half), args,
    )


def out_rows(mid, hidden, wd_a, wd_b, bd, out):
    half = wd_a.shape[0]
    out[...] = (
        mid[...] + dot_nn(hidden[:, :half], wd_a[...]) + dot_nn(hidden[:, half:], wd_b[...]) + bd[...]
    ).astype(BF16)


def out_kernel(scal, mid, hidden, wd_a, wd_b, bd, *refs):
    out_rows(mid, hidden, wd_a, wd_b, bd, refs[-1])


def out_down_kernel(scal, mid, hidden, wd_a, wd_b, bd, before, d0, d1, out, down, d_all):
    out_rows(mid, hidden, wd_a, wd_b, bd, out)

    @pl.when(pl.program_id(0) == 0)
    def _():
        place(scal[1], (d0, d1), d_all, BF16)
        down[...] = d_all[...].T.astype(F32)


def part_spec(first, cols):
    return pl.BlockSpec((TM, cols), lambda i, *_: (i + first, 0))


def out_block(first, tiles, scal, mid, hidden, wd, bd, before, pieces=()):
    total, d = mid.shape
    args = (mid, hidden, *wd, bd)
    specs = [part_spec(first, d), part_spec(first, hidden.shape[1])]
    specs += [const_spec(a.shape) for a in (*wd, bd)]
    alias = {}
    if before is not None:
        alias = {len(args) + 1: 0}
        args += (before,)
        specs += [pl.BlockSpec(memory_space=pl.ANY)]
    outs, out_specs, scratch = [((total, d), BF16)], [part_spec(first, d)], []
    if pieces:
        args += tuple(pieces)
        specs += [const_spec(p.shape) for p in pieces]
        shape = (pieces[0].shape[2], d)
        outs += [(shape, F32)]
        out_specs += [const_spec(shape)]
        scratch = [pltpu.VMEM(shape[::-1], BF16)]
    return call(
        out_down_kernel if pieces else out_kernel, "layer_out", tiles, (scal,), specs, outs, out_specs, scratch,
        2 * tiles * TM * d * hidden.shape[1], tiles * TM * (6 * d + 2 * hidden.shape[1]), args, alias,
    )


def attend_back_kernel(
    heads, scal, nn, proj, probs, gctx, w, gain, shift, gproj, pack_keep, pack_send, kpad, vpad, dk, dv, acc, acc_b, gprob, gscore
):
    s = pl.program_id(0)
    clear(s, acc, acc_b)
    width = heads * HEAD_DIM
    edge = jnp.zeros((WIN - QB, width), BF16)
    for pad, j in ((kpad, 1), (vpad, 2)):
        pad[0 : WIN - QB, :] = edge
        pad[SEQ_LEN:, :] = edge
        pad[MARGIN : MARGIN + SEQ_LEN, :] = proj[:, j * width : (j + 1) * width]
    mask = head_mask(1.0, heads)
    dk[0 : (WIN - QB), :] = jnp.zeros(((WIN - QB), width), F32)
    dv[0 : (WIN - QB), :] = jnp.zeros(((WIN - QB), width), F32)
    scale = HEAD_DIM**-0.5

    def rows(b):
        return slice(b * QB, (b + 1) * QB)

    def keys(b):
        return slice(b * QB, b * QB + WIN)

    def own(b):
        return slice(b * WIN, (b + 1) * WIN)

    for b in range(NBLK):
        gprob[own(b), :] = dot_nt(vpad[keys(b), :], spread(gctx[rows(b), :], mask, heads))
    for b in range(NBLK):
        p = probs[own(b), :].astype(F32)
        gp = gprob[own(b), :]
        gscore[own(b), :] = (p * (gp - jnp.sum(p * gp, axis=0, keepdims=True))).astype(BF16)
    for b in range(NBLK):
        gproj[rows(b), 0:width] = (pair_rows(gscore[own(b), :], kpad[keys(b), :], heads) * scale).astype(BF16)
    for b in range(NBLK):
        key_term = dot_nn(gscore[own(b), :], spread(proj[rows(b), 0:width], mask, heads)) * scale
        value_term = dot_nn(probs[own(b), :], spread(gctx[rows(b), :], mask, heads))
        for total, term in ((dk, key_term), (dv, value_term)):
            total[b * QB : b * QB + (WIN - QB), :] += term[: (WIN - QB)]
            total[b * QB + (WIN - QB) : b * QB + WIN, :] = term[(WIN - QB) :]
    gproj[:, width : 2 * width] = dk[MARGIN : MARGIN + SEQ_LEN, :].astype(BF16)
    gproj[:, 2 * width :] = dv[MARGIN : MARGIN + SEQ_LEN, :].astype(BF16)
    gp_all = gproj[...]
    acc[:, : 3 * width] += dot_tn(nn[...], gp_all)
    acc_b[...] += jnp.sum(gp_all.astype(F32), axis=0, keepdims=True)

    @pl.when(s == pl.num_programs(0) - 1)
    def _():
        d = acc.shape[0]
        column = lambda v: jnp.broadcast_to(v[...], (EXTRA, d)).T[:, 0:1]
        gain_col, shift_col = column(gain), column(shift)
        gain_grad, shift_grad = jnp.zeros((d, EXTRA), F32), jnp.zeros((d, EXTRA), F32)
        for j in range(3):
            for c in range(0, width, EXTRA):
                at = slice(j * width + c, j * width + c + EXTRA)
                weight = w[:, at].astype(F32)
                total, sums = acc[:, at], acc_b[:, at]
                gain_grad += weight * total
                shift_grad += weight * sums
                acc[:, at] = gain_col * total + shift_col * sums
        gain_grad = jnp.sum(gain_grad, axis=1, keepdims=True)
        shift_grad = jnp.sum(shift_grad, axis=1, keepdims=True)
        put_vectors(acc, 3 * width, [jnp.concatenate([acc_b[:, :width], acc_b[:, 2 * width :]], axis=1)])
        lane = lax.broadcasted_iota(jnp.int32, (d, EXTRA), 1)
        extra = jnp.where(lane == 1, gain_grad, acc[:, 3 * width :])
        acc[:, 3 * width :] = jnp.where(lane == 2, shift_grad, extra)
        put_blocks(scal[1], [pack_keep, pack_send], acc, slice(None))


def attention_backward(scal, nn, proj, probs, gctx, w, gain, shift):
    total, d = nn.shape
    seqs = total // SEQ_LEN
    width = gctx.shape[1]
    heads = width // HEAD_DIM

    def body(*refs):
        attend_back_kernel(heads, *refs)

    pad = SEQ_LEN + WIN - QB
    columns = 3 * width + EXTRA
    pack = (BLOCKS // 2, d // BLOCKS, columns)
    return call(
        body, "attend_back", seqs, (scal,),
        [
            rows_spec(SEQ_LEN, d), rows_spec(SEQ_LEN, 3 * width),
            rows_spec(NBLK * WIN, heads * QB), rows_spec(SEQ_LEN, width),
            const_spec(w.shape), const_spec(gain.shape), const_spec(shift.shape),
        ],
        [((total, 3 * width), BF16), (pack, BF16), (pack, BF16)],
        [rows_spec(SEQ_LEN, 3 * width), const_spec(pack), const_spec(pack)],
        [
            pltpu.VMEM((pad, width), BF16), pltpu.VMEM((pad, width), BF16),
            pltpu.VMEM((pad, width), F32), pltpu.VMEM((pad, width), F32),
            pltpu.VMEM((d, columns), F32), pltpu.VMEM((1, 3 * width), F32),
            pltpu.VMEM((NBLK * WIN, heads * QB), F32), pltpu.VMEM((NBLK * WIN, heads * QB), BF16),
        ],
        2 * total * d * 3 * width + 16 * total * WIN * width, total * (d + 9 * width) * 2,
        (nn, proj, probs, gctx, w, gain, shift),
    )


def last_kernel(per_seq, first, scal, x, gmid, gp_a, gp_b, w_a, w_b, gain, *refs):
    gin, back_a, back_b = refs[-3:]
    i = pl.program_id(0)
    rows = x.shape[0]
    tile = i + first
    back_a[...] = dot_nt(gp_a[...], w_a[...])
    back_b[...] = dot_nt(gp_b[...], w_b[...])
    for sub in subs(rows):
        keep = keep_of((SUB, x.shape[1]), (tile % per_seq) * rows + sub.start, tile // per_seq, scal)
        nn, r = normalize(x[sub, :].astype(F32) * keep)
        u = (back_a[sub, :] + back_b[sub, :]) * gain[...]
        mean_un = jnp.mean(u * nn, axis=-1, keepdims=True)
        a = r * (u - jnp.mean(u, axis=-1, keepdims=True) - nn * mean_un)
        gin[sub, :] = (gmid[sub, :].astype(F32) + a) * keep


def last_block(part, parts, scal, x, gmid, gp_a, gp_b, w_a, w_b, gain, before):
    total, d = x.shape
    tiles = total // TM // parts

    def body(*refs):
        last_kernel(SEQ_LEN // TM, part * tiles, *refs)

    width = gp_a.shape[1]
    args = (x, gmid, gp_a, gp_b, w_a, w_b, gain)
    specs = [part_spec(part * tiles, c) for c in (d, d, width, width)]
    specs += [const_spec(a.shape) for a in args[4:]]
    alias = {}
    if before is not None:
        alias = {len(args) + 1: 0}
        args += (before,)
        specs += [pl.BlockSpec(memory_space=pl.ANY)]
    return call(
        body, "input_gradient", tiles, (scal,), specs, [((total, d), F32)], [part_spec(part * tiles, d)],
        [pltpu.VMEM((TM, d), F32)] * 2,
        4 * tiles * TM * d * width, tiles * TM * (10 * d + 4 * width), args, alias,
    )[0]


def place(me, pieces, out, kind, columns=slice(None)):
    each = pieces[0].shape[0]
    rows = pieces[0].shape[1]
    for j in range(BLOCKS):
        at = pl.ds(pl.multiple_of((j ^ me) * rows, rows), rows)
        out[at, :] = pieces[j // each][j % each, :, columns].astype(kind)


def unpack_kernel(scal, u0, u1, q0, q1, side_y, side_d, up, out, *refs):
    vectors, (bias_up, qkv, bias_q, gain, shift, u_side, q_all, q_side) = refs[:4], refs[4:]
    me = scal[0]
    half, side = up.shape[1], out.shape[1] // 2
    rows = out.shape[0]
    place(me, (u0, u1), up, F32, slice(0, half))
    place(me, (u0, u1), u_side, F32, slice(half, u0.shape[2]))
    out[:, :side] = u_side[:rows, :side]
    out[:, side:] = u_side[rows:, :side]
    sums = u_side[:, side:].T
    for k in range(4):
        vectors[k][...] = sums[k : k + 1, :]
    bias_up[...] = jnp.concatenate([sums[4:5, :], sums[5:6, :]], axis=1)
    place(scal[1], (q0, q1), q_all, F32)
    width = qkv.shape[2]
    for j in range(3):
        qkv[j] = q_all[:, j * width : (j + 1) * width]
    sums = q_all[:, 3 * width :].T
    bias_q[...] = jnp.concatenate([sums[0:1, :width], sums[0:1, width:]], axis=0)
    place(scal[1], (side_y, side_d), q_side, F32)
    sums += q_side[...].T
    gain[...] = sums[1:2, :]
    shift[...] = sums[2:3, :]


def unpack(scal, pieces, up, out, qkv):
    d = up[0]
    shapes = [up, out, *[(1, d)] * 4, (1, up[1]), qkv, (2, qkv[2]), (1, d), (1, d)]
    natural = [(d, pieces[0].shape[2] - up[1]), (d, pieces[2].shape[2]), (d, EXTRA)]
    return call(
        unpack_kernel, "unpack", 1, (scal,), [const_spec(p.shape) for p in pieces], [(s, F32) for s in shapes],
        [const_spec(s) for s in shapes], [pltpu.VMEM(s, F32) for s in natural], 0,
        6 * sum(p.size for p in pieces), tuple(pieces),
    )


def make_body(mesh):
    tp = mesh.shape["tensor"]
    dp = mesh.shape["dp"]
    paired = tp == 2 and dp == BLOCKS

    def across(v):
        return lax.ppermute(v, "tensor", [(0, 1), (1, 0)])

    def swap(v, distance):
        return lax.ppermute(v, "dp", [(i, i ^ distance) for i in range(dp)])

    def core(v):
        return swap(v, 1)

    def diagonal(v):
        pairs = [(2 * i + j, 2 * (i ^ 1) + 1 - j) for i in range(dp) for j in range(2)]
        return lax.ppermute(v, ("dp", "tensor"), pairs)

    def plus(first, *rest):
        total = first.astype(F32)
        for v in rest:
            total = total + v.astype(F32)
        return total.astype(first.dtype)

    def lower(v):
        return v[: v.shape[0] // 2]

    def upper(v):
        return v[v.shape[0] // 2 :]

    def join(a, b):
        return jnp.concatenate([a, b], axis=0)

    def window(kernel, args, moves):
        args, sent = lax.optimization_barrier((args, [v for v, _ in moves]))
        arrived = [move(v) for v, (_, move) in zip(sent, moves)]
        return lax.optimization_barrier((kernel(*args), arrived, sent))

    def body(
        inputs, cotangent, lengths, time_span, freq_span, gain_one, shift_one, qkv_weight, qkv_bias,
        out_weight, out_bias, gain_two, shift_two, up_weight, up_bias, down_weight, down_bias,
    ):
        total, d = inputs.shape
        seqs = total // SEQ_LEN
        here = lax.axis_index("tensor") * seqs
        index = lax.axis_index("dp")
        label = label_q = jnp.int32(0)
        if paired:
            label = ((index & 1) << 3) | ((index & 2) << 1) | ((index & 4) >> 1)
            label_q = ((index & 1) << 3) | (index & 4)
        place_here = jnp.stack([label, label_q, here, index & 1 if paired else jnp.int32(0)]).astype(jnp.int32)
        ends = [span[:, k] for span in (time_span, freq_span) for k in range(2)]
        scal = jnp.concatenate([place_here, lengths, *ends])
        row = lambda v: v.reshape(1, -1)
        stack_biases = lambda b, u: jnp.concatenate([b, u.reshape(-1, b.shape[1])], axis=0)

        def attend_a(rows, w, bias):
            return attention_forward(True, scal, rows, w, bias, row(gain_one), row(shift_one))

        def attend_b(rows, w, bias):
            return attention_forward(False, scal, rows, w, bias, None, None)

        def up(ctx_a, ctx_b, wo_a, wu_a, parts, biases):
            return up_block(
                scal, inputs, cotangent, ctx_a, ctx_b, wo_a, wu_a, parts, row(out_bias), row(gain_two),
                row(shift_two), biases,
            )

        def down(mid, n2, pre, ctx_a, ctx_b, wo_a, wu_a, parts, wd):
            return down_block(scal, cotangent, mid, n2, pre, ctx_a, ctx_b, wo_a, wu_a, parts, wd, row(gain_two))

        def back(nn, proj, probs, gctx, w):
            return attention_backward(scal, nn, proj, probs, gctx, w, row(gain_one), row(shift_one))

        def last(part, parts):
            return lambda gmid, gp_a, gp_b, w_a, w_b, before: last_block(
                part, parts, scal, inputs, gmid, gp_a, gp_b, w_a, w_b, row(gain_one), before
            )

        def out(first, tiles):
            return lambda mid, hidden, wd, before, *pieces: out_block(
                first, tiles, scal, mid, hidden, wd, row(down_bias), before, pieces
            )

        turned = lambda w: jnp.transpose(w, (1, 0, 2))
        if paired:
            odd = index & 1

            def part_of(v):
                rows = v.shape[0] // 2
                return lax.dynamic_slice_in_dim(v, odd * rows, rows, 0)

            biases = stack_biases(qkv_bias, up_bias)
            qkv_a = turned(qkv_weight)
            side = d // 2
            low, high = qkv_a.reshape(2, -1, side)
            first_rows = jnp.where(
                odd == 0,
                jnp.concatenate([low, out_weight[:, :side]], axis=0),
                jnp.concatenate([high, out_weight[:, side:]], axis=0),
            )
            (nn, n1, proj_a, ctx_a, probs_a, side_a), (first_half, biases_b), _ = window(
                attend_a, (inputs, qkv_a, biases), [(first_rows, across), (biases, across)]
            )
            first_pair = (first_half, core(first_half))
            (proj_b, ctx_b, probs_b, side_b), (up_half,), _ = window(
                attend_b, (n1, first_pair, biases_b), [(part_of(up_weight), across)]
            )
            pairs = (first_pair, (up_half, core(up_half)))
            (mid, n2, hidden, pre, d_own, d_other), (down_b,), _ = window(
                up, (ctx_a, ctx_b, out_weight, up_weight, pairs, (biases, biases_b)), [(down_weight, across)]
            )
            wd = (down_weight, down_b)
            (gmid, gctx_a, gctx_b, u_own, u_other, u_send_own, u_send_other), (d_cross,), _ = window(
                down, (mid, n2, pre, ctx_a, ctx_b, out_weight, up_weight, pairs, wd), [(d_other, across)]
            )
            step = lambda distance: lambda v: swap(v, distance)
            u_other, u_own = plus(u_other, core(u_send_other)), plus(u_own, core(u_send_own))
            d_sum = plus(d_own, d_cross)
            d_sum = plus(lower(d_sum), core(upper(d_sum)))
            (gproj_b, q_other, q_send), (u_cross, d_in), _ = window(
                back, (nn, proj_b, probs_b, gctx_b, side_b), [(u_other, across), (upper(d_sum), step(4))]
            )
            u_sum = plus(u_own, u_cross)
            d_sum = plus(lower(d_sum), d_in)
            q_other = plus(q_other, core(q_send))
            (gproj_a, q_own, q_send), (u_in, d_in, q_cross), _ = window(
                back, (nn, proj_a, probs_a, gctx_a, side_a),
                [(upper(u_sum), step(2)), (d_sum, step(8)), (q_other, across)],
            )
            u_sum = plus(lower(u_sum), u_in)
            d_sum = plus(d_sum, d_in)
            q_terms = (q_own, core(q_send), q_cross)
            input_grad, (u_in, d_in, q_in), _ = window(
                last(0, 2), (gmid, gproj_a, gproj_b, side_a, side_b, None),
                [(upper(u_sum), step(4)), (d_sum, step(2)), (plus(*map(upper, q_terms)), step(4))],
            )
            u_sum = plus(lower(u_sum), u_in)
            d_sum = plus(d_sum, d_in)
            q_sum = plus(*map(lower, q_terms), q_in)
            input_grad, (u_in, d_in, q_in), _ = window(
                last(1, 2), (gmid, gproj_a, gproj_b, side_a, side_b, input_grad),
                [(u_sum, step(8)), (d_sum, step(4)), (q_sum, step(2))],
            )
            u_sum = plus(u_sum, u_in)
            d_sum = join(d_sum, d_in)
            q_sum = plus(q_sum, q_in)
            tiles = total // TM
            cuts = (0, tiles * 5 // 8, tiles * 7 // 8, tiles)
            (layer_out,), (u_in, d_in, q_in), _ = window(
                out(cuts[0], cuts[1] - cuts[0]), (mid, hidden, wd, None),
                [(u_sum, step(4)), (d_sum, core), (q_sum, step(8))],
            )
            u_sum = join(u_sum, u_in)
            q_sum = plus(q_sum, q_in)
            (layer_out, g_down), (u_in, q_in), _ = window(
                out(cuts[1], cuts[2] - cuts[1]), (mid, hidden, wd, layer_out, d_sum, d_in),
                [(u_sum, step(2)), (q_sum, step(4))],
            )
            u_sum = join(u_sum, u_in)
            q_sum = join(q_sum, q_in)
            sides = q_sum[:, :, q_sum.shape[2] - EXTRA :]
            (layer_out,), (u_in, q_in, side_y, side_d), _ = window(
                out(cuts[2], cuts[3] - cuts[2]), (mid, hidden, wd, layer_out),
                [(u_sum, core), (q_sum, core), (sides, across), (sides, diagonal)],
            )
            g_up, g_out, *shared_two, g_bu, g_qkv, g_qb, gain_grad, shift_grad = unpack(
                scal, (u_sum, u_in, q_sum, q_in, side_y, side_d), up_weight.shape, out_weight.shape, qkv_a.shape
            )
            g_qkv = turned(g_qkv)
            g_bu = g_bu.reshape(-1)
            shared_two = [v.reshape(-1) for v in shared_two]
            shared_one = [v.reshape(-1) for v in (gain_grad, shift_grad)]
        else:
            def halves(local, axis):
                return tuple(jnp.split(lax.all_gather(local, "tensor", axis=axis, tiled=True), 2, axis=axis))

            def sums(own, other, axis):
                whole = jnp.concatenate([own, other], axis=axis)
                part = lax.psum_scatter(whole, "tensor", scatter_dimension=axis, tiled=True)
                return lax.psum(part, "dp").astype(F32)

            natural = lambda *packs: jnp.concatenate(packs, axis=0).reshape(d, -1)
            qkv = [turned(w) for w in halves(qkv_weight, 2)]
            biases = [stack_biases(q, u) for q, u in zip(halves(qkv_bias, 1), halves(up_bias, 0))]
            wo, wu, wd = halves(out_weight, 0), halves(up_weight, 1), halves(down_weight, 0)
            nn, n1, proj_a, ctx_a, probs_a, side_a = attend_a(inputs, qkv[0], biases[0])
            halves_b = jnp.split(qkv[1].reshape(-1, qkv[1].shape[2]), 2, axis=0)
            proj_b, ctx_b, probs_b, side_b = attend_b(n1, halves_b, biases[1])
            parts = (jnp.split(wo[1], 2, axis=1), jnp.split(wu[1], 2, axis=0))
            mid, n2, hidden, pre, d_own, d_other = up(ctx_a, ctx_b, wo[0], wu[0], parts, biases)
            gmid, gctx_a, gctx_b, *u_packs = down(mid, n2, pre, ctx_a, ctx_b, wo[0], wu[0], parts, wd)
            gproj_b, *q_other = back(nn, proj_b, probs_b, gctx_b, side_b)
            gproj_a, *q_own = back(nn, proj_a, probs_a, gctx_a, side_a)
            input_grad = last(0, 1)(gmid, gproj_a, gproj_b, side_a, side_b, None)
            layer_out = out(0, total // TM)(mid, hidden, wd, None)[0]
            g_down = sums(natural(d_own), natural(d_other), 1).T
            u = natural(u_packs[0], u_packs[2]), natural(u_packs[1], u_packs[3])
            half, side = wu[0].shape[1], d // 2
            g_up = sums(u[0][:, :half], u[1][:, :half], 1)
            beside = [jnp.concatenate(jnp.split(v[:, half : half + side], 2, axis=0), axis=1) for v in u]
            g_out = sums(*beside, 0)
            q = natural(*q_own), natural(*q_other)
            wide = 3 * qkv[0].shape[2]
            g_qkv = sums(*[v[:, :wide].reshape(d, 3, -1) for v in q], 2)
            g_qb = sums(*[v[:, wide].reshape(2, -1) for v in q], 1)
            small_two = [v[:, half + side :].T for v in u]
            g_bu = sums(*[v[4:6].reshape(-1) for v in small_two], 0)
            shared_two = lax.psum(small_two[0][:4], ("dp", "tensor")).astype(F32)
            vectors = (q[0] + q[1])[:, wide + 1 : wide + 3].T
            shared_one = lax.psum(vectors, ("dp", "tensor")).astype(F32)
        return (
            layer_out, input_grad, shared_one[0], shared_one[1], g_qkv, g_qb, g_out, shared_two[2],
            shared_two[0], shared_two[1], g_up, g_bu, g_down, shared_two[3],
        )

    return body


def solution(mesh):
    in_specs = (
        P(("dp", "tensor"), None), P(("dp", "tensor"), None), P("dp"), P("dp", None), P("dp", None), P(), P(),
        P(None, None, "tensor"), P(None, "tensor"), P("tensor", None), P(), P(), P(), P(None, "tensor"),
        P("tensor"), P("tensor", None), P(),
    )
    out_specs = (
        P(("dp", "tensor"), None), P(("dp", "tensor"), None), P(), P(), P(None, None, "tensor"), P(None, "tensor"),
        P("tensor", None), P(), P(), P(), P(None, "tensor"), P("tensor"), P("tensor", None), P(),
    )
    return jax.shard_map(make_body(mesh), mesh=mesh, in_specs=in_specs, out_specs=out_specs, check_vma=False)
```

```python
import jax
import jax.numpy as jnp
from jax import lax
from jax.experimental import pallas as pl
from jax.experimental.pallas import tpu as pltpu
from jax.sharding import PartitionSpec as P

HEAD_DIM = 64
SEQ_LEN = 1024
LEFT = 10
RIGHT = 2
QB = 64
MARGIN = 14
WIN = QB + 16
NBLK = SEQ_LEN // QB
EPS = 1e-05
LN_ROWS = 256
NEG = -1000000000.0
F32 = jnp.float32
BF16 = jnp.bfloat16


def dot_nn(a, b):
    return jnp.dot(a, b, preferred_element_type=F32)


def dot_nt(a, b):
    return lax.dot_general(a, b, (((1,), (1,)), ((), ())), preferred_element_type=F32)


def dot_tn(a, b):
    return lax.dot_general(a, b, (((0,), (0,)), ((), ())), preferred_element_type=F32)


def length_of(scal, seq):
    return scal[4 + scal[2] + seq]


def keep_of(shape, first_pos, seq, scal):
    seqs = (scal.shape[0] - 4) // 5
    ends = [scal[4 + k * seqs + scal[2] + seq] for k in range(1, 5)]
    pos = first_pos + lax.broadcasted_iota(jnp.int32, (shape[0], 1), 0)
    col = lax.broadcasted_iota(jnp.int32, (1, shape[1]), 1)
    rows = jnp.where((pos >= ends[0]) & (pos < ends[1]), 0.0, 1.0)
    cols = jnp.where((col >= ends[2]) & (col < ends[3]), 0.0, 1.0)
    return rows * cols


def normalize(v):
    off = v - jnp.mean(v, axis=-1, keepdims=True)
    r = lax.rsqrt(jnp.mean(off * off, axis=-1, keepdims=True) + EPS)
    return off * r, r


def head_mask(scale, heads):
    row = lax.broadcasted_iota(jnp.int32, (heads * QB, heads * HEAD_DIM), 0)
    col = lax.broadcasted_iota(jnp.int32, (heads * QB, heads * HEAD_DIM), 1)
    return jnp.where(row // QB == col // HEAD_DIM, scale, 0.0).astype(BF16)


def spread(block, mask, heads):
    return jnp.concatenate([block] * heads, axis=0) * mask


def pair_rows(probs, window, heads):
    out = []
    low = lax.broadcasted_iota(jnp.int32, (QB, 2 * HEAD_DIM), 1) < HEAD_DIM
    for p in range(heads // 2):
        both = dot_tn(
            probs[:, p * 2 * QB : (p + 1) * 2 * QB],
            window[:, p * 2 * HEAD_DIM : (p + 1) * 2 * HEAD_DIM],
        )
        out.append(jnp.where(low, both[:QB], both[QB:]))
    return jnp.concatenate(out, axis=1)


def attend(length, proj, kpad, vpad, scores, ctx, probs_out, heads):
    width = heads * HEAD_DIM
    edge = jnp.zeros((WIN - QB, width), BF16)
    for pad, j in ((kpad, 1), (vpad, 2)):
        pad[0 : WIN - QB, :] = edge
        pad[SEQ_LEN:, :] = edge
        pad[MARGIN : MARGIN + SEQ_LEN, :] = proj[:, j * width : (j + 1) * width]
    mask = head_mask(HEAD_DIM**-0.5, heads)
    key = lax.broadcasted_iota(jnp.int32, (WIN, heads * QB), 0)
    query = lax.broadcasted_iota(jnp.int32, (WIN, heads * QB), 1) % QB
    rel = key - MARGIN - query
    band = jnp.where((rel >= -LEFT) & (rel <= RIGHT), 0.0, NEG)
    diagonal = jnp.where(rel == 0, 0.0, NEG)

    for b in range(NBLK):
        q_all = spread(proj[b * QB : (b + 1) * QB, 0:width], mask, heads)
        scores[b * WIN : (b + 1) * WIN, :] = dot_nt(kpad[b * QB : b * QB + WIN, :], q_all)
    for b in range(NBLK):
        at = slice(b * WIN, (b + 1) * WIN)
        pos = key + (b * QB - MARGIN)
        live = (pos < length) if b else (pos >= 0) & (pos < length)
        masked = scores[at, :] + jnp.where(live, band, diagonal)
        weights = jnp.exp(masked - jnp.max(masked, axis=0, keepdims=True))
        probs_out[at, :] = (weights / jnp.sum(weights, axis=0, keepdims=True)).astype(BF16)
    for b in range(NBLK):
        v_win = vpad[b * QB : b * QB + WIN, :]
        ctx[b * QB : (b + 1) * QB, :] = pair_rows(probs_out[b * WIN : (b + 1) * WIN, :], v_win, heads).astype(BF16)


def project(at, n1, w_side, bias, proj):
    width = bias.shape[1]
    value = dot_nn(n1[at, :], w_side[...])
    proj[at, :width] = (value[:, :width] + bias[0:1, :]).astype(BF16)
    proj[at, width : 2 * width] = value[:, width : 2 * width].astype(BF16)
    proj[at, 2 * width :] = (value[:, 2 * width :] + bias[1:2, :]).astype(BF16)


def parts_in_order(scal, mine, theirs):
    odd = jnp.where(scal[3] == 0, 0, 1)
    return ((mine, odd), (theirs, 1 - odd))


def first_kernel(heads, scal, x, w, bias, gain, shift, nn, n1, proj, ctx, probs, w_side, *scratch):
    s = pl.program_id(0)

    @pl.when(s == 0)
    def _():
        width = w.shape[2]
        for j in range(3):
            w_side[:, j * width : (j + 1) * width] = w[j]

    for first in range(0, SEQ_LEN, LN_ROWS):
        at = slice(first, first + LN_ROWS)
        for r in range(first, first + LN_ROWS, SUB):
            sub = slice(r, r + SUB)
            keep = keep_of((SUB, x.shape[1]), r, s, scal)
            value = normalize(x[sub, :].astype(F32) * keep)[0]
            nn[sub, :] = value.astype(BF16)
            n1[sub, :] = (value * gain[...] + shift[...]).astype(BF16)
        project(at, n1, w_side, bias, proj)
    attend(length_of(scal, s), proj, *scratch, ctx, probs, heads)


def second_kernel(heads, scal, n1, mine, theirs, bias, proj, ctx, probs, w_side, *scratch):
    s = pl.program_id(0)

    @pl.when(s == 0)
    def _():
        width = bias.shape[1]
        half = n1.shape[1] // 2
        for part, place_of in parts_in_order(scal, mine, theirs):
            for k in range(3):
                stretch = 3 * place_of + k
                row = pl.multiple_of((stretch % 2) * half, half)
                column = pl.multiple_of((stretch // 2) * width, width)
                w_side[pl.ds(row, half), pl.ds(column, width)] = part[k * half : (k + 1) * half, :]

    for first in range(0, SEQ_LEN, LN_ROWS):
        project(slice(first, first + LN_ROWS), n1, w_side, bias, proj)
    attend(length_of(scal, s), proj, *scratch, ctx, probs, heads)


def const_spec(shape):
    return pl.BlockSpec(shape, lambda *_: (0,) * len(shape), pipeline_mode=pl.Buffered(1))


def rows_spec(rows, cols):
    return pl.BlockSpec((rows, cols), lambda i, *_: (i, 0))


NEEDS = {
    "attend_first": 60, "attend_second": 60, "feed_up": 49, "feed_back": 42, "attend_back": 60,
    "input_gradient": 60, "layer_out": 57, "unpack": 20,
}


def params(name):
    return pltpu.CompilerParams(vmem_limit_bytes=NEEDS[name] * 1024 * 1024, dimension_semantics=("arbitrary",))


def attention_forward(first, scal, rows, w, bias, gain, shift):
    total, width_in = rows.shape
    seqs = total // SEQ_LEN
    width = bias.shape[1]
    heads = width // HEAD_DIM
    outs = [
        jax.ShapeDtypeStruct((total, 3 * width), BF16),
        jax.ShapeDtypeStruct((total, width), BF16),
        jax.ShapeDtypeStruct((seqs * NBLK * WIN, heads * QB), BF16),
        jax.ShapeDtypeStruct((width_in, 3 * width), BF16),
    ]
    out_specs = [
        rows_spec(SEQ_LEN, 3 * width),
        rows_spec(SEQ_LEN, width),
        rows_spec(NBLK * WIN, heads * QB),
        const_spec((width_in, 3 * width)),
    ]
    scratch = [pltpu.VMEM((SEQ_LEN + WIN - QB, width), BF16)] * 2
    scratch += [pltpu.VMEM((NBLK * WIN, heads * QB), F32)]
    flops = 2 * total * width_in * 3 * width + 8 * total * WIN * width
    cost = pl.CostEstimate(flops=flops, bytes_accessed=total * (width_in + 6 * width) * 2, transcendentals=0)
    if first:
        in_specs = [rows_spec(SEQ_LEN, width_in)] + [const_spec(v.shape) for v in (w, bias, gain, shift)]
        outs = [jax.ShapeDtypeStruct(rows.shape, BF16)] * 2 + outs
        out_specs = [rows_spec(SEQ_LEN, width_in)] * 2 + out_specs
        args = (rows, w, bias, gain, shift)
    else:
        half_spec = pl.BlockSpec((3 * width_in // 2, width), lambda *_: (0, 0), pipeline_mode=pl.Buffered(1))
        in_specs = [rows_spec(SEQ_LEN, width_in), half_spec, half_spec, const_spec(bias.shape)]
        args = (rows, *w, bias)

    def body(*refs):
        (first_kernel if first else second_kernel)(heads, *refs)

    return pl.pallas_call(
        body,
        grid_spec=pltpu.PrefetchScalarGridSpec(
            num_scalar_prefetch=1,
            grid=(seqs,),
            in_specs=in_specs,
            out_specs=out_specs,
            scratch_shapes=scratch,
        ),
        out_shape=outs,
        compiler_params=params("attend_first" if first else "attend_second"),
        cost_estimate=cost,
        name="attend_first" if first else "attend_second",
    )(scal, *args)


TM = 512
TU = 1024
TB = 512
FC = 512
FB = 512
SUB = 32
GELU_A = 0.7978845608028654
GELU_K = 0.044715 / 0.7978845608028654**2


def subs(rows):
    return [slice(r, r + SUB) for r in range(0, rows, SUB)]


def fold_rows(v):
    return jnp.sum(v.reshape(-1, 8, v.shape[-1]), axis=0)


def clear(i, *refs):
    @pl.when(i == 0)
    def _():
        for ref in refs:
            ref[...] = jnp.zeros_like(ref)


TAIL = 2
ONES = 16
EXTRA = 128
BLOCKS = 16


def put_blocks(me, packs, acc, columns):
    rows = packs[0].shape[1]
    each = BLOCKS // len(packs)
    for j in range(BLOCKS):
        first = pl.multiple_of((j ^ me) * rows, rows)
        packs[j // each][j % each] = acc[pl.ds(first, rows), columns].astype(BF16)


def put_vectors(acc, first, vectors):
    spare = EXTRA - len(vectors)
    rows = vectors[0].shape[1]
    acc[:rows, first:] = jnp.concatenate(vectors + [jnp.zeros((spare, rows), F32)], axis=0).T


def assemble(scal, wo_a, wo_m, wo_t, wu_m, wu_t, wo_s, wu_b):
    width, side, rows = wo_a.shape[0], wo_m.shape[1], wu_m.shape[0]
    wo_s[:width, :] = wo_a[...]
    for part, place_of in parts_in_order(scal, wo_m, wo_t):
        wo_s[width:, pl.ds(pl.multiple_of(place_of * side, side), side)] = part[...]
    for part, place_of in parts_in_order(scal, wu_m, wu_t):
        wu_b[pl.ds(pl.multiple_of(place_of * rows, rows), rows), :] = part[...]


def up_kernel(
    per_seq, scal,
    x, cot, ctx_a, ctx_b, wo_a, wo_m, wo_t, wu_a, wu_m, wu_t, bo, gain, shift, bias_a, bias_b,
    mid_out, n2_out, hidden_out, pre_out, pack_own, pack_other,
    acc_d, wo_s, wu_b, ctx_s, branch, n2_half, pre_even, pre_odd,
):
    i = pl.program_id(0)
    clear(i, acc_d)
    width = ctx_a.shape[1]

    @pl.when(i == 0)
    def _():
        assemble(scal, wo_a, wo_m, wo_t, wu_m, wu_t, wo_s, wu_b)

    rows = x.shape[0]
    ctx_s[:, :width] = ctx_a[...]
    ctx_s[:, width:] = ctx_b[...]
    branch[...] = dot_nn(ctx_s[...], wo_s[...])
    g_t = cot[...].T
    for sub in subs(rows):
        keep = keep_of((SUB, x.shape[1]), (i % per_seq) * rows + sub.start, i // per_seq, scal)
        mid = x[sub, :].astype(F32) * keep + branch[sub, :] + bo[...]
        mid_out[sub, :] = mid
        n2 = (normalize(mid)[0] * gain[...] + shift[...]).astype(BF16)
        n2_out[sub, :] = n2
        n2_half[sub, :] = n2 * 0.5
    half = wu_a.shape[1]
    chunks = [(part, c) for part in range(2) for c in range(half // FC)]
    pres = (pre_even, pre_odd)

    def up(n):
        part, c = chunks[n]
        pres[n % 2][...] = dot_nn(n2_half[...], (wu_a, wu_b)[part][:, c * FC : (c + 1) * FC])

    up(0)
    for n, (part, c) in enumerate(chunks):
        if n + 1 < len(chunks):
            up(n + 1)
        bias = (bias_a, bias_b)[part][:, c * FC : (c + 1) * FC] * 0.5
        ts = slice(part * half + c * FC, part * half + (c + 1) * FC)
        for sub in subs(rows):
            v = pres[n % 2][sub, :] + bias
            z = v * (2 * GELU_A)
            pre_out[sub, ts] = z.astype(BF16)
            t = jnp.tanh(z * (1.0 + GELU_K * (z * z)))
            hidden_out[sub, ts] = (v + v * t).astype(BF16)
        acc_d[:, ts] += dot_nn(g_t, hidden_out[:, ts])

    @pl.when(i == pl.num_programs(0) - 1)
    def _():
        put_blocks(scal[1], [pack_own], acc_d, slice(0, half))
        put_blocks(scal[1], [pack_other], acc_d, slice(half, 2 * half))


def call(kernel, name, grid, scalars, in_specs, outs, out_specs, scratch, flops, nbytes, args, alias=()):
    return pl.pallas_call(
        kernel,
        grid_spec=pltpu.PrefetchScalarGridSpec(
            num_scalar_prefetch=len(scalars), grid=(grid,), in_specs=in_specs, out_specs=out_specs,
            scratch_shapes=scratch,
        ),
        out_shape=[jax.ShapeDtypeStruct(s, t) for s, t in outs],
        compiler_params=params(name),
        input_output_aliases=dict(alias),
        cost_estimate=pl.CostEstimate(flops=flops, bytes_accessed=nbytes, transcendentals=0),
        name=name,
    )(*scalars, *args)


def tail_spec(v, rows):
    return pl.BlockSpec(
        (rows, v.shape[1]), lambda *_: (v.shape[0] // rows - 1, 0), pipeline_mode=pl.Buffered(1)
    )


def up_block(scal, x, cot, ctx_a, ctx_b, wo_a, wu_a, parts, bo, gain, shift, biases):
    total, d = x.shape
    width = ctx_a.shape[1]
    half = wu_a.shape[1]
    args = (x, cot, ctx_a, ctx_b, wo_a, *parts[0], wu_a, *parts[1], bo, gain, shift, *biases)
    in_specs = [rows_spec(TU, d), rows_spec(TU, d), rows_spec(TU, width), rows_spec(TU, width)]
    in_specs += [tail_spec(v, width) if k in (1, 2) else const_spec(v.shape) for k, v in enumerate(args[4:])]
    pack = (BLOCKS, d // BLOCKS, half)
    outs = [
        ((total, d), F32), ((total, d), BF16), ((total, 2 * half), BF16), ((total, 2 * half), BF16),
        (pack, BF16), (pack, BF16),
    ]
    out_specs = [rows_spec(TU, d), rows_spec(TU, d), rows_spec(TU, 2 * half), rows_spec(TU, 2 * half)]
    out_specs += [const_spec(s) for s, _ in outs[4:]]
    scratch = [
        pltpu.VMEM((d, 2 * half), F32), pltpu.VMEM((2 * width, d), BF16), pltpu.VMEM((d, half), BF16),
        pltpu.VMEM((TU, 2 * width), BF16),
        pltpu.VMEM((TU, d), F32), pltpu.VMEM((TU, d), BF16), pltpu.VMEM((TU, FC), F32), pltpu.VMEM((TU, FC), F32),
    ]

    def body(*refs):
        up_kernel(SEQ_LEN // TU, *refs)

    return call(
        body, "feed_up", total // TU, (scal,), in_specs, outs, out_specs, scratch,
        2 * total * d * (4 * half + 2 * width), total * (18 * d + 8 * half), args,
    )


def down_kernel(
    scal,
    cot, mid, n2_in, pre, ctx_a, ctx_b, wo_a, wo_m, wo_t, wu_a, wu_m, wu_t, wd_a, wd_b, gain,
    gmid_out, gctx_a, gctx_b, keep_own, keep_other, send_own, send_other,
    acc_own, acc_other, acc_small, wo_s, wu_b, ctx_s, n2_t, gh_even, gh_odd, gpre, back_a, back_b,
):
    i = pl.program_id(0)
    clear(i, acc_own, acc_other, acc_small)
    width = ctx_a.shape[1]

    @pl.when(i == 0)
    def _():
        assemble(scal, wo_a, wo_m, wo_t, wu_m, wu_t, wo_s, wu_b)


    rows = cot.shape[0]
    ctx_s[:, :width] = ctx_a[...]
    ctx_s[:, width:] = ctx_b[...]
    n2_t[:-ONES, :] = n2_in[...].T
    n2_t[-ONES:, :] = jnp.ones((ONES, rows), BF16)
    half = wu_a.shape[1]
    chunks = [(part, c) for part in range(2) for c in range(half // FB)]
    ghs = (gh_even, gh_odd)

    def up(n):
        part, c = chunks[n]
        ghs[n % 2][...] = dot_nt(cot[...], (wd_a, wd_b)[part][c * FB : (c + 1) * FB, :]).astype(BF16)

    def vector(n):
        part, c = chunks[n]
        ts = slice(part * half + c * FB, part * half + (c + 1) * FB)
        for sub in subs(rows):
            z = pre[sub, ts]
            k = z * z * GELU_K
            t = jnp.tanh(z * (k + 1.0))
            slope = (t + 1.0) * ((z * (k * 1.5 + 0.5)) * (1.0 - t) + 0.5)
            gpre[sub, ts] = slope * ghs[n % 2][sub, :]

    def use(n):
        part, c = chunks[n]
        ts = slice(part * half + c * FB, part * half + (c + 1) * FB)
        (acc_own, acc_other)[part][:, c * FB : (c + 1) * FB] += dot_nn(n2_t[...], gpre[:, ts])

    up(0)
    for n in range(len(chunks)):
        if n + 1 < len(chunks):
            up(n + 1)
        if n:
            use(n - 1)
        vector(n)
    use(len(chunks) - 1)
    sums = [jnp.zeros((8, cot.shape[1]), F32) for _ in range(4)]
    side = cot.shape[1] // 2
    parts = [slice(k * rows // TAIL, (k + 1) * rows // TAIL) for k in range(TAIL)]

    def back(at):
        back_a[at, :] = dot_nt(gpre[at, :half], wu_a[...])
        back_b[at, :] = dot_nt(gpre[at, half:], wu_b[...])

    back(parts[0])
    for k, at in enumerate(parts):
        if k + 1 < TAIL:
            back(parts[k + 1])
        for r in range(at.start, at.stop, SUB):
            sub = slice(r, r + SUB)
            gn2 = back_a[sub, :] + back_b[sub, :]
            nn, r_std = normalize(mid[sub, :])
            gnn = gn2 * nn
            u = gn2 * gain[...]
            mean_un = jnp.mean(gnn * gain[...], axis=-1, keepdims=True)
            g = cot[sub, :].astype(F32)
            gm = g + r_std * (u - jnp.mean(u, axis=-1, keepdims=True) - nn * mean_un)
            gmid_out[sub, :] = gm.astype(BF16)
            for q, term in enumerate((gnn, gn2, gm, g)):
                sums[q] += fold_rows(term)
        gctx = dot_nt(gmid_out[at, :], wo_s[...])
        gctx_a[at, :] = gctx[:, :width].astype(BF16)
        gctx_b[at, :] = gctx[:, width:].astype(BF16)
    both = dot_tn(ctx_s[...], gmid_out[...])
    for acc, part in ((acc_own, both[:width]), (acc_other, both[width:])):
        acc[:width, half : half + side] += part[:, :side]
        acc[width : 2 * width, half : half + side] += part[:, side:]
    for k in range(4):
        acc_small[8 * k : 8 * k + 8, :] += sums[k]

    @pl.when(i == pl.num_programs(0) - 1)
    def _():
        vectors = [jnp.sum(acc_small[8 * k : 8 * k + 8, :], axis=0, keepdims=True) for k in range(4)]
        d = cot.shape[1]
        for acc, keep, send in ((acc_own, keep_own, send_own), (acc_other, keep_other, send_other)):
            mine = acc[d : d + 1, :half]
            put_vectors(acc, half + side, vectors + [mine[:, :d], mine[:, d:]])
            put_blocks(scal[0], [keep, send], acc, slice(None))


def down_block(scal, cot, mid, n2, pre, ctx_a, ctx_b, wo_a, wu_a, parts, wd, gain):
    total, d = cot.shape
    width = ctx_a.shape[1]
    half = wu_a.shape[1]
    args = (cot, mid, n2, pre, ctx_a, ctx_b, wo_a, *parts[0], wu_a, *parts[1], *wd, gain)
    in_specs = [rows_spec(TB, d), rows_spec(TB, d), rows_spec(TB, d), rows_spec(TB, 2 * half)]
    in_specs += [rows_spec(TB, width), rows_spec(TB, width)]
    in_specs += [tail_spec(v, width) if k in (1, 2) else const_spec(v.shape) for k, v in enumerate(args[6:])]
    columns = half + d // 2 + EXTRA
    pack = (BLOCKS // 2, d // BLOCKS, columns)
    outs = [((total, d), BF16), ((total, width), BF16), ((total, width), BF16), *[(pack, BF16)] * 4]
    out_specs = [rows_spec(TB, d), rows_spec(TB, width), rows_spec(TB, width)]
    out_specs += [const_spec(s) for s, _ in outs[3:]]
    scratch = [
        pltpu.VMEM((d + ONES, columns), F32), pltpu.VMEM((d + ONES, columns), F32),
        pltpu.VMEM((32, d), F32), pltpu.VMEM((2 * width, d), BF16), pltpu.VMEM((d, half), BF16),
        pltpu.VMEM((TB, 2 * width), BF16),
        pltpu.VMEM((d + ONES, TB), BF16),
        pltpu.VMEM((TB, FB), BF16), pltpu.VMEM((TB, FB), BF16), pltpu.VMEM((TB, 2 * half), BF16),
        pltpu.VMEM((TB, d), F32), pltpu.VMEM((TB, d), F32),
    ]
    return call(
        down_kernel, "feed_back", total // TB, (scal,), in_specs, outs, out_specs, scratch,
        2 * total * d * (6 * half + 4 * width), total * (16 * d + 4 * half), args,
    )


def out_rows(mid, hidden, wd_a, wd_b, bd, out):
    half = wd_a.shape[0]
    out[...] = (
        mid[...] + dot_nn(hidden[:, :half], wd_a[...]) + dot_nn(hidden[:, half:], wd_b[...]) + bd[...]
    ).astype(BF16)


def out_kernel(scal, mid, hidden, wd_a, wd_b, bd, *refs):
    out_rows(mid, hidden, wd_a, wd_b, bd, refs[-1])


def out_down_kernel(scal, mid, hidden, wd_a, wd_b, bd, before, d0, d1, out, down, d_all):
    out_rows(mid, hidden, wd_a, wd_b, bd, out)

    @pl.when(pl.program_id(0) == 0)
    def _():
        place(scal[1], (d0, d1), d_all, BF16)
        down[...] = d_all[...].T.astype(F32)


def part_spec(first, cols):
    return pl.BlockSpec((TM, cols), lambda i, *_: (i + first, 0))


def out_block(first, tiles, scal, mid, hidden, wd, bd, before, pieces=()):
    total, d = mid.shape
    args = (mid, hidden, *wd, bd)
    specs = [part_spec(first, d), part_spec(first, hidden.shape[1])]
    specs += [const_spec(a.shape) for a in (*wd, bd)]
    alias = {}
    if before is not None:
        alias = {len(args) + 1: 0}
        args += (before,)
        specs += [pl.BlockSpec(memory_space=pl.ANY)]
    outs, out_specs, scratch = [((total, d), BF16)], [part_spec(first, d)], []
    if pieces:
        args += tuple(pieces)
        specs += [const_spec(p.shape) for p in pieces]
        shape = (pieces[0].shape[2], d)
        outs += [(shape, F32)]
        out_specs += [const_spec(shape)]
        scratch = [pltpu.VMEM(shape[::-1], BF16)]
    return call(
        out_down_kernel if pieces else out_kernel, "layer_out", tiles, (scal,), specs, outs, out_specs, scratch,
        2 * tiles * TM * d * hidden.shape[1], tiles * TM * (6 * d + 2 * hidden.shape[1]), args, alias,
    )


def attend_back_kernel(
    heads, scal, nn, proj, probs, gctx, w, gain, shift, gproj, pack_keep, pack_send, kpad, vpad, dk, dv, acc, acc_b, gprob, gscore
):
    s = pl.program_id(0)
    clear(s, acc, acc_b)
    width = heads * HEAD_DIM
    edge = jnp.zeros((WIN - QB, width), BF16)
    for pad, j in ((kpad, 1), (vpad, 2)):
        pad[0 : WIN - QB, :] = edge
        pad[SEQ_LEN:, :] = edge
        pad[MARGIN : MARGIN + SEQ_LEN, :] = proj[:, j * width : (j + 1) * width]
    mask = head_mask(1.0, heads)
    dk[0 : (WIN - QB), :] = jnp.zeros(((WIN - QB), width), F32)
    dv[0 : (WIN - QB), :] = jnp.zeros(((WIN - QB), width), F32)
    scale = HEAD_DIM**-0.5

    def rows(b):
        return slice(b * QB, (b + 1) * QB)

    def keys(b):
        return slice(b * QB, b * QB + WIN)

    def own(b):
        return slice(b * WIN, (b + 1) * WIN)

    for b in range(NBLK):
        gprob[own(b), :] = dot_nt(vpad[keys(b), :], spread(gctx[rows(b), :], mask, heads))
    for b in range(NBLK):
        p = probs[own(b), :].astype(F32)
        gp = gprob[own(b), :]
        gscore[own(b), :] = (p * (gp - jnp.sum(p * gp, axis=0, keepdims=True))).astype(BF16)
    for b in range(NBLK):
        gproj[rows(b), 0:width] = (pair_rows(gscore[own(b), :], kpad[keys(b), :], heads) * scale).astype(BF16)
    for b in range(NBLK):
        key_term = dot_nn(gscore[own(b), :], spread(proj[rows(b), 0:width], mask, heads)) * scale
        value_term = dot_nn(probs[own(b), :], spread(gctx[rows(b), :], mask, heads))
        for total, term in ((dk, key_term), (dv, value_term)):
            total[b * QB : b * QB + (WIN - QB), :] += term[: (WIN - QB)]
            total[b * QB + (WIN - QB) : b * QB + WIN, :] = term[(WIN - QB) :]
    gproj[:, width : 2 * width] = dk[MARGIN : MARGIN + SEQ_LEN, :].astype(BF16)
    gproj[:, 2 * width :] = dv[MARGIN : MARGIN + SEQ_LEN, :].astype(BF16)
    gp_all = gproj[...]
    acc[:, : 3 * width] += dot_tn(nn[...], gp_all)
    acc_b[...] += jnp.sum(gp_all.astype(F32), axis=0, keepdims=True)

    @pl.when(s == pl.num_programs(0) - 1)
    def _():
        d = acc.shape[0]
        column = lambda v: jnp.broadcast_to(v[...], (EXTRA, d)).T[:, 0:1]
        gain_col, shift_col = column(gain), column(shift)
        gain_grad, shift_grad = jnp.zeros((d, EXTRA), F32), jnp.zeros((d, EXTRA), F32)
        for j in range(3):
            for c in range(0, width, EXTRA):
                at = slice(j * width + c, j * width + c + EXTRA)
                weight = w[:, at].astype(F32)
                total, sums = acc[:, at], acc_b[:, at]
                gain_grad += weight * total
                shift_grad += weight * sums
                acc[:, at] = gain_col * total + shift_col * sums
        gain_grad = jnp.sum(gain_grad, axis=1, keepdims=True)
        shift_grad = jnp.sum(shift_grad, axis=1, keepdims=True)
        put_vectors(acc, 3 * width, [jnp.concatenate([acc_b[:, :width], acc_b[:, 2 * width :]], axis=1)])
        lane = lax.broadcasted_iota(jnp.int32, (d, EXTRA), 1)
        extra = jnp.where(lane == 1, gain_grad, acc[:, 3 * width :])
        acc[:, 3 * width :] = jnp.where(lane == 2, shift_grad, extra)
        put_blocks(scal[1], [pack_keep, pack_send], acc, slice(None))


def attention_backward(scal, nn, proj, probs, gctx, w, gain, shift):
    total, d = nn.shape
    seqs = total // SEQ_LEN
    width = gctx.shape[1]
    heads = width // HEAD_DIM

    def body(*refs):
        attend_back_kernel(heads, *refs)

    pad = SEQ_LEN + WIN - QB
    columns = 3 * width + EXTRA
    pack = (BLOCKS // 2, d // BLOCKS, columns)
    return call(
        body, "attend_back", seqs, (scal,),
        [
            rows_spec(SEQ_LEN, d), rows_spec(SEQ_LEN, 3 * width),
            rows_spec(NBLK * WIN, heads * QB), rows_spec(SEQ_LEN, width),
            const_spec(w.shape), const_spec(gain.shape), const_spec(shift.shape),
        ],
        [((total, 3 * width), BF16), (pack, BF16), (pack, BF16)],
        [rows_spec(SEQ_LEN, 3 * width), const_spec(pack), const_spec(pack)],
        [
            pltpu.VMEM((pad, width), BF16), pltpu.VMEM((pad, width), BF16),
            pltpu.VMEM((pad, width), F32), pltpu.VMEM((pad, width), F32),
            pltpu.VMEM((d, columns), F32), pltpu.VMEM((1, 3 * width), F32),
            pltpu.VMEM((NBLK * WIN, heads * QB), F32), pltpu.VMEM((NBLK * WIN, heads * QB), BF16),
        ],
        2 * total * d * 3 * width + 16 * total * WIN * width, total * (d + 9 * width) * 2,
        (nn, proj, probs, gctx, w, gain, shift),
    )


def last_kernel(per_seq, first, scal, x, gmid, gp_a, gp_b, w_a, w_b, gain, *refs):
    gin, back_a, back_b = refs[-3:]
    i = pl.program_id(0)
    rows = x.shape[0]
    tile = i + first
    back_a[...] = dot_nt(gp_a[...], w_a[...])
    back_b[...] = dot_nt(gp_b[...], w_b[...])
    for sub in subs(rows):
        keep = keep_of((SUB, x.shape[1]), (tile % per_seq) * rows + sub.start, tile // per_seq, scal)
        nn, r = normalize(x[sub, :].astype(F32) * keep)
        u = (back_a[sub, :] + back_b[sub, :]) * gain[...]
        mean_un = jnp.mean(u * nn, axis=-1, keepdims=True)
        a = r * (u - jnp.mean(u, axis=-1, keepdims=True) - nn * mean_un)
        gin[sub, :] = (gmid[sub, :].astype(F32) + a) * keep


def last_block(part, parts, scal, x, gmid, gp_a, gp_b, w_a, w_b, gain, before):
    total, d = x.shape
    tiles = total // TM // parts

    def body(*refs):
        last_kernel(SEQ_LEN // TM, part * tiles, *refs)

    width = gp_a.shape[1]
    args = (x, gmid, gp_a, gp_b, w_a, w_b, gain)
    specs = [part_spec(part * tiles, c) for c in (d, d, width, width)]
    specs += [const_spec(a.shape) for a in args[4:]]
    alias = {}
    if before is not None:
        alias = {len(args) + 1: 0}
        args += (before,)
        specs += [pl.BlockSpec(memory_space=pl.ANY)]
    return call(
        body, "input_gradient", tiles, (scal,), specs, [((total, d), F32)], [part_spec(part * tiles, d)],
        [pltpu.VMEM((TM, d), F32)] * 2,
        4 * tiles * TM * d * width, tiles * TM * (10 * d + 4 * width), args, alias,
    )[0]


def place(me, pieces, out, kind, columns=slice(None)):
    each = pieces[0].shape[0]
    rows = pieces[0].shape[1]
    for j in range(BLOCKS):
        at = pl.ds(pl.multiple_of((j ^ me) * rows, rows), rows)
        out[at, :] = pieces[j // each][j % each, :, columns].astype(kind)


def unpack_kernel(scal, u0, u1, q0, q1, side_y, side_d, up, out, *refs):
    vectors, (bias_up, qkv, bias_q, gain, shift, u_side, q_all, q_side) = refs[:4], refs[4:]
    me = scal[0]
    half, side = up.shape[1], out.shape[1] // 2
    rows = out.shape[0]
    place(me, (u0, u1), up, F32, slice(0, half))
    place(me, (u0, u1), u_side, F32, slice(half, u0.shape[2]))
    out[:, :side] = u_side[:rows, :side]
    out[:, side:] = u_side[rows:, :side]
    sums = u_side[:, side:].T
    for k in range(4):
        vectors[k][...] = sums[k : k + 1, :]
    bias_up[...] = jnp.concatenate([sums[4:5, :], sums[5:6, :]], axis=1)
    place(scal[1], (q0, q1), q_all, F32)
    width = qkv.shape[2]
    for j in range(3):
        qkv[j] = q_all[:, j * width : (j + 1) * width]
    sums = q_all[:, 3 * width :].T
    bias_q[...] = jnp.concatenate([sums[0:1, :width], sums[0:1, width:]], axis=0)
    place(scal[1], (side_y, side_d), q_side, F32)
    sums += q_side[...].T
    gain[...] = sums[1:2, :]
    shift[...] = sums[2:3, :]


def unpack(scal, pieces, up, out, qkv):
    d = up[0]
    shapes = [up, out, *[(1, d)] * 4, (1, up[1]), qkv, (2, qkv[2]), (1, d), (1, d)]
    natural = [(d, pieces[0].shape[2] - up[1]), (d, pieces[2].shape[2]), (d, EXTRA)]
    return call(
        unpack_kernel, "unpack", 1, (scal,), [const_spec(p.shape) for p in pieces], [(s, F32) for s in shapes],
        [const_spec(s) for s in shapes], [pltpu.VMEM(s, F32) for s in natural], 0,
        6 * sum(p.size for p in pieces), tuple(pieces),
    )


def make_body(mesh):
    tp = mesh.shape["tensor"]
    dp = mesh.shape["dp"]
    paired = tp == 2 and dp == BLOCKS

    def across(v):
        return lax.ppermute(v, "tensor", [(0, 1), (1, 0)])

    def swap(v, distance):
        return lax.ppermute(v, "dp", [(i, i ^ distance) for i in range(dp)])

    def core(v):
        return swap(v, 1)

    def diagonal(v):
        pairs = [(2 * i + j, 2 * (i ^ 1) + 1 - j) for i in range(dp) for j in range(2)]
        return lax.ppermute(v, ("dp", "tensor"), pairs)

    def plus(first, *rest):
        total = first.astype(F32)
        for v in rest:
            total = total + v.astype(F32)
        return total.astype(first.dtype)

    def lower(v):
        return v[: v.shape[0] // 2]

    def upper(v):
        return v[v.shape[0] // 2 :]

    def join(a, b):
        return jnp.concatenate([a, b], axis=0)

    def window(kernel, args, moves):
        args, sent = lax.optimization_barrier((args, [v for v, _ in moves]))
        arrived = [move(v) for v, (_, move) in zip(sent, moves)]
        return lax.optimization_barrier((kernel(*args), arrived, sent))

    def body(
        inputs, cotangent, lengths, time_span, freq_span, gain_one, shift_one, qkv_weight, qkv_bias,
        out_weight, out_bias, gain_two, shift_two, up_weight, up_bias, down_weight, down_bias,
    ):
        total, d = inputs.shape
        seqs = total // SEQ_LEN
        here = lax.axis_index("tensor") * seqs
        index = lax.axis_index("dp")
        label = label_q = jnp.int32(0)
        if paired:
            label = ((index & 1) << 3) | ((index & 2) << 1) | ((index & 4) >> 1)
            label_q = ((index & 1) << 3) | (index & 4)
        place_here = jnp.stack([label, label_q, here, index & 1 if paired else jnp.int32(0)]).astype(jnp.int32)
        ends = [span.T.reshape(-1) for span in (time_span, freq_span)]
        scal = jnp.concatenate([place_here, lengths, *ends])
        row = lambda v: v.reshape(1, -1)

        def attend_a(rows, w, bias):
            return attention_forward(True, scal, rows, w, bias, row(gain_one), row(shift_one))

        def attend_b(rows, w, bias):
            return attention_forward(False, scal, rows, w, bias, None, None)

        def up(ctx_a, ctx_b, wo_a, wu_a, parts, biases):
            return up_block(
                scal, inputs, cotangent, ctx_a, ctx_b, wo_a, wu_a, parts, row(out_bias), row(gain_two),
                row(shift_two), biases,
            )

        def down(mid, n2, pre, ctx_a, ctx_b, wo_a, wu_a, parts, wd):
            return down_block(scal, cotangent, mid, n2, pre, ctx_a, ctx_b, wo_a, wu_a, parts, wd, row(gain_two))

        def back(nn, proj, probs, gctx, w):
            return attention_backward(scal, nn, proj, probs, gctx, w, row(gain_one), row(shift_one))

        def last(part, parts):
            return lambda gmid, gp_a, gp_b, w_a, w_b, before: last_block(
                part, parts, scal, inputs, gmid, gp_a, gp_b, w_a, w_b, row(gain_one), before
            )

        def out(first, tiles):
            return lambda mid, hidden, wd, before, *pieces: out_block(
                first, tiles, scal, mid, hidden, wd, row(down_bias), before, pieces
            )

        turned = lambda w: jnp.transpose(w, (1, 0, 2))
        if paired:
            odd = index & 1

            def part_of(v):
                rows = v.shape[0] // 2
                return lax.dynamic_slice_in_dim(v, odd * rows, rows, 0)

            qkv_a = turned(qkv_weight)
            side = d // 2
            low, high = qkv_a.reshape(2, -1, side)
            first_rows = jnp.where(
                odd == 0,
                jnp.concatenate([low, out_weight[:, :side]], axis=0),
                jnp.concatenate([high, out_weight[:, side:]], axis=0),
            )
            (nn, n1, proj_a, ctx_a, probs_a, side_a), (first_half, bias_b), _ = window(
                attend_a, (inputs, qkv_a, qkv_bias), [(first_rows, across), (qkv_bias, across)]
            )
            first_pair = (first_half, core(first_half))
            (proj_b, ctx_b, probs_b, side_b), (up_half, up_bias_b), _ = window(
                attend_b, (n1, first_pair, bias_b), [(part_of(up_weight), across), (row(up_bias), across)]
            )
            pairs = (first_pair, (up_half, core(up_half)))
            (mid, n2, hidden, pre, d_own, d_other), (down_b,), _ = window(
                up, (ctx_a, ctx_b, out_weight, up_weight, pairs, (row(up_bias), up_bias_b)), [(down_weight, across)]
            )
            wd = (down_weight, down_b)
            (gmid, gctx_a, gctx_b, u_own, u_other, u_send_own, u_send_other), (d_cross,), _ = window(
                down, (mid, n2, pre, ctx_a, ctx_b, out_weight, up_weight, pairs, wd), [(d_other, across)]
            )
            step = lambda distance: lambda v: swap(v, distance)
            u_other, u_own = plus(u_other, core(u_send_other)), plus(u_own, core(u_send_own))
            d_sum = plus(d_own, d_cross)
            d_sum = plus(lower(d_sum), core(upper(d_sum)))
            (gproj_b, q_other, q_send), (u_cross, d_in), _ = window(
                back, (nn, proj_b, probs_b, gctx_b, side_b), [(u_other, across), (upper(d_sum), step(4))]
            )
            u_sum = plus(u_own, u_cross)
            d_sum = plus(lower(d_sum), d_in)
            q_other = plus(q_other, core(q_send))
            (gproj_a, q_own, q_send), (u_in, d_in, q_cross), _ = window(
                back, (nn, proj_a, probs_a, gctx_a, side_a),
                [(upper(u_sum), step(2)), (d_sum, step(8)), (q_other, across)],
            )
            u_sum = plus(lower(u_sum), u_in)
            d_sum = plus(d_sum, d_in)
            q_terms = (q_own, core(q_send), q_cross)
            input_grad, (u_in, d_in, q_in), _ = window(
                last(0, 2), (gmid, gproj_a, gproj_b, side_a, side_b, None),
                [(upper(u_sum), step(4)), (d_sum, step(2)), (plus(*map(upper, q_terms)), step(4))],
            )
            u_sum = plus(lower(u_sum), u_in)
            d_sum = plus(d_sum, d_in)
            q_sum = plus(*map(lower, q_terms), q_in)
            input_grad, (u_in, d_in, q_in), _ = window(
                last(1, 2), (gmid, gproj_a, gproj_b, side_a, side_b, input_grad),
                [(u_sum, step(8)), (d_sum, step(4)), (q_sum, step(2))],
            )
            u_sum = plus(u_sum, u_in)
            d_sum = join(d_sum, d_in)
            q_sum = plus(q_sum, q_in)
            tiles = total // TM
            cuts = (0, tiles * 5 // 8, tiles * 7 // 8, tiles)
            (layer_out,), (u_in, d_in, q_in), _ = window(
                out(cuts[0], cuts[1] - cuts[0]), (mid, hidden, wd, None),
                [(u_sum, step(4)), (d_sum, core), (q_sum, step(8))],
            )
            u_sum = join(u_sum, u_in)
            q_sum = plus(q_sum, q_in)
            (layer_out, g_down), (u_in, q_in), _ = window(
                out(cuts[1], cuts[2] - cuts[1]), (mid, hidden, wd, layer_out, d_sum, d_in),
                [(u_sum, step(2)), (q_sum, step(4))],
            )
            u_sum = join(u_sum, u_in)
            q_sum = join(q_sum, q_in)
            sides = q_sum[:, :, q_sum.shape[2] - EXTRA :]
            (layer_out,), (u_in, q_in, side_y, side_d), _ = window(
                out(cuts[2], cuts[3] - cuts[2]), (mid, hidden, wd, layer_out),
                [(u_sum, core), (q_sum, core), (sides, across), (sides, diagonal)],
            )
            g_up, g_out, *shared_two, g_bu, g_qkv, g_qb, gain_grad, shift_grad = unpack(
                scal, (u_sum, u_in, q_sum, q_in, side_y, side_d), up_weight.shape, out_weight.shape, qkv_a.shape
            )
            g_qkv = turned(g_qkv)
            g_bu = g_bu.reshape(-1)
            shared_two = [v.reshape(-1) for v in shared_two]
            shared_one = [v.reshape(-1) for v in (gain_grad, shift_grad)]
        else:
            def halves(local, axis):
                return tuple(jnp.split(lax.all_gather(local, "tensor", axis=axis, tiled=True), 2, axis=axis))

            def sums(own, other, axis):
                whole = jnp.concatenate([own, other], axis=axis)
                part = lax.psum_scatter(whole, "tensor", scatter_dimension=axis, tiled=True)
                return lax.psum(part, "dp").astype(F32)

            natural = lambda *packs: jnp.concatenate(packs, axis=0).reshape(d, -1)
            qkv = [turned(w) for w in halves(qkv_weight, 2)]
            biases = halves(qkv_bias, 1)
            up_biases = [row(b) for b in halves(up_bias, 0)]
            wo, wu, wd = halves(out_weight, 0), halves(up_weight, 1), halves(down_weight, 0)
            nn, n1, proj_a, ctx_a, probs_a, side_a = attend_a(inputs, qkv[0], biases[0])
            halves_b = jnp.split(qkv[1].reshape(-1, qkv[1].shape[2]), 2, axis=0)
            proj_b, ctx_b, probs_b, side_b = attend_b(n1, halves_b, biases[1])
            parts = (jnp.split(wo[1], 2, axis=1), jnp.split(wu[1], 2, axis=0))
            mid, n2, hidden, pre, d_own, d_other = up(ctx_a, ctx_b, wo[0], wu[0], parts, up_biases)
            gmid, gctx_a, gctx_b, *u_packs = down(mid, n2, pre, ctx_a, ctx_b, wo[0], wu[0], parts, wd)
            gproj_b, *q_other = back(nn, proj_b, probs_b, gctx_b, side_b)
            gproj_a, *q_own = back(nn, proj_a, probs_a, gctx_a, side_a)
            input_grad = last(0, 1)(gmid, gproj_a, gproj_b, side_a, side_b, None)
            layer_out = out(0, total // TM)(mid, hidden, wd, None)[0]
            g_down = sums(natural(d_own), natural(d_other), 1).T
            u = natural(u_packs[0], u_packs[2]), natural(u_packs[1], u_packs[3])
            half, side = wu[0].shape[1], d // 2
            g_up = sums(u[0][:, :half], u[1][:, :half], 1)
            beside = [jnp.concatenate(jnp.split(v[:, half : half + side], 2, axis=0), axis=1) for v in u]
            g_out = sums(*beside, 0)
            q = natural(*q_own), natural(*q_other)
            wide = 3 * qkv[0].shape[2]
            g_qkv = sums(*[v[:, :wide].reshape(d, 3, -1) for v in q], 2)
            g_qb = sums(*[v[:, wide].reshape(2, -1) for v in q], 1)
            small_two = [v[:, half + side :].T for v in u]
            g_bu = sums(*[v[4:6].reshape(-1) for v in small_two], 0)
            shared_two = lax.psum(small_two[0][:4], ("dp", "tensor")).astype(F32)
            vectors = (q[0] + q[1])[:, wide + 1 : wide + 3].T
            shared_one = lax.psum(vectors, ("dp", "tensor")).astype(F32)
        return (
            layer_out, input_grad, shared_one[0], shared_one[1], g_qkv, g_qb, g_out, shared_two[2],
            shared_two[0], shared_two[1], g_up, g_bu, g_down, shared_two[3],
        )

    return body


def solution(mesh):
    in_specs = (
        P(("dp", "tensor"), None), P(("dp", "tensor"), None), P("dp"), P("dp", None), P("dp", None), P(), P(),
        P(None, None, "tensor"), P(None, "tensor"), P("tensor", None), P(), P(), P(), P(None, "tensor"),
        P("tensor"), P("tensor", None), P(),
    )
    out_specs = (
        P(("dp", "tensor"), None), P(("dp", "tensor"), None), P(), P(), P(None, None, "tensor"), P(None, "tensor"),
        P("tensor", None), P(), P(), P(), P(None, "tensor"), P("tensor"), P("tensor", None), P(),
    )
    return jax.shard_map(make_body(mesh), mesh=mesh, in_specs=in_specs, out_specs=out_specs, check_vma=False)
```

```python
import jax
import jax.numpy as jnp
from jax import lax
from jax.experimental import pallas as pl
from jax.experimental.pallas import tpu as pltpu
from jax.sharding import PartitionSpec as P

HEAD_DIM = 64
SEQ_LEN = 1024
LEFT = 10
RIGHT = 2
QB = 64
MARGIN = 14
WIN = QB + 16
NBLK = SEQ_LEN // QB
EPS = 1e-05
LN_ROWS = 256
NEG = -1000000000.0
F32 = jnp.float32
BF16 = jnp.bfloat16


def dot_nn(a, b):
    return jnp.dot(a, b, preferred_element_type=F32)


def dot_nt(a, b):
    return lax.dot_general(a, b, (((1,), (1,)), ((), ())), preferred_element_type=F32)


def dot_tn(a, b):
    return lax.dot_general(a, b, (((0,), (0,)), ((), ())), preferred_element_type=F32)


def length_of(scal, seq):
    return scal[4 + scal[2] + seq]


def keep_of(shape, first_pos, seq, scal):
    seqs = (scal.shape[0] - 4) // 5
    ends = [scal[4 + k * seqs + scal[2] + seq] for k in range(1, 5)]
    pos = first_pos + lax.broadcasted_iota(jnp.int32, (shape[0], 1), 0)
    col = lax.broadcasted_iota(jnp.int32, (1, shape[1]), 1)
    rows = jnp.where((pos >= ends[0]) & (pos < ends[1]), 0.0, 1.0)
    cols = jnp.where((col >= ends[2]) & (col < ends[3]), 0.0, 1.0)
    return rows * cols


def normalize(v):
    off = v - jnp.mean(v, axis=-1, keepdims=True)
    r = lax.rsqrt(jnp.mean(off * off, axis=-1, keepdims=True) + EPS)
    return off * r, r


def head_mask(scale, heads):
    row = lax.broadcasted_iota(jnp.int32, (heads * QB, heads * HEAD_DIM), 0)
    col = lax.broadcasted_iota(jnp.int32, (heads * QB, heads * HEAD_DIM), 1)
    return jnp.where(row // QB == col // HEAD_DIM, scale, 0.0).astype(BF16)


def spread(block, mask, heads):
    return jnp.concatenate([block] * heads, axis=0) * mask


def pair_rows(probs, window, heads):
    out = []
    low = lax.broadcasted_iota(jnp.int32, (QB, 2 * HEAD_DIM), 1) < HEAD_DIM
    for p in range(heads // 2):
        both = dot_tn(
            probs[:, p * 2 * QB : (p + 1) * 2 * QB],
            window[:, p * 2 * HEAD_DIM : (p + 1) * 2 * HEAD_DIM],
        )
        out.append(jnp.where(low, both[:QB], both[QB:]))
    return jnp.concatenate(out, axis=1)


def attend(length, proj, kpad, vpad, scores, ctx, probs_out, heads):
    width = heads * HEAD_DIM
    edge = jnp.zeros((WIN - QB, width), BF16)
    for pad, j in ((kpad, 1), (vpad, 2)):
        pad[0 : WIN - QB, :] = edge
        pad[SEQ_LEN:, :] = edge
        pad[MARGIN : MARGIN + SEQ_LEN, :] = proj[:, j * width : (j + 1) * width]
    mask = head_mask(HEAD_DIM**-0.5, heads)
    key = lax.broadcasted_iota(jnp.int32, (WIN, heads * QB), 0)
    query = lax.broadcasted_iota(jnp.int32, (WIN, heads * QB), 1) % QB
    rel = key - MARGIN - query
    band = jnp.where((rel >= -LEFT) & (rel <= RIGHT), 0.0, NEG)
    diagonal = jnp.where(rel == 0, 0.0, NEG)

    for b in range(NBLK):
        q_all = spread(proj[b * QB : (b + 1) * QB, 0:width], mask, heads)
        scores[b * WIN : (b + 1) * WIN, :] = dot_nt(kpad[b * QB : b * QB + WIN, :], q_all)
    for b in range(NBLK):
        at = slice(b * WIN, (b + 1) * WIN)
        pos = key + (b * QB - MARGIN)
        live = (pos < length) if b else (pos >= 0) & (pos < length)
        masked = scores[at, :] + jnp.where(live, band, diagonal)
        weights = jnp.exp(masked - jnp.max(masked, axis=0, keepdims=True))
        probs_out[at, :] = (weights / jnp.sum(weights, axis=0, keepdims=True)).astype(BF16)
    for b in range(NBLK):
        v_win = vpad[b * QB : b * QB + WIN, :]
        ctx[b * QB : (b + 1) * QB, :] = pair_rows(probs_out[b * WIN : (b + 1) * WIN, :], v_win, heads).astype(BF16)


def project(at, n1, w_side, bias, proj):
    width = bias.shape[1]
    value = dot_nn(n1[at, :], w_side[...])
    proj[at, :width] = (value[:, :width] + bias[0:1, :]).astype(BF16)
    proj[at, width : 2 * width] = value[:, width : 2 * width].astype(BF16)
    proj[at, 2 * width :] = (value[:, 2 * width :] + bias[1:2, :]).astype(BF16)


def parts_in_order(scal, mine, theirs):
    odd = jnp.where(scal[3] == 0, 0, 1)
    return ((mine, odd), (theirs, 1 - odd))


def first_kernel(heads, scal, x, w, bias, gain, shift, nn, n1, proj, ctx, probs, w_side, *scratch):
    s = pl.program_id(0)

    @pl.when(s == 0)
    def _():
        width = w.shape[2]
        for j in range(3):
            w_side[:, j * width : (j + 1) * width] = w[j]

    for first in range(0, SEQ_LEN, LN_ROWS):
        at = slice(first, first + LN_ROWS)
        for r in range(first, first + LN_ROWS, SUB):
            sub = slice(r, r + SUB)
            keep = keep_of((SUB, x.shape[1]), r, s, scal)
            value = normalize(x[sub, :].astype(F32) * keep)[0]
            nn[sub, :] = value.astype(BF16)
            n1[sub, :] = (value * gain[...] + shift[...]).astype(BF16)
        project(at, n1, w_side, bias, proj)
    attend(length_of(scal, s), proj, *scratch, ctx, probs, heads)


def second_kernel(heads, scal, n1, mine, theirs, bias, proj, ctx, probs, w_side, *scratch):
    s = pl.program_id(0)

    @pl.when(s == 0)
    def _():
        width = bias.shape[1]
        half = n1.shape[1] // 2
        for part, place_of in parts_in_order(scal, mine, theirs):
            for k in range(3):
                stretch = 3 * place_of + k
                row = pl.multiple_of((stretch % 2) * half, half)
                column = pl.multiple_of((stretch // 2) * width, width)
                w_side[pl.ds(row, half), pl.ds(column, width)] = part[k * half : (k + 1) * half, :]

    for first in range(0, SEQ_LEN, LN_ROWS):
        project(slice(first, first + LN_ROWS), n1, w_side, bias, proj)
    attend(length_of(scal, s), proj, *scratch, ctx, probs, heads)


def const_spec(shape):
    return pl.BlockSpec(shape, lambda *_: (0,) * len(shape), pipeline_mode=pl.Buffered(1))


def rows_spec(rows, cols):
    return pl.BlockSpec((rows, cols), lambda i, *_: (i, 0))


NEEDS = {
    "attend_first": 60, "attend_second": 48, "feed_up": 47, "feed_back": 40, "attend_back": 60,
    "input_gradient": 60, "layer_out": 57, "unpack": 20,
}


def params(name):
    return pltpu.CompilerParams(vmem_limit_bytes=NEEDS[name] * 1024 * 1024, dimension_semantics=("arbitrary",))


def attention_forward(first, scal, rows, w, bias, gain, shift):
    total, width_in = rows.shape
    seqs = total // SEQ_LEN
    width = bias.shape[1]
    heads = width // HEAD_DIM
    outs = [
        jax.ShapeDtypeStruct((total, 3 * width), BF16),
        jax.ShapeDtypeStruct((total, width), BF16),
        jax.ShapeDtypeStruct((seqs * NBLK * WIN, heads * QB), BF16),
        jax.ShapeDtypeStruct((width_in, 3 * width), BF16),
    ]
    out_specs = [
        rows_spec(SEQ_LEN, 3 * width),
        rows_spec(SEQ_LEN, width),
        rows_spec(NBLK * WIN, heads * QB),
        const_spec((width_in, 3 * width)),
    ]
    scratch = [pltpu.VMEM((SEQ_LEN + WIN - QB, width), BF16)] * 2
    scratch += [pltpu.VMEM((NBLK * WIN, heads * QB), F32)]
    flops = 2 * total * width_in * 3 * width + 8 * total * WIN * width
    cost = pl.CostEstimate(flops=flops, bytes_accessed=total * (width_in + 6 * width) * 2, transcendentals=0)
    if first:
        in_specs = [rows_spec(SEQ_LEN, width_in)] + [const_spec(v.shape) for v in (w, bias, gain, shift)]
        outs = [jax.ShapeDtypeStruct(rows.shape, BF16)] * 2 + outs
        out_specs = [rows_spec(SEQ_LEN, width_in)] * 2 + out_specs
        args = (rows, w, bias, gain, shift)
    else:
        half_spec = pl.BlockSpec((3 * width_in // 2, width), lambda *_: (0, 0), pipeline_mode=pl.Buffered(1))
        in_specs = [rows_spec(SEQ_LEN, width_in), half_spec, half_spec, const_spec(bias.shape)]
        args = (rows, *w, bias)

    def body(*refs):
        (first_kernel if first else second_kernel)(heads, *refs)

    return pl.pallas_call(
        body,
        grid_spec=pltpu.PrefetchScalarGridSpec(
            num_scalar_prefetch=1,
            grid=(seqs,),
            in_specs=in_specs,
            out_specs=out_specs,
            scratch_shapes=scratch,
        ),
        out_shape=outs,
        compiler_params=params("attend_first" if first else "attend_second"),
        cost_estimate=cost,
        name="attend_first" if first else "attend_second",
    )(scal, *args)


TM = 512
TU = 1024
TB = 512
FC = 512
FB = 512
SUB = 32
GELU_A = 0.7978845608028654
GELU_K = 0.044715 / 0.7978845608028654**2


def subs(rows):
    return [slice(r, r + SUB) for r in range(0, rows, SUB)]


def fold_rows(v):
    return jnp.sum(v.reshape(-1, 8, v.shape[-1]), axis=0)


def clear(i, *refs):
    @pl.when(i == 0)
    def _():
        for ref in refs:
            ref[...] = jnp.zeros_like(ref)


TAIL = 2
ONES = 16
EXTRA = 128
BLOCKS = 16


def put_blocks(me, packs, acc, columns):
    rows = packs[0].shape[1]
    each = BLOCKS // len(packs)
    for j in range(BLOCKS):
        first = pl.multiple_of((j ^ me) * rows, rows)
        packs[j // each][j % each] = acc[pl.ds(first, rows), columns].astype(BF16)


def put_vectors(acc, first, vectors):
    spare = EXTRA - len(vectors)
    rows = vectors[0].shape[1]
    acc[:rows, first:] = jnp.concatenate(vectors + [jnp.zeros((spare, rows), F32)], axis=0).T


def assemble(scal, wo_a, wo_m, wo_t, wu_m, wu_t, wo_s, wu_b):
    width, side, rows = wo_a.shape[0], wo_m.shape[1], wu_m.shape[0]
    wo_s[:width, :] = wo_a[...]
    for part, place_of in parts_in_order(scal, wo_m, wo_t):
        wo_s[width:, pl.ds(pl.multiple_of(place_of * side, side), side)] = part[...]
    for part, place_of in parts_in_order(scal, wu_m, wu_t):
        wu_b[pl.ds(pl.multiple_of(place_of * rows, rows), rows), :] = part[...]


def up_kernel(
    per_seq, scal,
    x, cot, ctx_a, ctx_b, wo_a, wo_m, wo_t, wu_a, wu_m, wu_t, bo, gain, shift, bias_a, bias_b,
    mid_out, n2_out, hidden_out, pre_out, pack_own, pack_other,
    acc_d, wo_s, wu_b, ctx_s, branch, n2_half, pre_even, pre_odd,
):
    i = pl.program_id(0)
    clear(i, acc_d)
    width = ctx_a.shape[1]

    @pl.when(i == 0)
    def _():
        assemble(scal, wo_a, wo_m, wo_t, wu_m, wu_t, wo_s, wu_b)

    rows = x.shape[0]
    ctx_s[:, :width] = ctx_a[...]
    ctx_s[:, width:] = ctx_b[...]
    branch[...] = dot_nn(ctx_s[...], wo_s[...])
    g_t = cot[...].T
    for sub in subs(rows):
        keep = keep_of((SUB, x.shape[1]), (i % per_seq) * rows + sub.start, i // per_seq, scal)
        mid = x[sub, :].astype(F32) * keep + branch[sub, :] + bo[...]
        mid_out[sub, :] = mid
        n2 = (normalize(mid)[0] * gain[...] + shift[...]).astype(BF16)
        n2_out[sub, :] = n2
        n2_half[sub, :] = n2 * 0.5
    half = wu_a.shape[1]
    chunks = [(part, c) for part in range(2) for c in range(half // FC)]
    pres = (pre_even, pre_odd)

    def up(n):
        part, c = chunks[n]
        pres[n % 2][...] = dot_nn(n2_half[...], (wu_a, wu_b)[part][:, c * FC : (c + 1) * FC])

    up(0)
    for n, (part, c) in enumerate(chunks):
        if n + 1 < len(chunks):
            up(n + 1)
        bias = (bias_a, bias_b)[part][:, c * FC : (c + 1) * FC] * 0.5
        ts = slice(part * half + c * FC, part * half + (c + 1) * FC)
        for sub in subs(rows):
            v = pres[n % 2][sub, :] + bias
            z = v * (2 * GELU_A)
            pre_out[sub, ts] = z.astype(BF16)
            t = jnp.tanh(z * (1.0 + GELU_K * (z * z)))
            hidden_out[sub, ts] = (v + v * t).astype(BF16)
        acc_d[:, ts] += dot_nn(g_t, hidden_out[:, ts])

    @pl.when(i == pl.num_programs(0) - 1)
    def _():
        put_blocks(scal[1], [pack_own], acc_d, slice(0, half))
        put_blocks(scal[1], [pack_other], acc_d, slice(half, 2 * half))


def call(kernel, name, grid, scalars, in_specs, outs, out_specs, scratch, flops, nbytes, args, alias=()):
    return pl.pallas_call(
        kernel,
        grid_spec=pltpu.PrefetchScalarGridSpec(
            num_scalar_prefetch=len(scalars), grid=(grid,), in_specs=in_specs, out_specs=out_specs,
            scratch_shapes=scratch,
        ),
        out_shape=[jax.ShapeDtypeStruct(s, t) for s, t in outs],
        compiler_params=params(name),
        input_output_aliases=dict(alias),
        cost_estimate=pl.CostEstimate(flops=flops, bytes_accessed=nbytes, transcendentals=0),
        name=name,
    )(*scalars, *args)


def tail_spec(v, rows):
    return pl.BlockSpec(
        (rows, v.shape[1]), lambda *_: (v.shape[0] // rows - 1, 0), pipeline_mode=pl.Buffered(1)
    )


def up_block(scal, x, cot, ctx_a, ctx_b, wo_a, wu_a, parts, bo, gain, shift, biases):
    total, d = x.shape
    width = ctx_a.shape[1]
    half = wu_a.shape[1]
    args = (x, cot, ctx_a, ctx_b, wo_a, *parts[0], wu_a, *parts[1], bo, gain, shift, *biases)
    in_specs = [rows_spec(TU, d), rows_spec(TU, d), rows_spec(TU, width), rows_spec(TU, width)]
    in_specs += [tail_spec(v, width) if k in (1, 2) else const_spec(v.shape) for k, v in enumerate(args[4:])]
    pack = (BLOCKS, d // BLOCKS, half)
    outs = [
        ((total, d), F32), ((total, d), BF16), ((total, 2 * half), BF16), ((total, 2 * half), BF16),
        (pack, BF16), (pack, BF16),
    ]
    out_specs = [rows_spec(TU, d), rows_spec(TU, d), rows_spec(TU, 2 * half), rows_spec(TU, 2 * half)]
    out_specs += [const_spec(s) for s, _ in outs[4:]]
    scratch = [
        pltpu.VMEM((d, 2 * half), F32), pltpu.VMEM((2 * width, d), BF16), pltpu.VMEM((d, half), BF16),
        pltpu.VMEM((TU, 2 * width), BF16),
        pltpu.VMEM((TU, d), F32), pltpu.VMEM((TU, d), BF16), pltpu.VMEM((TU, FC), F32), pltpu.VMEM((TU, FC), F32),
    ]

    def body(*refs):
        up_kernel(SEQ_LEN // TU, *refs)

    return call(
        body, "feed_up", total // TU, (scal,), in_specs, outs, out_specs, scratch,
        2 * total * d * (4 * half + 2 * width), total * (18 * d + 8 * half), args,
    )


def down_kernel(
    scal,
    cot, mid, n2_in, pre, ctx_a, ctx_b, wo_a, wo_m, wo_t, wu_a, wu_m, wu_t, wd_a, wd_b, gain,
    gmid_out, gctx_a, gctx_b, keep_own, keep_other, send_own, send_other,
    acc_own, acc_other, acc_small, wo_s, wu_b, ctx_s, n2_t, gh_even, gh_odd, gpre, back_a, back_b,
):
    i = pl.program_id(0)
    clear(i, acc_own, acc_other, acc_small)
    width = ctx_a.shape[1]

    @pl.when(i == 0)
    def _():
        assemble(scal, wo_a, wo_m, wo_t, wu_m, wu_t, wo_s, wu_b)


    rows = cot.shape[0]
    ctx_s[:, :width] = ctx_a[...]
    ctx_s[:, width:] = ctx_b[...]
    n2_t[:-ONES, :] = n2_in[...].T
    n2_t[-ONES:, :] = jnp.ones((ONES, rows), BF16)
    half = wu_a.shape[1]
    chunks = [(part, c) for part in range(2) for c in range(half // FB)]
    ghs = (gh_even, gh_odd)

    def up(n):
        part, c = chunks[n]
        ghs[n % 2][...] = dot_nt(cot[...], (wd_a, wd_b)[part][c * FB : (c + 1) * FB, :]).astype(BF16)

    def vector(n):
        part, c = chunks[n]
        ts = slice(part * half + c * FB, part * half + (c + 1) * FB)
        for sub in subs(rows):
            z = pre[sub, ts]
            k = z * z * GELU_K
            t = jnp.tanh(z * (k + 1.0))
            slope = (t + 1.0) * ((z * (k * 1.5 + 0.5)) * (1.0 - t) + 0.5)
            gpre[sub, ts] = slope * ghs[n % 2][sub, :]

    def use(n):
        part, c = chunks[n]
        ts = slice(part * half + c * FB, part * half + (c + 1) * FB)
        (acc_own, acc_other)[part][:, c * FB : (c + 1) * FB] += dot_nn(n2_t[...], gpre[:, ts])

    up(0)
    for n in range(len(chunks)):
        if n + 1 < len(chunks):
            up(n + 1)
        if n:
            use(n - 1)
        vector(n)
    use(len(chunks) - 1)
    sums = [jnp.zeros((8, cot.shape[1]), F32) for _ in range(4)]
    side = cot.shape[1] // 2
    parts = [slice(k * rows // TAIL, (k + 1) * rows // TAIL) for k in range(TAIL)]

    def back(at):
        back_a[at, :] = dot_nt(gpre[at, :half], wu_a[...])
        back_b[at, :] = dot_nt(gpre[at, half:], wu_b[...])

    back(parts[0])
    for k, at in enumerate(parts):
        if k + 1 < TAIL:
            back(parts[k + 1])
        for r in range(at.start, at.stop, SUB):
            sub = slice(r, r + SUB)
            gn2 = back_a[sub, :] + back_b[sub, :]
            nn, r_std = normalize(mid[sub, :])
            gnn = gn2 * nn
            u = gn2 * gain[...]
            mean_un = jnp.mean(gnn * gain[...], axis=-1, keepdims=True)
            g = cot[sub, :].astype(F32)
            gm = g + r_std * (u - jnp.mean(u, axis=-1, keepdims=True) - nn * mean_un)
            gmid_out[sub, :] = gm.astype(BF16)
            for q, term in enumerate((gnn, gn2, gm, g)):
                sums[q] += fold_rows(term)
        gctx = dot_nt(gmid_out[at, :], wo_s[...])
        gctx_a[at, :] = gctx[:, :width].astype(BF16)
        gctx_b[at, :] = gctx[:, width:].astype(BF16)
    both = dot_tn(ctx_s[...], gmid_out[...])
    for acc, part in ((acc_own, both[:width]), (acc_other, both[width:])):
        acc[:width, half : half + side] += part[:, :side]
        acc[width : 2 * width, half : half + side] += part[:, side:]
    for k in range(4):
        acc_small[8 * k : 8 * k + 8, :] += sums[k]

    @pl.when(i == pl.num_programs(0) - 1)
    def _():
        vectors = [jnp.sum(acc_small[8 * k : 8 * k + 8, :], axis=0, keepdims=True) for k in range(4)]
        d = cot.shape[1]
        for acc, keep, send in ((acc_own, keep_own, send_own), (acc_other, keep_other, send_other)):
            mine = acc[d : d + 1, :half]
            put_vectors(acc, half + side, vectors + [mine[:, :d], mine[:, d:]])
            put_blocks(scal[0], [keep, send], acc, slice(None))


def down_block(scal, cot, mid, n2, pre, ctx_a, ctx_b, wo_a, wu_a, parts, wd, gain):
    total, d = cot.shape
    width = ctx_a.shape[1]
    half = wu_a.shape[1]
    args = (cot, mid, n2, pre, ctx_a, ctx_b, wo_a, *parts[0], wu_a, *parts[1], *wd, gain)
    in_specs = [rows_spec(TB, d), rows_spec(TB, d), rows_spec(TB, d), rows_spec(TB, 2 * half)]
    in_specs += [rows_spec(TB, width), rows_spec(TB, width)]
    in_specs += [tail_spec(v, width) if k in (1, 2) else const_spec(v.shape) for k, v in enumerate(args[6:])]
    columns = half + d // 2 + EXTRA
    pack = (BLOCKS // 2, d // BLOCKS, columns)
    outs = [((total, d), BF16), ((total, width), BF16), ((total, width), BF16), *[(pack, BF16)] * 4]
    out_specs = [rows_spec(TB, d), rows_spec(TB, width), rows_spec(TB, width)]
    out_specs += [const_spec(s) for s, _ in outs[3:]]
    scratch = [
        pltpu.VMEM((d + ONES, columns), F32), pltpu.VMEM((d + ONES, columns), F32),
        pltpu.VMEM((32, d), F32), pltpu.VMEM((2 * width, d), BF16), pltpu.VMEM((d, half), BF16),
        pltpu.VMEM((TB, 2 * width), BF16),
        pltpu.VMEM((d + ONES, TB), BF16),
        pltpu.VMEM((TB, FB), BF16), pltpu.VMEM((TB, FB), BF16), pltpu.VMEM((TB, 2 * half), BF16),
        pltpu.VMEM((TB, d), F32), pltpu.VMEM((TB, d), F32),
    ]
    return call(
        down_kernel, "feed_back", total // TB, (scal,), in_specs, outs, out_specs, scratch,
        2 * total * d * (6 * half + 4 * width), total * (16 * d + 4 * half), args,
    )


def out_rows(mid, hidden, wd_a, wd_b, bd, out):
    half = wd_a.shape[0]
    out[...] = (
        mid[...] + dot_nn(hidden[:, :half], wd_a[...]) + dot_nn(hidden[:, half:], wd_b[...]) + bd[...]
    ).astype(BF16)


def out_kernel(scal, mid, hidden, wd_a, wd_b, bd, *refs):
    out_rows(mid, hidden, wd_a, wd_b, bd, refs[-1])


def out_down_kernel(scal, mid, hidden, wd_a, wd_b, bd, before, d0, d1, out, down, d_all):
    out_rows(mid, hidden, wd_a, wd_b, bd, out)

    @pl.when(pl.program_id(0) == 0)
    def _():
        place(scal[1], (d0, d1), d_all, BF16)
        down[...] = d_all[...].T.astype(F32)


def part_spec(first, cols):
    return pl.BlockSpec((TM, cols), lambda i, *_: (i + first, 0))


def out_block(first, tiles, scal, mid, hidden, wd, bd, before, pieces=()):
    total, d = mid.shape
    args = (mid, hidden, *wd, bd)
    specs = [part_spec(first, d), part_spec(first, hidden.shape[1])]
    specs += [const_spec(a.shape) for a in (*wd, bd)]
    alias = {}
    if before is not None:
        alias = {len(args) + 1: 0}
        args += (before,)
        specs += [pl.BlockSpec(memory_space=pl.ANY)]
    outs, out_specs, scratch = [((total, d), BF16)], [part_spec(first, d)], []
    if pieces:
        args += tuple(pieces)
        specs += [const_spec(p.shape) for p in pieces]
        shape = (pieces[0].shape[2], d)
        outs += [(shape, F32)]
        out_specs += [const_spec(shape)]
        scratch = [pltpu.VMEM(shape[::-1], BF16)]
    return call(
        out_down_kernel if pieces else out_kernel, "layer_out", tiles, (scal,), specs, outs, out_specs, scratch,
        2 * tiles * TM * d * hidden.shape[1], tiles * TM * (6 * d + 2 * hidden.shape[1]), args, alias,
    )


def attend_back_kernel(
    heads, scal, nn, proj, probs, gctx, w, gain, shift, gproj, pack_keep, pack_send, kpad, vpad, dk, dv, acc, acc_b, gprob, gscore
):
    s = pl.program_id(0)
    clear(s, acc, acc_b)
    width = heads * HEAD_DIM
    edge = jnp.zeros((WIN - QB, width), BF16)
    for pad, j in ((kpad, 1), (vpad, 2)):
        pad[0 : WIN - QB, :] = edge
        pad[SEQ_LEN:, :] = edge
        pad[MARGIN : MARGIN + SEQ_LEN, :] = proj[:, j * width : (j + 1) * width]
    mask = head_mask(1.0, heads)
    dk[0 : (WIN - QB), :] = jnp.zeros(((WIN - QB), width), F32)
    dv[0 : (WIN - QB), :] = jnp.zeros(((WIN - QB), width), F32)
    scale = HEAD_DIM**-0.5

    def rows(b):
        return slice(b * QB, (b + 1) * QB)

    def keys(b):
        return slice(b * QB, b * QB + WIN)

    def own(b):
        return slice(b * WIN, (b + 1) * WIN)

    for b in range(NBLK):
        gprob[own(b), :] = dot_nt(vpad[keys(b), :], spread(gctx[rows(b), :], mask, heads))
    for b in range(NBLK):
        p = probs[own(b), :].astype(F32)
        gp = gprob[own(b), :]
        gscore[own(b), :] = (p * (gp - jnp.sum(p * gp, axis=0, keepdims=True))).astype(BF16)
    for b in range(NBLK):
        gproj[rows(b), 0:width] = (pair_rows(gscore[own(b), :], kpad[keys(b), :], heads) * scale).astype(BF16)
    for b in range(NBLK):
        key_term = dot_nn(gscore[own(b), :], spread(proj[rows(b), 0:width], mask, heads)) * scale
        value_term = dot_nn(probs[own(b), :], spread(gctx[rows(b), :], mask, heads))
        for total, term in ((dk, key_term), (dv, value_term)):
            total[b * QB : b * QB + (WIN - QB), :] += term[: (WIN - QB)]
            total[b * QB + (WIN - QB) : b * QB + WIN, :] = term[(WIN - QB) :]
    gproj[:, width : 2 * width] = dk[MARGIN : MARGIN + SEQ_LEN, :].astype(BF16)
    gproj[:, 2 * width :] = dv[MARGIN : MARGIN + SEQ_LEN, :].astype(BF16)
    gp_all = gproj[...]
    acc[:, : 3 * width] += dot_tn(nn[...], gp_all)
    acc_b[...] += jnp.sum(gp_all.astype(F32), axis=0, keepdims=True)

    @pl.when(s == pl.num_programs(0) - 1)
    def _():
        d = acc.shape[0]
        column = lambda v: jnp.broadcast_to(v[...], (EXTRA, d)).T[:, 0:1]
        gain_col, shift_col = column(gain), column(shift)
        gain_grad, shift_grad = jnp.zeros((d, EXTRA), F32), jnp.zeros((d, EXTRA), F32)
        for j in range(3):
            for c in range(0, width, EXTRA):
                at = slice(j * width + c, j * width + c + EXTRA)
                weight = w[:, at].astype(F32)
                total, sums = acc[:, at], acc_b[:, at]
                gain_grad += weight * total
                shift_grad += weight * sums
                acc[:, at] = gain_col * total + shift_col * sums
        gain_grad = jnp.sum(gain_grad, axis=1, keepdims=True)
        shift_grad = jnp.sum(shift_grad, axis=1, keepdims=True)
        put_vectors(acc, 3 * width, [jnp.concatenate([acc_b[:, :width], acc_b[:, 2 * width :]], axis=1)])
        lane = lax.broadcasted_iota(jnp.int32, (d, EXTRA), 1)
        extra = jnp.where(lane == 1, gain_grad, acc[:, 3 * width :])
        acc[:, 3 * width :] = jnp.where(lane == 2, shift_grad, extra)
        put_blocks(scal[1], [pack_keep, pack_send], acc, slice(None))


def attention_backward(scal, nn, proj, probs, gctx, w, gain, shift):
    total, d = nn.shape
    seqs = total // SEQ_LEN
    width = gctx.shape[1]
    heads = width // HEAD_DIM

    def body(*refs):
        attend_back_kernel(heads, *refs)

    pad = SEQ_LEN + WIN - QB
    columns = 3 * width + EXTRA
    pack = (BLOCKS // 2, d // BLOCKS, columns)
    return call(
        body, "attend_back", seqs, (scal,),
        [
            rows_spec(SEQ_LEN, d), rows_spec(SEQ_LEN, 3 * width),
            rows_spec(NBLK * WIN, heads * QB), rows_spec(SEQ_LEN, width),
            const_spec(w.shape), const_spec(gain.shape), const_spec(shift.shape),
        ],
        [((total, 3 * width), BF16), (pack, BF16), (pack, BF16)],
        [rows_spec(SEQ_LEN, 3 * width), const_spec(pack), const_spec(pack)],
        [
            pltpu.VMEM((pad, width), BF16), pltpu.VMEM((pad, width), BF16),
            pltpu.VMEM((pad, width), F32), pltpu.VMEM((pad, width), F32),
            pltpu.VMEM((d, columns), F32), pltpu.VMEM((1, 3 * width), F32),
            pltpu.VMEM((NBLK * WIN, heads * QB), F32), pltpu.VMEM((NBLK * WIN, heads * QB), BF16),
        ],
        2 * total * d * 3 * width + 16 * total * WIN * width, total * (d + 9 * width) * 2,
        (nn, proj, probs, gctx, w, gain, shift),
    )


def last_kernel(per_seq, first, scal, x, gmid, gp_a, gp_b, w_a, w_b, gain, *refs):
    gin, back_a, back_b = refs[-3:]
    i = pl.program_id(0)
    rows = x.shape[0]
    tile = i + first
    back_a[...] = dot_nt(gp_a[...], w_a[...])
    back_b[...] = dot_nt(gp_b[...], w_b[...])
    for sub in subs(rows):
        keep = keep_of((SUB, x.shape[1]), (tile % per_seq) * rows + sub.start, tile // per_seq, scal)
        nn, r = normalize(x[sub, :].astype(F32) * keep)
        u = (back_a[sub, :] + back_b[sub, :]) * gain[...]
        mean_un = jnp.mean(u * nn, axis=-1, keepdims=True)
        a = r * (u - jnp.mean(u, axis=-1, keepdims=True) - nn * mean_un)
        gin[sub, :] = (gmid[sub, :].astype(F32) + a) * keep


def last_block(part, parts, scal, x, gmid, gp_a, gp_b, w_a, w_b, gain, before):
    total, d = x.shape
    tiles = total // TM // parts

    def body(*refs):
        last_kernel(SEQ_LEN // TM, part * tiles, *refs)

    width = gp_a.shape[1]
    args = (x, gmid, gp_a, gp_b, w_a, w_b, gain)
    specs = [part_spec(part * tiles, c) for c in (d, d, width, width)]
    specs += [const_spec(a.shape) for a in args[4:]]
    alias = {}
    if before is not None:
        alias = {len(args) + 1: 0}
        args += (before,)
        specs += [pl.BlockSpec(memory_space=pl.ANY)]
    return call(
        body, "input_gradient", tiles, (scal,), specs, [((total, d), F32)], [part_spec(part * tiles, d)],
        [pltpu.VMEM((TM, d), F32)] * 2,
        4 * tiles * TM * d * width, tiles * TM * (10 * d + 4 * width), args, alias,
    )[0]


def place(me, pieces, out, kind, columns=slice(None)):
    each = pieces[0].shape[0]
    rows = pieces[0].shape[1]
    for j in range(BLOCKS):
        at = pl.ds(pl.multiple_of((j ^ me) * rows, rows), rows)
        out[at, :] = pieces[j // each][j % each, :, columns].astype(kind)


def unpack_kernel(scal, u0, u1, q0, q1, side_y, side_d, up, out, *refs):
    vectors, (bias_up, qkv, bias_q, gain, shift, u_side, q_all, q_side) = refs[:4], refs[4:]
    me = scal[0]
    half, side = up.shape[1], out.shape[1] // 2
    rows = out.shape[0]
    place(me, (u0, u1), up, F32, slice(0, half))
    place(me, (u0, u1), u_side, F32, slice(half, u0.shape[2]))
    out[:, :side] = u_side[:rows, :side]
    out[:, side:] = u_side[rows:, :side]
    sums = u_side[:, side:].T
    for k in range(4):
        vectors[k][...] = sums[k : k + 1, :]
    bias_up[...] = jnp.concatenate([sums[4:5, :], sums[5:6, :]], axis=1)
    place(scal[1], (q0, q1), q_all, F32)
    width = qkv.shape[2]
    for j in range(3):
        qkv[j] = q_all[:, j * width : (j + 1) * width]
    sums = q_all[:, 3 * width :].T
    bias_q[...] = jnp.concatenate([sums[0:1, :width], sums[0:1, width:]], axis=0)
    place(scal[1], (side_y, side_d), q_side, F32)
    sums += q_side[...].T
    gain[...] = sums[1:2, :]
    shift[...] = sums[2:3, :]


def unpack(scal, pieces, up, out, qkv):
    d = up[0]
    shapes = [up, out, *[(1, d)] * 4, (1, up[1]), qkv, (2, qkv[2]), (1, d), (1, d)]
    natural = [(d, pieces[0].shape[2] - up[1]), (d, pieces[2].shape[2]), (d, EXTRA)]
    return call(
        unpack_kernel, "unpack", 1, (scal,), [const_spec(p.shape) for p in pieces], [(s, F32) for s in shapes],
        [const_spec(s) for s in shapes], [pltpu.VMEM(s, F32) for s in natural], 0,
        6 * sum(p.size for p in pieces), tuple(pieces),
    )


def make_body(mesh):
    tp = mesh.shape["tensor"]
    dp = mesh.shape["dp"]
    paired = tp == 2 and dp == BLOCKS

    def across(v):
        return lax.ppermute(v, "tensor", [(0, 1), (1, 0)])

    def swap(v, distance):
        return lax.ppermute(v, "dp", [(i, i ^ distance) for i in range(dp)])

    def core(v):
        return swap(v, 1)

    def diagonal(v):
        pairs = [(2 * i + j, 2 * (i ^ 1) + 1 - j) for i in range(dp) for j in range(2)]
        return lax.ppermute(v, ("dp", "tensor"), pairs)

    def plus(first, *rest):
        total = first.astype(F32)
        for v in rest:
            total = total + v.astype(F32)
        return total.astype(first.dtype)

    def lower(v):
        return v[: v.shape[0] // 2]

    def upper(v):
        return v[v.shape[0] // 2 :]

    def join(a, b):
        return jnp.concatenate([a, b], axis=0)

    def window(kernel, args, moves):
        args, sent = lax.optimization_barrier((args, [v for v, _ in moves]))
        arrived = [move(v) for v, (_, move) in zip(sent, moves)]
        return lax.optimization_barrier((kernel(*args), arrived, sent))

    def body(
        inputs, cotangent, lengths, time_span, freq_span, gain_one, shift_one, qkv_weight, qkv_bias,
        out_weight, out_bias, gain_two, shift_two, up_weight, up_bias, down_weight, down_bias,
    ):
        total, d = inputs.shape
        seqs = total // SEQ_LEN
        here = lax.axis_index("tensor") * seqs
        index = lax.axis_index("dp")
        label = label_q = jnp.int32(0)
        if paired:
            label = ((index & 1) << 3) | ((index & 2) << 1) | ((index & 4) >> 1)
            label_q = ((index & 1) << 3) | (index & 4)
        place_here = jnp.stack([label, label_q, here, index & 1 if paired else jnp.int32(0)]).astype(jnp.int32)
        ends = [span.T.reshape(-1) for span in (time_span, freq_span)]
        scal = jnp.concatenate([place_here, lengths, *ends])
        row = lambda v: v.reshape(1, -1)

        def attend_a(rows, w, bias):
            return attention_forward(True, scal, rows, w, bias, row(gain_one), row(shift_one))

        def attend_b(rows, w, bias):
            return attention_forward(False, scal, rows, w, bias, None, None)

        def up(ctx_a, ctx_b, wo_a, wu_a, parts, biases):
            return up_block(
                scal, inputs, cotangent, ctx_a, ctx_b, wo_a, wu_a, parts, row(out_bias), row(gain_two),
                row(shift_two), biases,
            )

        def down(mid, n2, pre, ctx_a, ctx_b, wo_a, wu_a, parts, wd):
            return down_block(scal, cotangent, mid, n2, pre, ctx_a, ctx_b, wo_a, wu_a, parts, wd, row(gain_two))

        def back(nn, proj, probs, gctx, w):
            return attention_backward(scal, nn, proj, probs, gctx, w, row(gain_one), row(shift_one))

        def last(part, parts):
            return lambda gmid, gp_a, gp_b, w_a, w_b, before: last_block(
                part, parts, scal, inputs, gmid, gp_a, gp_b, w_a, w_b, row(gain_one), before
            )

        def out(first, tiles):
            return lambda mid, hidden, wd, before, *pieces: out_block(
                first, tiles, scal, mid, hidden, wd, row(down_bias), before, pieces
            )

        turned = lambda w: jnp.transpose(w, (1, 0, 2))
        if paired:
            odd = index & 1

            def part_of(v):
                rows = v.shape[0] // 2
                return lax.dynamic_slice_in_dim(v, odd * rows, rows, 0)

            qkv_a = turned(qkv_weight)
            side = d // 2
            low, high = qkv_a.reshape(2, -1, side)
            first_rows = jnp.where(
                odd == 0,
                jnp.concatenate([low, out_weight[:, :side]], axis=0),
                jnp.concatenate([high, out_weight[:, side:]], axis=0),
            )
            (nn, n1, proj_a, ctx_a, probs_a, side_a), (first_half, bias_b), _ = window(
                attend_a, (inputs, qkv_a, qkv_bias), [(first_rows, across), (qkv_bias, across)]
            )
            first_pair = (first_half, core(first_half))
            (proj_b, ctx_b, probs_b, side_b), (up_half, up_bias_b), _ = window(
                attend_b, (n1, first_pair, bias_b), [(part_of(up_weight), across), (row(up_bias), across)]
            )
            pairs = (first_pair, (up_half, core(up_half)))
            (mid, n2, hidden, pre, d_own, d_other), (down_b,), _ = window(
                up, (ctx_a, ctx_b, out_weight, up_weight, pairs, (row(up_bias), up_bias_b)), [(down_weight, across)]
            )
            wd = (down_weight, down_b)
            (gmid, gctx_a, gctx_b, u_own, u_other, u_send_own, u_send_other), (d_cross,), _ = window(
                down, (mid, n2, pre, ctx_a, ctx_b, out_weight, up_weight, pairs, wd), [(d_other, across)]
            )
            step = lambda distance: lambda v: swap(v, distance)
            u_other, u_own = plus(u_other, core(u_send_other)), plus(u_own, core(u_send_own))
            d_sum = plus(d_own, d_cross)
            d_sum = plus(lower(d_sum), core(upper(d_sum)))
            (gproj_b, q_other, q_send), (u_cross, d_in), _ = window(
                back, (nn, proj_b, probs_b, gctx_b, side_b), [(u_other, across), (upper(d_sum), step(4))]
            )
            u_sum = plus(u_own, u_cross)
            d_sum = plus(lower(d_sum), d_in)
            q_other = plus(q_other, core(q_send))
            (gproj_a, q_own, q_send), (u_in, d_in, q_cross), _ = window(
                back, (nn, proj_a, probs_a, gctx_a, side_a),
                [(upper(u_sum), step(2)), (d_sum, step(8)), (q_other, across)],
            )
            u_sum = plus(lower(u_sum), u_in)
            d_sum = plus(d_sum, d_in)
            q_terms = (q_own, core(q_send), q_cross)
            input_grad, (u_in, d_in, q_in), _ = window(
                last(0, 2), (gmid, gproj_a, gproj_b, side_a, side_b, None),
                [(upper(u_sum), step(4)), (d_sum, step(2)), (plus(*map(upper, q_terms)), step(4))],
            )
            u_sum = plus(lower(u_sum), u_in)
            d_sum = plus(d_sum, d_in)
            q_sum = plus(*map(lower, q_terms), q_in)
            input_grad, (u_in, d_in, q_in), _ = window(
                last(1, 2), (gmid, gproj_a, gproj_b, side_a, side_b, input_grad),
                [(u_sum, step(8)), (d_sum, step(4)), (q_sum, step(2))],
            )
            u_sum = plus(u_sum, u_in)
            d_sum = join(d_sum, d_in)
            q_sum = plus(q_sum, q_in)
            tiles = total // TM
            cuts = (0, tiles * 5 // 8, tiles * 7 // 8, tiles)
            (layer_out,), (u_in, d_in, q_in), _ = window(
                out(cuts[0], cuts[1] - cuts[0]), (mid, hidden, wd, None),
                [(u_sum, step(4)), (d_sum, core), (q_sum, step(8))],
            )
            u_sum = join(u_sum, u_in)
            q_sum = plus(q_sum, q_in)
            (layer_out, g_down), (u_in, q_in), _ = window(
                out(cuts[1], cuts[2] - cuts[1]), (mid, hidden, wd, layer_out, d_sum, d_in),
                [(u_sum, step(2)), (q_sum, step(4))],
            )
            u_sum = join(u_sum, u_in)
            q_sum = join(q_sum, q_in)
            sides = q_sum[:, :, q_sum.shape[2] - EXTRA :]
            (layer_out,), (u_in, q_in, side_y, side_d), _ = window(
                out(cuts[2], cuts[3] - cuts[2]), (mid, hidden, wd, layer_out),
                [(u_sum, core), (q_sum, core), (sides, across), (sides, diagonal)],
            )
            g_up, g_out, *shared_two, g_bu, g_qkv, g_qb, gain_grad, shift_grad = unpack(
                scal, (u_sum, u_in, q_sum, q_in, side_y, side_d), up_weight.shape, out_weight.shape, qkv_a.shape
            )
            g_qkv = turned(g_qkv)
            g_bu = g_bu.reshape(-1)
            shared_two = [v.reshape(-1) for v in shared_two]
            shared_one = [v.reshape(-1) for v in (gain_grad, shift_grad)]
        else:
            def halves(local, axis):
                return tuple(jnp.split(lax.all_gather(local, "tensor", axis=axis, tiled=True), 2, axis=axis))

            def sums(own, other, axis):
                whole = jnp.concatenate([own, other], axis=axis)
                part = lax.psum_scatter(whole, "tensor", scatter_dimension=axis, tiled=True)
                return lax.psum(part, "dp").astype(F32)

            natural = lambda *packs: jnp.concatenate(packs, axis=0).reshape(d, -1)
            qkv = [turned(w) for w in halves(qkv_weight, 2)]
            biases = halves(qkv_bias, 1)
            up_biases = [row(b) for b in halves(up_bias, 0)]
            wo, wu, wd = halves(out_weight, 0), halves(up_weight, 1), halves(down_weight, 0)
            nn, n1, proj_a, ctx_a, probs_a, side_a = attend_a(inputs, qkv[0], biases[0])
            halves_b = jnp.split(qkv[1].reshape(-1, qkv[1].shape[2]), 2, axis=0)
            proj_b, ctx_b, probs_b, side_b = attend_b(n1, halves_b, biases[1])
            parts = (jnp.split(wo[1], 2, axis=1), jnp.split(wu[1], 2, axis=0))
            mid, n2, hidden, pre, d_own, d_other = up(ctx_a, ctx_b, wo[0], wu[0], parts, up_biases)
            gmid, gctx_a, gctx_b, *u_packs = down(mid, n2, pre, ctx_a, ctx_b, wo[0], wu[0], parts, wd)
            gproj_b, *q_other = back(nn, proj_b, probs_b, gctx_b, side_b)
            gproj_a, *q_own = back(nn, proj_a, probs_a, gctx_a, side_a)
            input_grad = last(0, 1)(gmid, gproj_a, gproj_b, side_a, side_b, None)
            layer_out = out(0, total // TM)(mid, hidden, wd, None)[0]
            g_down = sums(natural(d_own), natural(d_other), 1).T
            u = natural(u_packs[0], u_packs[2]), natural(u_packs[1], u_packs[3])
            half, side = wu[0].shape[1], d // 2
            g_up = sums(u[0][:, :half], u[1][:, :half], 1)
            beside = [jnp.concatenate(jnp.split(v[:, half : half + side], 2, axis=0), axis=1) for v in u]
            g_out = sums(*beside, 0)
            q = natural(*q_own), natural(*q_other)
            wide = 3 * qkv[0].shape[2]
            g_qkv = sums(*[v[:, :wide].reshape(d, 3, -1) for v in q], 2)
            g_qb = sums(*[v[:, wide].reshape(2, -1) for v in q], 1)
            small_two = [v[:, half + side :].T for v in u]
            g_bu = sums(*[v[4:6].reshape(-1) for v in small_two], 0)
            shared_two = lax.psum(small_two[0][:4], ("dp", "tensor")).astype(F32)
            vectors = (q[0] + q[1])[:, wide + 1 : wide + 3].T
            shared_one = lax.psum(vectors, ("dp", "tensor")).astype(F32)
        return (
            layer_out, input_grad, shared_one[0], shared_one[1], g_qkv, g_qb, g_out, shared_two[2],
            shared_two[0], shared_two[1], g_up, g_bu, g_down, shared_two[3],
        )

    return body


def solution(mesh):
    in_specs = (
        P(("dp", "tensor"), None), P(("dp", "tensor"), None), P("dp"), P("dp", None), P("dp", None), P(), P(),
        P(None, None, "tensor"), P(None, "tensor"), P("tensor", None), P(), P(), P(), P(None, "tensor"),
        P("tensor"), P("tensor", None), P(),
    )
    out_specs = (
        P(("dp", "tensor"), None), P(("dp", "tensor"), None), P(), P(), P(None, None, "tensor"), P(None, "tensor"),
        P("tensor", None), P(), P(), P(), P(None, "tensor"), P("tensor"), P("tensor", None), P(),
    )
    return jax.shard_map(make_body(mesh), mesh=mesh, in_specs=in_specs, out_specs=out_specs, check_vma=False)
```
